32 devices in a mesh: seq: 8 (over z, y), row: 4 (over x, core).
Axes of the slice: x: 2, y: 2, z: 4, core: 2. Of those that a mesh axis runs over, the one named last changes fastest.
Arguments:
- block_input: bfloat16 [4, 1024, 2048], P('row', 'seq'), may hold values from -6 to 6
- memory: bfloat16 [4, 1024, 2048], P('row', 'seq'), may hold values from -6 to 6
- key_cache: bfloat16 [4, 1024, 2048], P('row', 'seq'), may hold values from -12 to 12
- value_cache: bfloat16 [4, 1024, 2048], P('row', 'seq'), may hold values from -6 to 6
- doc_lengths: int32 [4, 8], replicated, may hold values from 1 to 1024, as said below
- gmu_gate: bfloat16 [2048, 2048], P('seq', 'row'), may hold values from -0.125 to 0.125
- gmu_out: bfloat16 [2048, 2048], P('row', 'seq'), may hold values from -0.125 to 0.125
- ffn1_gate: bfloat16 [2048, 8192], P('seq', 'row'), may hold values from -0.125 to 0.125
- ffn1_up: bfloat16 [2048, 8192], P('seq', 'row'), may hold values from -0.125 to 0.125
- ffn1_down: bfloat16 [8192, 2048], P('row', 'seq'), may hold values from -0.0625 to 0.0625
- query_weight: bfloat16 [2048, 2048], P('seq', 'row'), may hold values from -0.125 to 0.125
- attn_out: bfloat16 [2048, 2048], P('row', 'seq'), may hold values from -0.5 to 0.5
- ffn2_gate: bfloat16 [2048, 8192], P('seq', 'row'), may hold values from -0.125 to 0.125
- ffn2_up: bfloat16 [2048, 8192], P('seq', 'row'), may hold values from -0.125 to 0.125
- ffn2_down: bfloat16 [8192, 2048], P('row', 'seq'), may hold values from -0.0625 to 0.0625
- gain_a: float32 [2048], replicated, may hold values from 0.5 to 1.5
- gain_b: float32 [2048], replicated, may hold values from 0.5 to 1.5
- gain_c: float32 [2048], replicated, may hold values from 0.5 to 1.5
- gain_d: float32 [2048], replicated, may hold values from 0.5 to 1.5
- cotangent: bfloat16 [4, 1024, 2048], P('row', 'seq'), may hold values from -6 to 6
Outputs:
- mixed: float32 [4, 1024, 2048], P('row', 'seq')
- input_grad: float32 [4, 1024, 2048], P('row', 'seq')
- memory_grad: float32 [4, 1024, 2048], P('row', 'seq')
- key_grad: float32 [4, 1024, 2048], P('row', 'seq')
- value_grad: float32 [4, 1024, 2048], P('row', 'seq')
- gmu_gate_grad: float32 [2048, 2048], P('seq', 'row')
- gmu_out_grad: float32 [2048, 2048], P('row', 'seq')
- ffn1_gate_grad: float32 [2048, 8192], P('seq', 'row')
- ffn1_up_grad: float32 [2048, 8192], P('seq', 'row')
- ffn1_down_grad: float32 [8192, 2048], P('row', 'seq')
- query_weight_grad: float32 [2048, 2048], P('seq', 'row')
- attn_out_grad: float32 [2048, 2048], P('row', 'seq')
- ffn2_gate_grad: float32 [2048, 8192], P('seq', 'row')
- ffn2_up_grad: float32 [2048, 8192], P('seq', 'row')
- ffn2_down_grad: float32 [8192, 2048], P('row', 'seq')
- gain_a_grad: float32 [2048], replicated
- gain_b_grad: float32 [2048], replicated
- gain_c_grad: float32 [2048], replicated
- gain_d_grad: float32 [2048], replicated
The draws below stay inside these ranges and needn't reach their ends.
Inputs may be any that keep to these rules, and one draw needn't show every extreme that they name: `doc_lengths`: each row's 8 lengths sum to 1024.
All inputs are finite; a program needn't handle non-finite values.
Results may differ from the reference program's by a relative error of at most 0.04.
Values may be sent and summed in bfloat16 or wider, within the bound.
A program may use at most 256 MiB of HBM per device.

```python
import jax
import jax.numpy as jnp
from jax import lax

D = 2048
FF = 8192
HEADS = 16
HEAD_DIM = 128
TOK_DEV = 128
NDOC = 8
LEN = 1024
ROWS = 4


def draw_doc_lengths(key, part):
    key = jax.random.fold_in(key, 7)
    key_short, key_long = jax.random.split(key)
    short_most = max((TOK_DEV - 1) // (NDOC - 1), 1)
    short_docs = jax.random.randint(key_short, (ROWS, NDOC), 1, short_most + 1)
    long_index = jax.random.randint(key_long, (ROWS, 1), 0, NDOC)
    is_long = jnp.arange(NDOC)[None, :] == long_index
    others = jnp.sum(jnp.where(is_long, 0, short_docs), axis=1, keepdims=True)
    return jnp.where(is_long, LEN - others, short_docs).astype(jnp.int32)


def levels(rng, shape, pieces, least, top_value):
    def one(axis_at, parts):
        heights = jax.random.uniform(jax.random.fold_in(jax.random.fold_in(rng, 6), axis_at), (parts,), jnp.float32, least / len(pieces), top_value / len(pieces))
        return jnp.repeat(jnp.exp(heights), shape[axis_at] // parts).reshape((-1,) + (1,) * (len(shape) - axis_at - 1))

    factor_of = one(*pieces[0])
    for cut in pieces[1:]:
        factor_of = factor_of * one(*cut)
    return factor_of


def noise(stream_key, dims, deviation, bound, cuts=(), kind=jnp.bfloat16):
    values = jax.random.normal(stream_key, dims, jnp.float32) * deviation
    if len(cuts) > 0:
        values = levels(stream_key, dims, cuts, -0.22, 0.18) * values
    return jnp.clip(values, min=-bound, max=bound).astype(kind)


def setup_inputs(seed: int = 0) -> dict:
    keys = jax.random.split(jax.random.key(seed), 21)
    return {
        "block_input": noise(keys[0], (ROWS, LEN, D), 1.0, 6.0, ((0, 4), (1, 8))),
        "memory": noise(keys[1], (ROWS, LEN, D), 1.0, 6.0, ((0, 4), (1, 8))),
        "key_cache": noise(keys[2], (ROWS, LEN, HEADS * HEAD_DIM), 2.0, 12.0, ((0, 4), (1, 8))),
        "value_cache": noise(keys[3], (ROWS, LEN, HEADS * HEAD_DIM), 1.0, 6.0, ((0, 4), (1, 8))),
        "doc_lengths": draw_doc_lengths(jax.random.fold_in(keys[20], 71), 0),
        "gmu_gate": noise(keys[5], (D, D), D ** -0.5, 0.125, ((0, 8), (1, 4))),
        "gmu_out": noise(keys[6], (D, D), D ** -0.5, 0.125, ((0, 4), (1, 8))),
        "ffn1_gate": noise(keys[7], (D, FF), D ** -0.5, 0.125, ((0, 8), (1, 4))),
        "ffn1_up": noise(keys[8], (D, FF), D ** -0.5, 0.125, ((0, 8), (1, 4))),
        "ffn1_down": noise(keys[9], (FF, D), FF ** -0.5, 0.0625, ((0, 4), (1, 8))),
        "query_weight": noise(keys[10], (D, HEADS * HEAD_DIM), D ** -0.5, 0.125, ((0, 8), (1, 4))),
        "attn_out": noise(keys[11], (HEADS * HEAD_DIM, D), (D // 16) ** -0.5, 0.5, ((0, 4), (1, 8))),
        "ffn2_gate": noise(keys[12], (D, FF), D ** -0.5, 0.125, ((0, 8), (1, 4))),
        "ffn2_up": noise(keys[13], (D, FF), D ** -0.5, 0.125, ((0, 8), (1, 4))),
        "ffn2_down": noise(keys[14], (FF, D), FF ** -0.5, 0.0625, ((0, 4), (1, 8))),
        "gain_a": jnp.clip(1.0 + 0.1 * jax.random.normal(keys[15], (D,), jnp.float32), 0.5, 1.5),
        "gain_b": jnp.clip(1.0 + 0.1 * jax.random.normal(keys[16], (D,), jnp.float32), 0.5, 1.5),
        "gain_c": jnp.clip(1.0 + 0.1 * jax.random.normal(keys[17], (D,), jnp.float32), 0.5, 1.5),
        "gain_d": jnp.clip(1.0 + 0.1 * jax.random.normal(keys[18], (D,), jnp.float32), 0.5, 1.5),
        "cotangent": noise(keys[19], (ROWS, LEN, D), 1.0, 6.0, ((0, 4), (1, 8))),
    }


@jax.custom_vjp
def low(v):
    return lax.optimization_barrier(v.astype(jnp.bfloat16)).astype(jnp.float32)

@jax.custom_vjp
def low_back(v):
    return v

def low_keep(v):
    return (low(v), None)

def low_pass(kept, grad):
    return (grad,)

def back_keep(v):
    return (v, None)

def back_low(kept, grad):
    return (low(grad),)
low.defvjp(low_keep, low_pass)
low_back.defvjp(back_keep, back_low)
EPSILON = 1e-05
MASKED = -1e+30

def matmul(left, right):
    return jnp.dot(left, right, precision=lax.Precision.HIGHEST, preferred_element_type=jnp.float32)

def rms_norm(values, gain_vec):
    return values * lax.rsqrt(lax.optimization_barrier(jnp.mean(values * values, axis=-1, keepdims=True)) + EPSILON) * gain_vec

def feed_forward(normed, gate_weight, up_weight, down_weight):
    gate_val = low_back(matmul(normed, gate_weight))
    up_val = low_back(matmul(normed, up_weight))
    hidden = low(jax.nn.silu(gate_val) * up_val)
    return low_back(matmul(hidden, down_weight))

def head_attention(query_head, key_head, value_head, head_docs):
    positions = jnp.arange(query_head.shape[0], dtype=jnp.int32)
    allowed = (positions[None, :] <= positions[:, None]) & (head_docs[:, None] == head_docs[None, :])
    scores = low_back(jnp.dot(query_head, key_head.T, precision=lax.Precision.HIGHEST, preferred_element_type=jnp.float32) * HEAD_DIM ** (-0.5))
    scores = jnp.where(allowed, scores, MASKED)
    row_max = lax.optimization_barrier(jnp.max(scores, axis=-1, keepdims=True))
    expo = jnp.exp(scores - row_max)
    probs = expo / lax.optimization_barrier(jnp.sum(expo, axis=-1, keepdims=True))
    return jnp.dot(low(probs), value_head, precision=lax.Precision.HIGHEST, preferred_element_type=jnp.float32)

def split_heads(values):
    return values.reshape(ROWS, LEN, HEADS, HEAD_DIM).transpose(0, 2, 1, 3).reshape(ROWS * HEADS, LEN, HEAD_DIM)

def reference(block_input, memory, key_cache, value_cache, doc_lengths, gmu_gate, gmu_out, ffn1_gate, ffn1_up, ffn1_down, query_weight, attn_out, ffn2_gate, ffn2_up, ffn2_down, gain_a, gain_b, gain_c, gain_d, cotangent):
    doc_ends = jnp.cumsum(doc_lengths, axis=1, dtype=jnp.int32)
    positions = jnp.arange(LEN, dtype=jnp.int32)
    doc_ids = lax.optimization_barrier(jnp.sum((positions[None, :, None] >= doc_ends[:, None, :]).astype(jnp.int32), axis=-1))
    head_docs = jnp.repeat(doc_ids, HEADS, axis=0)
    block_head = jax.checkpoint(head_attention)

    def forward(x_in, mem_in, keys_in, vals_in, w_gg, w_go, w_1g, w_1u, w_1d, w_q, w_ao, w_2g, w_2u, w_2d, g_a, g_b, g_c, g_d):
        x_zero = x_in.reshape(-1, D)
        normed_a = low(rms_norm(x_zero, g_a))
        gmu_pre = low_back(matmul(normed_a, w_gg))
        gmu_act = low(mem_in.reshape(-1, D) * jax.nn.silu(gmu_pre))
        x_one = x_zero + low_back(matmul(gmu_act, w_go))
        x_two = x_one + feed_forward(low(rms_norm(x_one, g_b)), w_1g, w_1u, w_1d)
        normed_c = low(rms_norm(x_two, g_c))
        queries = low(low_back(matmul(normed_c, w_q)))
        heads_out = lax.map(lambda items: block_head(items[0], items[1], items[2], items[3]), (split_heads(queries), split_heads(keys_in), split_heads(vals_in), head_docs))
        attended = heads_out.reshape(ROWS, HEADS, LEN, HEAD_DIM).transpose(0, 2, 1, 3).reshape(-1, HEADS * HEAD_DIM)
        attended = low(low_back(attended))
        x_three = x_two + low_back(matmul(attended, w_ao))
        mixed = x_three + feed_forward(low(rms_norm(x_three, g_d)), w_2g, w_2u, w_2d)
        return mixed.reshape(ROWS, LEN, D)
    floats = [block_input, memory, key_cache, value_cache, gmu_gate, gmu_out, ffn1_gate, ffn1_up, ffn1_down, query_weight, attn_out, ffn2_gate, ffn2_up, ffn2_down, gain_a, gain_b, gain_c, gain_d]
    floats = [item.astype(jnp.float32) for item in floats]
    mixed, pullback = jax.vjp(forward, *floats)
    grads = pullback(cotangent.astype(jnp.float32))
    return (mixed, grads[0], grads[1], grads[2], grads[3], grads[4], grads[5], grads[6], grads[7], grads[8], grads[9], grads[10], grads[11], grads[12], grads[13], grads[14], grads[15], grads[16], grads[17])
```

```python
import jax
import jax.numpy as jnp
from jax import lax
from jax.experimental import pallas as pl
from jax.experimental.pallas import tpu as pltpu
from jax.sharding import PartitionSpec as P

HEAD_DIM = 128


EPSILON = 1e-05
MASKED = -1e30
BF = jnp.bfloat16
F32 = jnp.float32


def passed_along(value, axis, steps):
    count = lax.axis_size(axis)
    first, last = (max(0, -steps), min(count, count - steps))
    return lax.ppermute(value, axis, [(source, source + steps) for source in range(first, last)])


def shifted(value, axis, steps):
    count = lax.axis_size(axis)
    pairs = [(source, (source + steps) % count) for source in range(count)]
    return lax.ppermute(value, axis, pairs)


def swapped(value, axis, mask):
    count = lax.axis_size(axis)
    return lax.ppermute(value, axis, [(source, source ^ mask) for source in range(count)])


def silu_slope(values):
    sigmoid = jax.nn.sigmoid(values)
    return sigmoid * (1.0 + values * (1.0 - sigmoid))


def rms_forward(values, gain_vec):
    inverse = lax.rsqrt(jnp.mean(values * values, axis=-1, keepdims=True) + EPSILON)
    return (values * inverse * gain_vec, inverse)


def rms_backward(values, inverse, gain_vec, grad_normed):
    scaled = grad_normed * gain_vec
    gain_grad = jnp.sum(grad_normed * values * inverse, axis=0)
    inner_sum = jnp.mean(scaled * values, axis=-1, keepdims=True)
    return (inverse * scaled - values * inverse * inverse * inverse * inner_sum, gain_grad)


def doc_numbers(doc_lengths, positions):
    doc_ends = jnp.cumsum(doc_lengths, axis=1, dtype=jnp.int32)
    return jnp.sum((positions[None, :, None] >= doc_ends[:, None, :]).astype(jnp.int32), axis=-1)


def dot_plain(left, right):
    return jnp.dot(left, right, preferred_element_type=F32)


def dot_left_t(left, right):
    return lax.dot_general(left, right, (((0,), (0,)), ((), ())), preferred_element_type=F32)


def dot_right_t(left, right):
    return lax.dot_general(left, right, (((1,), (1,)), ((), ())), preferred_element_type=F32)


def tile_mask(docs_col, docs_row, start, tile):
    keys = start + tile
    q_pos = lax.broadcasted_iota(jnp.int32, (tile, keys), 0) + start
    k_pos = lax.broadcasted_iota(jnp.int32, (tile, keys), 1)
    return (k_pos <= q_pos) & (docs_col[pl.ds(start, tile), :] == docs_row[:, pl.ds(0, keys)])


def attention_forward_kernel(tile, q_ref, k_ref, v_ref, docs_col, docs_row, out_ref, stat_ref):
    length = q_ref.shape[0]
    scale = HEAD_DIM ** (-0.5)
    for start in range(0, length, tile):
        keys = start + tile
        allowed = tile_mask(docs_col, docs_row, start, tile)
        scores = dot_right_t(q_ref[pl.ds(start, tile), :], k_ref[pl.ds(0, keys), :]) * scale
        scores = jnp.where(allowed, scores, MASKED)
        top = jnp.max(scores, axis=1, keepdims=True)
        expo = jnp.exp(scores - top)
        total = jnp.sum(expo, axis=1, keepdims=True)
        probs = (expo * (1.0 / total)).astype(BF)
        out_ref[pl.ds(start, tile), :] = dot_plain(probs, v_ref[pl.ds(0, keys), :]).astype(BF)
        stat_ref[pl.ds(start, tile), :] = jnp.broadcast_to(top + jnp.log(total), (tile, HEAD_DIM))


def attention_forward(q, k, v, docs):
    length, lanes = q.shape
    heads = lanes // HEAD_DIM
    tile = min(256, length)
    block = pl.BlockSpec((length, HEAD_DIM), lambda h: (0, h))
    return pl.pallas_call(
        lambda *refs: attention_forward_kernel(tile, *refs),
        grid=(heads,),
        in_specs=[
            block,
            block,
            block,
            pl.BlockSpec((length, 1), lambda h: (0, 0)),
            pl.BlockSpec((1, length), lambda h: (0, 0)),
        ],
        out_specs=[block, block],
        out_shape=[
            jax.ShapeDtypeStruct((length, lanes), BF),
            jax.ShapeDtypeStruct((length, lanes), F32),
        ],
        compiler_params=pltpu.CompilerParams(vmem_limit_bytes=40 * 2**20),
    )(q, k, v, docs[:, None], docs[None, :])


def attention_backward_kernel(
    tile, q_ref, k_ref, v_ref, dout_ref, stat_ref, docs_col, docs_row, dq_ref, dk_ref, dv_ref, dk_acc, dv_acc
):
    length = q_ref.shape[0]
    scale = HEAD_DIM ** (-0.5)
    for start in reversed(range(0, length, tile)):
        keys = start + tile
        allowed = tile_mask(docs_col, docs_row, start, tile)
        q = q_ref[pl.ds(start, tile), :]
        dout = dout_ref[pl.ds(start, tile), :]
        k = k_ref[pl.ds(0, keys), :]
        scores = dot_right_t(q, k) * scale
        probs = jnp.where(allowed, jnp.exp(scores - stat_ref[pl.ds(start, tile), 0:1]), 0.0)
        dprob = dot_right_t(dout, v_ref[pl.ds(0, keys), :])
        delta = jnp.sum(probs * dprob, axis=1, keepdims=True)
        dscores = (probs * (dprob - delta)).astype(BF)
        dq_ref[pl.ds(start, tile), :] = (dot_plain(dscores, k) * scale).astype(BF)
        dk = dot_left_t(dscores, q)
        dv = dot_left_t(probs.astype(BF), dout)
        if keys == length:
            dk_acc[...] = dk
            dv_acc[...] = dv
        else:
            dk_acc[pl.ds(0, keys), :] += dk
            dv_acc[pl.ds(0, keys), :] += dv
    dk_ref[...] = (dk_acc[...] * scale).astype(BF)
    dv_ref[...] = dv_acc[...].astype(BF)


def attention_backward(q, k, v, dout, stat, docs):
    length, lanes = q.shape
    heads = lanes // HEAD_DIM
    tile = min(256, length)
    block = pl.BlockSpec((length, HEAD_DIM), lambda h: (0, h))
    shape = jax.ShapeDtypeStruct((length, lanes), BF)
    return pl.pallas_call(
        lambda *refs: attention_backward_kernel(tile, *refs),
        grid=(heads,),
        in_specs=[
            block,
            block,
            block,
            block,
            block,
            pl.BlockSpec((length, 1), lambda h: (0, 0)),
            pl.BlockSpec((1, length), lambda h: (0, 0)),
        ],
        out_specs=[block, block, block],
        out_shape=[shape, shape, shape],
        scratch_shapes=[pltpu.VMEM((length, HEAD_DIM), F32), pltpu.VMEM((length, HEAD_DIM), F32)],
        compiler_params=pltpu.CompilerParams(vmem_limit_bytes=40 * 2**20),
    )(q, k, v, dout, stat, docs[:, None], docs[None, :])


def ring_attention(queries, kv_here, doc_lengths, tok_len, head_count):
    seq_count = lax.axis_size("seq")
    seq_index = lax.axis_index("seq")
    row_count = queries.shape[0]
    score_scale = HEAD_DIM ** (-0.5)
    local_pos = jnp.arange(tok_len, dtype=jnp.int32)

    def allowed_pairs(source):
        q_positions = seq_index * tok_len + local_pos
        key_pos = source * tok_len + local_pos
        q_docs = doc_numbers(doc_lengths, q_positions)
        key_docs = doc_numbers(doc_lengths, key_pos)
        causal = key_pos[None, :] <= q_positions[:, None]
        same_doc = q_docs[:, :, None] == key_docs[:, None, :]
        return (causal[None] & same_doc)[:, :, None, :]

    def absorb(softmax_state, kv_block, source):
        run_max, totals, accum = softmax_state
        scores = jnp.einsum("rihd,rjhd->rihj", queries, kv_block[0], preferred_element_type=F32)
        allowed = allowed_pairs(source)
        scores = jnp.where(allowed, scores * score_scale, MASKED)
        new_max = jnp.maximum(run_max, jnp.max(scores, axis=-1, keepdims=True))
        weights = jnp.where(allowed, jnp.exp(scores - new_max), 0.0)
        shrink = jnp.exp(run_max - new_max)
        totals = totals * shrink + jnp.sum(weights, axis=-1, keepdims=True)
        accum = accum * shrink + jnp.einsum(
            "rihj,rjhd->rihd", weights.astype(BF), kv_block[1], preferred_element_type=F32
        )
        return (new_max, totals, accum)

    stat_shape = (row_count, tok_len, head_count, 1)
    start_state = (
        jnp.full(stat_shape, MASKED, F32),
        jnp.zeros(stat_shape, F32),
        jnp.zeros((row_count, tok_len, head_count, HEAD_DIM), F32),
    )
    first_state = absorb(start_state, kv_here, seq_index)

    def cycle_forward(section_num, carry):
        softmax_state, kv_block = carry
        kv_block = passed_along(kv_block, "seq", 1)
        source = (seq_index - section_num) % seq_count
        return (absorb(softmax_state, kv_block, source), kv_block)

    final_state, _ = lax.fori_loop(1, seq_count, cycle_forward, (first_state, kv_here))
    run_max, totals, accum = final_state
    outputs = accum / totals
    log_sums = run_max + jnp.log(totals)

    def backward(dout):
        row_delta = jnp.sum(dout.astype(F32) * outputs, axis=-1, keepdims=True)
        head_shape = (row_count, tok_len, head_count, HEAD_DIM)

        def cycle_backward(section_num, carry):
            query_acc, kv_block, grad_block = carry
            source = (seq_index - section_num) % seq_count
            scores = jnp.einsum("rihd,rjhd->rihj", queries, kv_block[0], preferred_element_type=F32)
            allowed = allowed_pairs(source)
            probs = jnp.where(allowed, jnp.exp(scores * score_scale - log_sums), 0.0)
            dprob = jnp.einsum("rihd,rjhd->rihj", dout, kv_block[1], preferred_element_type=F32)
            dscores = (probs * (dprob - row_delta)).astype(BF)
            query_acc = (
                query_acc
                + jnp.einsum("rihj,rjhd->rihd", dscores, kv_block[0], preferred_element_type=F32)
                * score_scale
            )
            key_part = (
                jnp.einsum("rihj,rihd->rjhd", dscores, queries, preferred_element_type=F32)
                * score_scale
            )
            value_part = jnp.einsum(
                "rihj,rihd->rjhd", probs.astype(BF), dout, preferred_element_type=F32
            )
            grad_block = grad_block + jnp.stack([key_part, value_part])
            kv_block = passed_along(kv_block, "seq", 1)
            grad_block = shifted(grad_block.astype(BF), "seq", 1).astype(grad_block.dtype)
            return (query_acc, kv_block, grad_block)

        query_acc, _, grad_block = lax.fori_loop(
            0,
            seq_count,
            cycle_backward,
            (jnp.zeros(head_shape, F32), kv_here, jnp.zeros((2,) + head_shape, F32)),
        )
        return query_acc.astype(BF), grad_block.astype(BF)

    return outputs.astype(BF), backward


def body(
    block_input,
    memory,
    key_cache,
    value_cache,
    doc_lengths,
    gmu_gate,
    gmu_out,
    ffn1_gate,
    ffn1_up,
    ffn1_down,
    query_weight,
    attn_out,
    ffn2_gate,
    ffn2_up,
    ffn2_down,
    gain_a,
    gain_b,
    gain_c,
    gain_d,
    cotangent,
):
    seq_count = lax.axis_size("seq")
    row_count = lax.axis_size("row")
    seq_index = lax.axis_index("seq")
    tok_len = block_input.shape[1]
    width = block_input.shape[2]
    head_count = query_weight.shape[1] // HEAD_DIM
    depth = ffn1_gate.shape[0]
    half = ffn1_gate.shape[1] // 2
    z_count = seq_count // 2
    z_index, y_index = seq_index // 2, seq_index % 2
    parity = z_index % 2

    def spread(normed):
        return lax.all_gather(normed[None], "row", axis=0, tiled=True).reshape(
            row_count * tok_len, width
        )

    def collect(partial_value):
        return lax.psum_scatter(
            partial_value.reshape(row_count, tok_len, width).astype(BF),
            "row",
            scatter_dimension=0,
            tiled=True,
        ).astype(F32)[0]

    def spread_wide(normed):
        both = jnp.stack([normed, swapped(normed, "seq", 2)])
        return lax.all_gather(both[None], "row", axis=0, tiled=True).reshape(
            2 * row_count * tok_len, width
        )

    def collect_wide(partial_value):
        parts = partial_value.reshape(row_count, 2, tok_len, width).astype(BF)
        summed = lax.psum_scatter(parts, "row", scatter_dimension=0, tiled=True)[0]
        other = swapped(summed[1], "seq", 2)
        return summed[0].astype(F32) + other.astype(F32)

    def gather_ffn(gate, up, down):
        shard = jnp.stack([gate, up, down.T])
        whole = jnp.zeros((z_count, 2, 3, depth, half), BF)
        for step in range(z_count):
            want = (parity + step) % 2
            piece = lax.dynamic_slice_in_dim(shard, want * half, half, axis=2)
            if step:
                piece = swapped(piece, "seq", 2 * step)
            over = swapped(piece, "seq", 1)
            source = z_index ^ step
            whole = lax.dynamic_update_slice(whole, piece[None, None], (source, y_index, 0, 0, 0))
            whole = lax.dynamic_update_slice(whole, over[None, None], (source, 1 - y_index, 0, 0, 0))
        whole = whole.transpose(2, 0, 1, 3, 4).reshape(3, seq_count * depth, half)
        return whole[0], whole[1], whole[2]

    def scatter_ffn(gate_grad, up_grad, down_grad_t):
        whole = jnp.stack([gate_grad.astype(BF), up_grad.astype(BF), down_grad_t.astype(BF)])
        whole = whole.reshape(3, z_count, 2, depth, half)
        sums = [None, None]
        for step in range(z_count):
            target = z_index ^ step
            there = lax.dynamic_slice(
                whole, (0, target, 1 - y_index, 0, 0), (3, 1, 1, depth, half)
            )[:, 0, 0]
            here = lax.dynamic_slice(whole, (0, target, y_index, 0, 0), (3, 1, 1, depth, half))[:, 0, 0]
            total = here.astype(F32) + swapped(there, "seq", 1).astype(F32)
            if step:
                total = swapped(total.astype(BF), "seq", 2 * step).astype(F32)
            kind = step % 2
            sums[kind] = total if sums[kind] is None else sums[kind] + total
        pair = jnp.stack(sums)
        lower = lax.dynamic_index_in_dim(pair, parity, 0, keepdims=False)
        upper = lax.dynamic_index_in_dim(pair, 1 - parity, 0, keepdims=False)
        full = jnp.concatenate([lower, upper], axis=2)
        return full[0], full[1], full[2].T

    gmu_gate_full = lax.all_gather(gmu_gate, "seq", axis=0, tiled=True)
    gmu_out_full = lax.all_gather(gmu_out, "seq", axis=1, tiled=True)
    gate_one_w, up_one_w, down_one_t = gather_ffn(ffn1_gate, ffn1_up, ffn1_down)
    query_full = lax.all_gather(query_weight, "seq", axis=0, tiled=True)
    aout_full = lax.all_gather(attn_out, "seq", axis=1, tiled=True)
    gate_two_w, up_two_w, down_two_t = gather_ffn(ffn2_gate, ffn2_up, ffn2_down)

    def ffn_forward(rows_in, gate_weight, up_weight, down_weight_t):
        gate_val = dot_plain(rows_in, gate_weight)
        up_val = dot_plain(rows_in, up_weight)
        hidden = (jax.nn.silu(gate_val) * up_val).astype(BF)
        return (dot_right_t(hidden, down_weight_t), gate_val, up_val, hidden)

    def ffn_backward(cot_rows, rows_in, gate_val, up_val, hidden, gate_weight, up_weight, down_weight_t):
        dhid = dot_plain(cot_rows, down_weight_t)
        dgate = (dhid * up_val * silu_slope(gate_val)).astype(BF)
        dup = (dhid * jax.nn.silu(gate_val)).astype(BF)
        drows = dot_right_t(dgate, gate_weight) + dot_right_t(dup, up_weight)
        down_grad_t = dot_left_t(cot_rows, hidden)
        gate_grad = dot_left_t(rows_in, dgate)
        up_grad = dot_left_t(rows_in, dup)
        return (drows, gate_grad, up_grad, down_grad_t)

    mem_cols = lax.all_to_all(memory, "row", split_axis=2, concat_axis=0, tiled=True)
    mem_cols = mem_cols.reshape(row_count * tok_len, -1).astype(F32)
    kv_here = lax.all_to_all(
        jnp.concatenate([key_cache, value_cache], axis=0)[:, None], "row", split_axis=3, concat_axis=1, tiled=True
    )

    by_heads = seq_count % row_count == 0 and head_count % (seq_count // row_count) == 0
    share = max(1, seq_count // row_count)

    def to_heads(value):
        count = value.shape[0]
        value = value.reshape(count, row_count, tok_len, share, -1).transpose(1, 3, 0, 2, 4)
        value = value.reshape(seq_count, count, tok_len, -1)
        value = lax.all_to_all(value, "seq", split_axis=0, concat_axis=0, tiled=True)
        return value.transpose(1, 0, 2, 3).reshape(count, seq_count * tok_len, -1)

    def from_heads(value):
        count = value.shape[0]
        value = value.reshape(count, seq_count, tok_len, -1).transpose(1, 0, 2, 3)
        value = lax.all_to_all(value, "seq", split_axis=0, concat_axis=0, tiled=True)
        value = value.reshape(row_count, share, count, tok_len, -1).transpose(2, 0, 3, 1, 4)
        return value.reshape(count, row_count, tok_len, head_count * HEAD_DIM)

    x_zero = block_input[0].astype(F32)
    normed_a, inv_a = rms_forward(x_zero, gain_a)
    rows_a = spread(normed_a.astype(BF))
    gmu_pre = dot_plain(rows_a, gmu_gate_full)
    gmu_act = (mem_cols * jax.nn.silu(gmu_pre)).astype(BF)
    x_one = x_zero + collect(dot_plain(gmu_act, gmu_out_full))
    normed_b, inv_b = rms_forward(x_one, gain_b)
    rows_b = spread_wide(normed_b.astype(BF))
    part_one, gate_one, up_one, hidden_one = ffn_forward(rows_b, gate_one_w, up_one_w, down_one_t)
    x_two = x_one + collect_wide(part_one)
    normed_c, inv_c = rms_forward(x_two, gain_c)
    rows_c = spread(normed_c.astype(BF))
    queries = dot_plain(rows_c, query_full).astype(BF)
    if by_heads:
        positions = jnp.arange(seq_count * tok_len, dtype=jnp.int32)
        docs = lax.dynamic_index_in_dim(
            doc_numbers(doc_lengths, positions), seq_index // share, 0, keepdims=False
        )
        kv_heads = to_heads(kv_here)
        q_heads = to_heads(queries.reshape(1, row_count, tok_len, -1))[0]
        out_heads, stats = attention_forward(q_heads, kv_heads[0], kv_heads[1], docs)
        attended = from_heads(out_heads[None])

        def attention_grad(dout):
            dout_heads = to_heads(dout.reshape(1, row_count, tok_len, -1))[0]
            dq, dk, dv = attention_backward(
                q_heads, kv_heads[0], kv_heads[1], dout_heads, stats, docs
            )
            return from_heads(dq[None]), from_heads(jnp.stack([dk, dv]))

    else:
        head_shape = (row_count, tok_len, head_count, HEAD_DIM)
        attended, ring_grad = ring_attention(
            queries.reshape(head_shape), kv_here.reshape((2,) + head_shape), doc_lengths, tok_len, head_count
        )

        def attention_grad(dout):
            return ring_grad(dout.reshape(head_shape))

    attended = attended.reshape(row_count * tok_len, head_count * HEAD_DIM)
    x_three = x_two + collect(dot_plain(attended, aout_full))
    normed_d, inv_d = rms_forward(x_three, gain_d)
    rows_d = spread_wide(normed_d.astype(BF))
    part_two, gate_two, up_two, hidden_two = ffn_forward(rows_d, gate_two_w, up_two_w, down_two_t)
    mixed = x_three + collect_wide(part_two)

    grad_y = cotangent[0].astype(F32)
    drows_d, gate_two_grad, up_two_grad, down_two_grad = ffn_backward(
        spread_wide(cotangent[0]), rows_d, gate_two, up_two, hidden_two, gate_two_w, up_two_w, down_two_t
    )
    dx_d, gain_d_grad = rms_backward(x_three, inv_d, gain_d, collect_wide(drows_d))
    grad_three = grad_y + dx_d
    cot_three = spread(grad_three.astype(BF))
    dattended = dot_right_t(cot_three, aout_full)
    aout_grad = dot_left_t(attended, cot_three)
    dqueries, kv_grad = attention_grad(dattended.astype(BF))
    dqueries = dqueries.reshape(row_count * tok_len, head_count * HEAD_DIM)
    query_grad = dot_left_t(rows_c, dqueries)
    dx_c, gain_c_grad = rms_backward(x_two, inv_c, gain_c, collect(dot_right_t(dqueries, query_full)))
    grad_two = grad_three + dx_c
    drows_b, gate_one_grad, up_one_grad, down_one_grad = ffn_backward(
        spread_wide(grad_two.astype(BF)), rows_b, gate_one, up_one, hidden_one, gate_one_w, up_one_w, down_one_t
    )
    dx_b, gain_b_grad = rms_backward(x_one, inv_b, gain_b, collect_wide(drows_b))
    grad_one = grad_two + dx_b
    cot_one = spread(grad_one.astype(BF))
    dact = dot_right_t(cot_one, gmu_out_full)
    gout_grad = dot_left_t(gmu_act, cot_one)
    mem_grad_cols = dact * jax.nn.silu(gmu_pre)
    dpre = (dact * mem_cols * silu_slope(gmu_pre)).astype(BF)
    gate_a_grad = dot_left_t(rows_a, dpre)
    dx_a, gain_a_grad = rms_backward(x_zero, inv_a, gain_a, collect(dot_right_t(dpre, gmu_gate_full)))
    input_grad = grad_one + dx_a

    mem_grad = lax.all_to_all(
        mem_grad_cols.reshape(row_count, tok_len, -1).astype(BF), "row", split_axis=0, concat_axis=2, tiled=True
    ).astype(F32)
    kv_home = lax.all_to_all(
        kv_grad.reshape(2, row_count, tok_len, -1), "row", split_axis=1, concat_axis=3, tiled=True
    ).astype(F32)

    def scatter(grad, dim):
        return lax.psum_scatter(grad.astype(BF), "seq", scatter_dimension=dim, tiled=True).astype(F32)

    gate_two_out, up_two_out, down_two_out = scatter_ffn(gate_two_grad, up_two_grad, down_two_grad)
    aout_out = scatter(aout_grad, 1)
    query_out = scatter(query_grad, 0)
    gate_one_out, up_one_out, down_one_out = scatter_ffn(gate_one_grad, up_one_grad, down_one_grad)
    gout_out = scatter(gout_grad, 1)
    gate_a_out = scatter(gate_a_grad, 0)
    gain_grads = lax.psum((gain_a_grad, gain_b_grad, gain_c_grad, gain_d_grad), ("seq", "row"))
    return (
        mixed[None],
        input_grad[None],
        mem_grad,
        kv_home[0],
        kv_home[1],
        gate_a_out,
        gout_out,
        gate_one_out,
        up_one_out,
        down_one_out,
        query_out,
        aout_out,
        gate_two_out,
        up_two_out,
        down_two_out,
        gain_grads[0],
        gain_grads[1],
        gain_grads[2],
        gain_grads[3],
    )


def solution(mesh):
    tokens = P("row", "seq", None)
    inner, outer = P("seq", "row"), P("row", "seq")
    in_specs = (
        (tokens,) * 4
        + (P(), inner, outer, inner, inner, outer, inner, outer, inner, inner, outer)
        + (P(),) * 4
        + (tokens,)
    )
    out_specs = (
        (tokens,) * 5
        + (inner, outer, inner, inner, outer, inner, outer, inner, inner, outer)
        + (P(),) * 4
    )
    return jax.shard_map(body, mesh=mesh, in_specs=in_specs, out_specs=out_specs, check_vma=False)
```

```python
from types import SimpleNamespace

import jax
import jax.numpy as jnp
from jax import lax
from jax.experimental import pallas as pl
from jax.experimental.pallas import tpu as pltpu
from jax.sharding import PartitionSpec as P

HEAD_DIM = 128


EPSILON = 1e-05
MASKED = -1e30
BF = jnp.bfloat16
F32 = jnp.float32


def passed_along(value, axis, steps):
    count = lax.axis_size(axis)
    first, last = (max(0, -steps), min(count, count - steps))
    return lax.ppermute(value, axis, [(source, source + steps) for source in range(first, last)])


def shifted(value, axis, steps):
    count = lax.axis_size(axis)
    pairs = [(source, (source + steps) % count) for source in range(count)]
    return lax.ppermute(value, axis, pairs)


def swapped(value, axis, mask):
    count = lax.axis_size(axis)
    return lax.ppermute(value, axis, [(source, source ^ mask) for source in range(count)])


def silu_slope(values):
    sigmoid = jax.nn.sigmoid(values)
    return sigmoid * (1.0 + values * (1.0 - sigmoid))


def rms_forward(values, gain_vec):
    inverse = lax.rsqrt(jnp.mean(values * values, axis=-1, keepdims=True) + EPSILON)
    return (values * inverse * gain_vec, inverse)


def rms_backward(values, inverse, gain_vec, grad_normed):
    scaled = grad_normed * gain_vec
    gain_grad = jnp.sum(grad_normed * values * inverse, axis=0)
    inner_sum = jnp.mean(scaled * values, axis=-1, keepdims=True)
    return (inverse * scaled - values * inverse * inverse * inverse * inner_sum, gain_grad)


def doc_numbers(doc_lengths, positions):
    doc_ends = jnp.cumsum(doc_lengths, axis=1, dtype=jnp.int32)
    return jnp.sum((positions[None, :, None] >= doc_ends[:, None, :]).astype(jnp.int32), axis=-1)


def dot_plain(left, right):
    return jnp.dot(left, right, preferred_element_type=F32)


def dot_left_t(left, right):
    return lax.dot_general(left, right, (((0,), (0,)), ((), ())), preferred_element_type=F32)


def dot_right_t(left, right):
    return lax.dot_general(left, right, (((1,), (1,)), ((), ())), preferred_element_type=F32)


def ring_attention(queries, kv_here, doc_lengths, tok_len, head_count):
    seq_count = lax.axis_size("seq")
    seq_index = lax.axis_index("seq")
    row_count = queries.shape[0]
    score_scale = HEAD_DIM ** (-0.5)
    local_pos = jnp.arange(tok_len, dtype=jnp.int32)

    def allowed_pairs(source):
        q_positions = seq_index * tok_len + local_pos
        key_pos = source * tok_len + local_pos
        q_docs = doc_numbers(doc_lengths, q_positions)
        key_docs = doc_numbers(doc_lengths, key_pos)
        causal = key_pos[None, :] <= q_positions[:, None]
        same_doc = q_docs[:, :, None] == key_docs[:, None, :]
        return (causal[None] & same_doc)[:, :, None, :]

    def absorb(softmax_state, kv_block, source):
        run_max, totals, accum = softmax_state
        scores = jnp.einsum("rihd,rjhd->rihj", queries, kv_block[0], preferred_element_type=F32)
        allowed = allowed_pairs(source)
        scores = jnp.where(allowed, scores * score_scale, MASKED)
        new_max = jnp.maximum(run_max, jnp.max(scores, axis=-1, keepdims=True))
        weights = jnp.where(allowed, jnp.exp(scores - new_max), 0.0)
        shrink = jnp.exp(run_max - new_max)
        totals = totals * shrink + jnp.sum(weights, axis=-1, keepdims=True)
        accum = accum * shrink + jnp.einsum(
            "rihj,rjhd->rihd", weights.astype(BF), kv_block[1], preferred_element_type=F32
        )
        return (new_max, totals, accum)

    stat_shape = (row_count, tok_len, head_count, 1)
    start_state = (
        jnp.full(stat_shape, MASKED, F32),
        jnp.zeros(stat_shape, F32),
        jnp.zeros((row_count, tok_len, head_count, HEAD_DIM), F32),
    )
    first_state = absorb(start_state, kv_here, seq_index)

    def cycle_forward(section_num, carry):
        softmax_state, kv_block = carry
        kv_block = passed_along(kv_block, "seq", 1)
        source = (seq_index - section_num) % seq_count
        return (absorb(softmax_state, kv_block, source), kv_block)

    final_state, _ = lax.fori_loop(1, seq_count, cycle_forward, (first_state, kv_here))
    run_max, totals, accum = final_state
    outputs = accum / totals
    log_sums = run_max + jnp.log(totals)

    def backward(dout):
        row_delta = jnp.sum(dout.astype(F32) * outputs, axis=-1, keepdims=True)
        head_shape = (row_count, tok_len, head_count, HEAD_DIM)

        def cycle_backward(section_num, carry):
            query_acc, kv_block, grad_block = carry
            source = (seq_index - section_num) % seq_count
            scores = jnp.einsum("rihd,rjhd->rihj", queries, kv_block[0], preferred_element_type=F32)
            allowed = allowed_pairs(source)
            probs = jnp.where(allowed, jnp.exp(scores * score_scale - log_sums), 0.0)
            dprob = jnp.einsum("rihd,rjhd->rihj", dout, kv_block[1], preferred_element_type=F32)
            dscores = (probs * (dprob - row_delta)).astype(BF)
            query_acc = (
                query_acc
                + jnp.einsum("rihj,rjhd->rihd", dscores, kv_block[0], preferred_element_type=F32)
                * score_scale
            )
            key_part = (
                jnp.einsum("rihj,rihd->rjhd", dscores, queries, preferred_element_type=F32)
                * score_scale
            )
            value_part = jnp.einsum(
                "rihj,rihd->rjhd", probs.astype(BF), dout, preferred_element_type=F32
            )
            grad_block = grad_block + jnp.stack([key_part, value_part])
            kv_block = passed_along(kv_block, "seq", 1)
            grad_block = shifted(grad_block.astype(BF), "seq", 1).astype(grad_block.dtype)
            return (query_acc, kv_block, grad_block)

        query_acc, _, grad_block = lax.fori_loop(
            0,
            seq_count,
            cycle_backward,
            (jnp.zeros(head_shape, F32), kv_here, jnp.zeros((2,) + head_shape, F32)),
        )
        return query_acc.astype(BF), grad_block.astype(BF)

    return outputs.astype(BF), backward


MESH = pl.DeviceIdType.MESH
VMEM_LIMIT = 62 * 2**20


def flipped(value, mask):
    bit = 1
    while bit <= mask:
        if mask & bit:
            value = value + bit - 2 * bit * lax.rem(lax.div(value, bit), 2)
        bit *= 2
    return value


def rows_at(index, size):
    return pl.ds(pl.multiple_of(index * size, size), size)


def part_of(index, size):
    return pl.ds(index * size, size)


class Links:
    def __init__(self, send, recv):
        self.send, self.recv, self.used, self.sent = send, recv, 0, []
        self.row, self.seq = lax.axis_index("row"), lax.axis_index("seq")
        self.z, self.y = lax.div(self.seq, 2), lax.rem(self.seq, 2)
        self.parity = lax.rem(self.z, 2)

    def device(self, row_mask, seq_mask):
        return {"row": flipped(self.row, row_mask), "seq": flipped(self.seq, seq_mask)}

    def greet(self, masks):
        barrier = pltpu.get_barrier_semaphore()
        for mask in masks:
            pl.semaphore_signal(barrier, inc=1, device_id=self.device(*mask), device_id_type=MESH)
        pl.semaphore_wait(barrier, len(masks))

    def slot(self):
        self.used += 1
        assert self.used <= self.send.shape[0]
        return self.used - 1

    def copy(self, src, dst, row_mask, seq_mask):
        slot = self.slot()
        move = pltpu.make_async_remote_copy(
            src_ref=src,
            dst_ref=dst,
            send_sem=self.send.at[slot],
            recv_sem=self.recv.at[slot],
            device_id=self.device(row_mask, seq_mask),
            device_id_type=MESH,
        )
        move.start()
        self.sent.append(move)
        return move

    def local(self, src, dst):
        move = pltpu.make_async_copy(src, dst, self.send.at[self.slot()])
        move.start()
        return move

    def finish(self, moves=None):
        moves = list(self.sent if moves is None else moves)
        for move in moves:
            move.wait_send()
        done = {id(move) for move in moves}
        self.sent = [move for move in self.sent if id(move) not in done]


def wait(moves):
    for move in moves:
        move.wait()


def landed(moves):
    for move in moves[0]:
        move.wait_recv()
    moves[1].wait()


class Gather:
    def __init__(self, links, shard, whole, outer, parts):
        self.links, self.shard, self.whole, self.outer, self.parts = links, shard, whole, outer, parts
        self.z_moves, self.y_moves = {}, {}

    def piece(self, step):
        if self.parts == 1:
            return self.shard
        part = lax.rem(self.links.parity + step, 2)
        if self.outer:
            return self.shard.at[rows_at(part, self.shard.shape[0] // 2), :]
        return self.shard.at[:, rows_at(part, self.shard.shape[1] // 2)]

    def place(self, source):
        if self.outer:
            return self.whole.at[:, rows_at(source, self.shard.shape[1])]
        return self.whole.at[rows_at(source, self.shard.shape[0]), :]

    def own(self):
        self.keep = self.links.local(self.piece(0), self.place(self.links.seq))
        self.y_moves[0] = self.links.copy(self.piece(0), self.place(self.links.seq), 0, 1)

    def over_z(self, *steps):
        for step in steps:
            if step == 3 and self.parts == 1:
                self.z_moves[2].wait_recv()
                here = self.place(flipped(self.links.seq, 4))
                self.z_moves[3] = self.links.copy(here, here, 0, 2)
            else:
                self.z_moves[step] = self.links.copy(self.piece(step), self.place(self.links.seq), 0, 2 * step)

    def over_y(self, *steps):
        for step in steps:
            if not (step == 2 and 3 in self.z_moves and self.parts == 1):
                self.z_moves[step].wait_recv()
            here = self.place(flipped(self.links.seq, 2 * step))
            self.y_moves[step] = self.links.copy(here, here, 0, 1)

    def arrived(self):
        self.keep.wait()
        for step in range(4):
            self.y_moves[step].wait_recv()


def each(weights, action, *steps):
    for step in steps:
        for weight in weights:
            action(weight, step)


def chip_masks(wide):
    return [(0, 0), (2, 0)] + ([(0, 2), (2, 2)] if wide else [])


def chip_rows(links, mask, wide, tok):
    chip = lax.div(flipped(links.row, mask[0]), 2)
    if wide:
        chip = chip * 2 + lax.rem(links.parity + mask[1] // 2, 2)
    return rows_at(chip, 2 * tok)


def block_rows(links, mask, wide, tok, other=0):
    chip = lax.div(flipped(links.row, mask[0]), 2)
    if wide:
        chip = chip * 2 + lax.rem(links.parity + mask[1] // 2, 2)
    return rows_at(chip * 2 + lax.rem(links.row + other, 2), tok)


class Spread:
    def __init__(self, links, whole, wide, tok):
        self.links, self.whole, self.wide, self.tok = links, whole, wide, tok
        self.masks = chip_masks(wide)

    def place(self, mask):
        return self.whole.at[block_rows(self.links, mask, self.wide, self.tok), :]

    def own(self):
        return block_rows(self.links, (0, 0), self.wide, self.tok)

    def start(self):
        here = self.place((0, 0))
        self.far = [self.links.copy(here, here, *mask) for mask in self.masks[1:]]
        self.near = [self.links.copy(here, here, 1, 0)]

    def forward(self):
        for mask, move in zip(self.masks[1:], self.far):
            move.wait_recv()
            there = self.place(mask)
            self.near.append(self.links.copy(there, there, 1, 0))

    def wait(self):
        for move in self.near:
            move.wait_recv()

    def by_chip(self, compute):
        for k, mask in enumerate(self.masks):
            if k:
                self.far[k - 1].wait_recv()
                there = self.place(mask)
                self.near.append(self.links.copy(there, there, 1, 0))
            self.near[k].wait_recv()
            compute(chip_rows(self.links, mask, self.wide, self.tok))

    def finish(self):
        self.links.finish(self.far + self.near)


class Collect:
    def __init__(self, links, parts, from_core, from_far, wide, tok):
        self.links, self.parts, self.wide, self.tok = links, parts, wide, tok
        self.from_core, self.from_far = from_core, from_far
        self.masks = chip_masks(wide)
        self.near, self.far = {}, {}

    def block(self, mask, other=0):
        return self.parts.at[block_rows(self.links, mask, self.wide, self.tok, other), :]

    def slot(self, ref, k):
        return ref.at[part_of(k, self.tok), :]

    def forward(self, k):
        self.near[k].wait_recv()
        mine = self.block(self.masks[k])
        mine[...] = (mine[...].astype(F32) + self.slot(self.from_core, k)[...].astype(F32)).astype(BF)
        self.far[k] = self.links.copy(mine, self.slot(self.from_far, k - 1), *self.masks[k])

    def run(self, compute):
        last = len(self.masks) - 1
        for k in range(last, -1, -1):
            compute(chip_rows(self.links, self.masks[k], self.wide, self.tok))
            self.near[k] = self.links.copy(self.block(self.masks[k], 1), self.slot(self.from_core, k), 1, 0)
            if k < last:
                self.forward(k + 1)

    def result(self):
        self.near[0].wait_recv()
        total = self.block((0, 0))[...].astype(F32) + self.slot(self.from_core, 0)[...].astype(F32)
        for k in range(1, len(self.masks)):
            self.far[k].wait_recv()
            total = total + self.slot(self.from_far, k - 1)[...].astype(F32)
        return total

    def finish(self):
        self.links.finish(list(self.near.values()) + list(self.far.values()))


def normed_block(values, gain):
    inverse = lax.rsqrt(jnp.mean(values * values, axis=-1, keepdims=True) + EPSILON)
    return (values * inverse * gain).astype(BF)


def norm_back(values, gain, grad_normed):
    inverse = lax.rsqrt(jnp.mean(values * values, axis=-1, keepdims=True) + EPSILON)
    scaled = grad_normed * gain
    gain_grad = jnp.sum(grad_normed * values * inverse, axis=0, keepdims=True)
    inner_sum = jnp.mean(scaled * values, axis=-1, keepdims=True)
    return inverse * scaled - values * inverse * inverse * inverse * inner_sum, gain_grad


def silu(values):
    return values * jax.nn.sigmoid(values)


def columns_loop(columns, tile, step):
    @pl.loop(0, columns // tile)
    def _(index):
        step(rows_at(index, tile))


def to_heads(links, src, dst, tok):
    wide = dst.shape[1]

    def block(seq):
        return src.at[rows_at(lax.div(seq, 2), tok), rows_at(lax.rem(seq, 2), wide)]

    here = dst.at[rows_at(links.seq, tok), :]
    moves = [links.copy(block(flipped(links.seq, mask)), here, 0, mask) for mask in range(1, 8)]
    return moves, links.local(block(links.seq), here)


def from_heads(links, src, dst, tok):
    wide = src.shape[1]
    here = dst.at[rows_at(links.z, tok), rows_at(links.y, wide)]
    moves = [links.copy(src.at[rows_at(flipped(links.seq, mask), tok), :], here, 0, mask) for mask in range(1, 8)]
    return moves, links.local(src.at[rows_at(links.seq, tok), :], here)


def to_columns(links, src, dst, tok, cols):
    here = dst.at[rows_at(links.row, tok), :]
    moves = [links.copy(src.at[:, rows_at(flipped(links.row, mask), cols)], here, mask, 0) for mask in (1, 2, 3)]
    return moves, links.local(src.at[:, rows_at(links.row, cols)], here)


def from_columns(links, src, dst, tok, cols):
    here = dst.at[:, rows_at(links.row, cols)]
    moves = [links.copy(src.at[rows_at(flipped(links.row, mask), tok), :], here, mask, 0) for mask in (1, 2, 3)]
    return moves, links.local(src.at[rows_at(links.row, tok), :], here)


def tile_mask(docs_col, docs_row, start, tile):
    keys = start + tile
    q_pos = lax.broadcasted_iota(jnp.int32, (tile, keys), 0) + start
    k_pos = lax.broadcasted_iota(jnp.int32, (tile, keys), 1)
    return (k_pos <= q_pos) & (docs_col[pl.ds(start, tile), :] == docs_row[:, pl.ds(0, keys)])


def softmax_tile(q, k, docs_col, docs_row, start, tile):
    scores = dot_right_t(q, k) * (HEAD_DIM ** (-0.5))
    scores = jnp.where(tile_mask(docs_col, docs_row, start, tile), scores, MASKED)
    expo = jnp.exp(scores - jnp.max(scores, axis=1, keepdims=True))
    return expo * (1.0 / jnp.sum(expo, axis=1, keepdims=True))


def attend(q_ref, k_ref, v_ref, docs_col, docs_row, out_ref):
    length = q_ref.shape[0]
    tile = min(256, length)

    @pl.loop(0, q_ref.shape[1] // HEAD_DIM)
    def _(head):
        lanes = rows_at(head, HEAD_DIM)
        for start in range(0, length, tile):
            keys, here = pl.ds(0, start + tile), pl.ds(start, tile)
            probs = softmax_tile(q_ref[here, lanes], k_ref[keys, lanes], docs_col, docs_row, start, tile)
            out_ref[here, lanes] = dot_plain(probs.astype(BF), v_ref[keys, lanes]).astype(BF)


def attend_back(q_ref, k_ref, v_ref, dout_ref, docs_col, docs_row, dq_ref, dk_ref, dv_ref, dk_acc, dv_acc):
    length = q_ref.shape[0]
    tile = min(256, length)
    scale = HEAD_DIM ** (-0.5)

    @pl.loop(0, q_ref.shape[1] // HEAD_DIM)
    def _(head):
        lanes = rows_at(head, HEAD_DIM)
        for start in reversed(range(0, length, tile)):
            keys, here = pl.ds(0, start + tile), pl.ds(start, tile)
            q, k, dout = q_ref[here, lanes], k_ref[keys, lanes], dout_ref[here, lanes]
            probs = softmax_tile(q, k, docs_col, docs_row, start, tile)
            dprob = dot_right_t(dout, v_ref[keys, lanes])
            delta = jnp.sum(probs * dprob, axis=1, keepdims=True)
            dscores = (probs * (dprob - delta)).astype(BF)
            dq_ref[here, lanes] = (dot_plain(dscores, k) * scale).astype(BF)
            dk, dv = dot_left_t(dscores, q), dot_left_t(probs.astype(BF), dout)
            if start + tile == length:
                dk_acc[...] = dk
                dv_acc[...] = dv
            else:
                dk_acc[keys, :] += dk
                dv_acc[keys, :] += dv
        dk_ref[:, lanes] = (dk_acc[...] * scale).astype(BF)
        dv_ref[:, lanes] = dv_acc[...].astype(BF)


def hidden_rows(r, rows_in, rows):
    def step(at):
        gate_val = dot_plain(rows_in[rows, :], r.gate_v[:, at])
        up_val = dot_plain(rows_in[rows, :], r.up_v[:, at])
        r.gate[rows, at] = gate_val.astype(BF)
        r.up[rows, at] = up_val.astype(BF)
        r.hidden[rows, at] = (silu(gate_val) * up_val).astype(BF)

    columns_loop(r.gate.shape[1], 256, step)


def hidden_back(r, rows):
    def step(at):
        dhid = dot_right_t(r.cot[rows, :], r.down_v[at, :])
        gate_val, up_val = r.gate[rows, at].astype(F32), r.up[rows, at].astype(F32)
        sigmoid = jax.nn.sigmoid(gate_val)
        r.gate[rows, at] = (dhid * up_val * (sigmoid * (1.0 + gate_val * (1.0 - sigmoid)))).astype(BF)
        r.up[rows, at] = (dhid * (gate_val * sigmoid)).astype(BF)

    columns_loop(r.gate.shape[1], 512, step)


def plain_rows(left, right, out):
    def compute(rows):
        def step(at):
            out[rows, at] = dot_plain(left[rows, :], right[:, at]).astype(BF)

        columns_loop(right.shape[1], 1024, step)

    return compute


def turned_rows(pairs, out):
    def compute(rows):
        def step(at):
            value = dot_right_t(pairs[0][0][rows, :], pairs[0][1][at, :])
            for left, right in pairs[1:]:
                value = value + dot_right_t(left[rows, :], right[at, :])
            out[rows, at] = value.astype(BF)

        columns_loop(pairs[0][1].shape[0], 512, step)

    return compute


def run_kernel(kernel, ident, moves, large, small, outs, scratch):
    anywhere = pl.BlockSpec(memory_space=pl.ANY)
    whole = pl.BlockSpec(memory_space=pltpu.VMEM)
    names = [*large, *small, *outs, *scratch]

    def body(*refs):
        kernel(Links(*refs[-2:]), SimpleNamespace(**dict(zip(names, refs[:-2], strict=True))))

    results = pl.pallas_call(
        body,
        out_shape=[jax.ShapeDtypeStruct(*item) for item in outs.values()],
        in_specs=[anywhere] * len(large) + [whole] * len(small),
        out_specs=[anywhere] * len(outs),
        scratch_shapes=[pltpu.VMEM(*item) for item in scratch.values()] + [pltpu.SemaphoreType.DMA((moves,))] * 2,
        compiler_params=pltpu.CompilerParams(
            collective_id=ident, has_side_effects=True, vmem_limit_bytes=VMEM_LIMIT
        ),
    )(*large.values(), *small.values())
    return SimpleNamespace(**dict(zip(outs, results, strict=True)))


def typed(kind, **shapes):
    return {name: (dims, kind) for name, dims in shapes.items()}


ALL_MASKS = [(1, 0), (2, 0), (3, 0), (0, 2), (2, 2)] + [(0, mask) for mask in (1, 3, 4, 5, 6, 7)]


def forward_kernel(links, r):
    links.greet(ALL_MASKS)
    row = links.row
    tok, width = r.x.shape
    cols = r.gmu_gate.shape[1]
    part = r.part
    outs = []

    def keep(ref, out):
        outs.append(links.local(ref, out))

    gmu_in, gmu_to = Gather(links, r.gmu_gate, r.gmu_gate_w, False, 1), Gather(links, r.gmu_out, r.gmu_out_w, True, 1)
    weights_g = [gmu_in, gmu_to]
    weights_1 = [
        Gather(links, r.f1_gate, r.f1_gate_w, False, 2),
        Gather(links, r.f1_up, r.f1_up_w, False, 2),
        Gather(links, r.f1_down, r.f1_down_w, True, 2),
    ]
    weights_q = [Gather(links, r.query, r.query_w, False, 1), Gather(links, r.attn_out, r.attn_out_w, True, 1)]
    weights_2 = [
        Gather(links, r.f2_gate, r.f2_gate_w, False, 2),
        Gather(links, r.f2_up, r.f2_up_w, False, 2),
        Gather(links, r.f2_down, r.f2_down_w, True, 2),
    ]
    gate_2, up_2, down_2 = weights_2

    each(weights_g, Gather.over_z, 2, 1)
    for weight in weights_g:
        weight.own()

    spread_a = Spread(links, r.rows_a, False, tok)
    r.rows_a[spread_a.own(), :] = normed_block(r.x[...].astype(F32), r.gain_a[...])
    spread_a.start()
    k_cols = to_columns(links, r.keys, r.k_cols, tok, cols)
    v_cols = to_columns(links, r.values, r.v_cols, tok, cols)
    mem_moves = to_columns(links, r.memory, r.mem, tok, cols)
    spread_a.forward()
    landed(k_cols)
    landed(v_cols)
    k_moves = to_heads(links, r.k_cols, r.k_heads, tok)
    v_moves = to_heads(links, r.v_cols, r.v_heads, tok)
    each(weights_g, Gather.over_z, 3)
    each(weights_1, Gather.over_z, 2, 1, 3)
    each(weights_g, Gather.over_y, 2, 1, 3)
    for weight in weights_1 + weights_q + [gate_2]:
        weight.own()
    spread_a.wait()
    landed(mem_moves)
    keep(r.rows_a, r.rows_a_out)
    keep(r.mem, r.mem_out)
    gmu_in.arrived()
    load_in = links.local(r.gmu_gate_w, r.in_v)
    gmu_to.arrived()
    load_out = links.local(r.gmu_out_w, r.out_v)
    load_in.wait()

    def gmu_step(at):
        value = dot_plain(r.rows_a[...], r.in_v[:, at])
        r.pre[:, at] = value.astype(BF)
        r.act[:, at] = (r.mem[:, at].astype(F32) * silu(value)).astype(BF)

    columns_loop(cols, 256, gmu_step)
    load_out.wait()
    collect_a = Collect(links, part, r.core_a, r.far_a, False, tok)
    collect_a.run(plain_rows(r.act, r.out_v, part))
    keep(r.pre, r.pre_out)
    keep(r.act, r.act_out)
    r.x_one[...] = r.x[...].astype(F32) + collect_a.result()
    keep(r.x_one, r.x_one_out)

    spread_b = Spread(links, r.rows_b, True, tok)
    r.rows_b[spread_b.own(), :] = normed_block(r.x_one[...], r.gain_b[...])
    spread_b.start()
    each(weights_q, Gather.over_z, 2, 1)
    each(weights_1, Gather.over_y, 2, 1, 3)
    spread_b.forward()
    spread_b.wait()
    keep(r.rows_b, r.rows_b_out)
    each(weights_q, Gather.over_z, 3)
    gate_2.over_z(2, 1, 3)
    loads = []
    for weight, place in zip(weights_1, (r.gate_v, r.up_v, r.down_v)):
        weight.arrived()
        loads.append(links.local(weight.whole, place))
    collect_a.finish()
    wait(loads)
    hidden_rows(r, r.rows_b, pl.ds(0, 8 * tok))
    spread_a.finish()
    outs[0].wait()
    del outs[0]
    collect_b = Collect(links, part, r.core_b, r.far_b, True, tok)
    collect_b.run(plain_rows(r.hidden, r.down_v, part))
    up_2.over_z(2, 1, 3)
    each(weights_q, Gather.over_y, 2, 1, 3)
    gate_2.over_y(2, 1, 3)
    landed(k_moves)
    landed(v_moves)
    keep(r.k_heads, r.k_heads_out)
    keep(r.v_heads, r.v_heads_out)
    keep(r.gate, r.gate_out)
    keep(r.up, r.up_out)
    keep(r.hidden, r.hidden_out)
    r.x_two[...] = r.x_one[...] + collect_b.result()
    keep(r.x_two, r.x_two_out)

    spread_c = Spread(links, r.rows_a, False, tok)
    r.rows_a[spread_c.own(), :] = normed_block(r.x_two[...], r.gain_c[...])
    spread_c.start()
    loads = []
    for weight, place in zip(weights_q, (r.in_v, r.out_v)):
        weight.arrived()
        loads.append(links.local(weight.whole, place))
    spread_c.forward()
    wait(loads)
    spread_c.wait()
    keep(r.rows_a, r.rows_c_out)

    def query_step(at):
        r.q_cols[:, at] = dot_plain(r.rows_a[...], r.in_v[:, at]).astype(BF)

    columns_loop(cols, 512, query_step)
    q_moves = to_heads(links, r.q_cols, r.q_heads, tok)
    down_2.over_z(2, 1)
    up_2.own()
    up_2.over_y(2, 1)
    landed(q_moves)
    keep(r.q_heads, r.q_heads_out)
    attend(r.q_heads, r.k_heads, r.v_heads, r.docs_col, r.docs_row, r.out_heads)
    spread_b.finish()
    wait(outs)
    outs.clear()
    out_moves = from_heads(links, r.out_heads, r.attended, tok)
    down_2.over_z(3)
    up_2.over_y(3)
    down_2.own()
    landed(out_moves)
    keep(r.attended, r.attended_out)
    collect_b.finish()
    collect_c = Collect(links, part, r.core_c, r.far_c, False, tok)
    collect_c.run(plain_rows(r.attended, r.out_v, part))
    r.x_three[...] = r.x_two[...] + collect_c.result()
    keep(r.x_three, r.x_three_out)
    spread_d = Spread(links, r.rows_b, True, tok)
    r.rows_b[spread_d.own(), :] = normed_block(r.x_three[...], r.gain_d[...])
    spread_d.start()
    spread_d.forward()
    down_2.over_y(2, 1, 3)
    spread_d.wait()
    keep(r.rows_b, r.rows_d_out)
    for weight in weights_2:
        weight.arrived()
    wait(outs)
    links.finish()


def forward_pass(large, small):
    tok, width = small["x"].shape
    cols = large["gmu_gate"].shape[1]
    half = large["f1_gate"].shape[1] // 2
    tokens = 4 * tok
    positions = small["docs_col"].shape[0]
    heads = (positions, cols * tokens // positions)
    inner, outer = (width, half), (half, width)
    outs = typed(
        BF,
        gmu_gate_w=(width, cols),
        gmu_out_w=(cols, width),
        f1_gate_w=inner,
        f1_up_w=inner,
        f1_down_w=outer,
        query_w=(width, cols),
        attn_out_w=(cols, width),
        f2_gate_w=inner,
        f2_up_w=inner,
        f2_down_w=outer,
        rows_a_out=(tokens, width),
        mem_out=(tokens, cols),
        pre_out=(tokens, cols),
        act_out=(tokens, cols),
        rows_b_out=(2 * tokens, width),
        gate_out=(2 * tokens, half),
        up_out=(2 * tokens, half),
        hidden_out=(2 * tokens, half),
        rows_c_out=(tokens, width),
        q_heads_out=heads,
        k_heads_out=heads,
        v_heads_out=heads,
        attended_out=(tokens, cols),
        rows_d_out=(2 * tokens, width),
    ) | typed(F32, x_one_out=(tok, width), x_two_out=(tok, width), x_three_out=(tok, width))
    scratch = typed(
        BF,
        rows_a=(tokens, width),
        mem=(tokens, cols),
        k_cols=(tokens, cols),
        v_cols=(tokens, cols),
        in_v=(width, cols),
        out_v=(cols, width),
        pre=(tokens, cols),
        act=(tokens, cols),
        part=(2 * tokens, width),
        core_a=(2 * tok, width),
        far_a=(tok, width),
        core_b=(4 * tok, width),
        far_b=(3 * tok, width),
        core_c=(2 * tok, width),
        far_c=(tok, width),
        rows_b=(2 * tokens, width),
        gate_v=inner,
        up_v=inner,
        down_v=outer,
        gate=(2 * tokens, half),
        up=(2 * tokens, half),
        hidden=(2 * tokens, half),
        q_cols=(tokens, cols),
        q_heads=heads,
        k_heads=heads,
        v_heads=heads,
        out_heads=heads,
        attended=(tokens, cols),
    ) | typed(F32, x_one=(tok, width), x_two=(tok, width), x_three=(tok, width))
    return run_kernel(forward_kernel, 0, 256, large, small, outs, scratch)


def weight_blocks(links, order, pairs, stages, blocks):
    size = stages[0].shape[0]
    depth = size // len(pairs)
    moves = [None, None]
    for count, block in enumerate(order):
        stage, kind = stages[count % 2], count % 2
        if moves[kind] is not None:
            moves[kind].wait()
        at = rows_at(block, depth)
        for k, (left, right) in enumerate(pairs):
            stage[part_of(k, depth), :] = dot_left_t(left[:, at], right[...]).astype(BF)
        moves[kind] = links.local(stage, blocks.at[rows_at(block, size), :])
    for move in moves:
        if move is not None:
            move.wait()


class Scatter:
    def __init__(self, links, blocks, land_y, land_z, here, there, total, out, parts):
        self.links, self.blocks, self.land_y, self.land_z = links, blocks, land_y, land_z
        self.here, self.there, self.total, self.out, self.parts = here, there, total, out, parts
        self.size = blocks.shape[0] // 8
        self.y_moves, self.z_moves = {}, {}

    def slot(self, ref, k):
        return ref.at[part_of(k, self.size), :]

    def block(self, step, y):
        return self.blocks.at[rows_at(2 * flipped(self.links.z, step) + y, self.size), :]

    def over_y(self, *steps):
        for step in steps:
            self.y_moves[step] = self.links.copy(
                self.block(step, 1 - self.links.y), self.slot(self.land_y, step), 0, 1
            )

    def over_z(self, *steps):
        for step in steps:
            first = self.links.local(self.block(step, self.links.y), self.here)
            self.y_moves[step].wait_recv()
            mine = self.slot(self.land_y, step)
            second = self.links.local(mine, self.there)
            first.wait()
            second.wait()
            total = self.here[...].astype(F32) + self.there[...].astype(F32)
            mask = 2 * step
            if self.parts == 1 and step == 2:
                self.z_moves[3].wait_recv()
                self.links.local(self.slot(self.land_z, 2), self.there).wait()
                total = total + self.there[...].astype(F32)
            elif self.parts == 1 and step == 3:
                mask = 2
            self.here[...] = total.astype(BF)
            self.links.local(self.here, mine).wait()
            self.z_moves[step] = self.links.copy(mine, self.slot(self.land_z, step - 1), 0, mask)

    def finish(self):
        rows, width = self.total.shape
        self.y_moves[0].wait_recv()
        steps = (2, 1) if self.parts == 1 else (2, 1, 3)
        for step in steps:
            self.z_moves[step].wait_recv()
        sources = [self.block(0, self.links.y), self.slot(self.land_y, 0)]
        sources += [self.slot(self.land_z, step - 1) for step in steps]
        parity = self.links.parity
        for start in range(0, self.size, rows):
            here = pl.ds(start, rows)
            spots = [ref.at[part_of(k, rows), :] for ref in (self.here, self.there) for k in range(2)]
            wait([self.links.local(source.at[here, :], spot) for source, spot in zip(sources, spots)])
            self.total[...] = spots[0][...].astype(F32) + spots[1][...].astype(F32) + spots[2][...].astype(F32)
            if self.parts == 1:
                self.total[...] = self.total[...] + spots[3][...].astype(F32)
                self.links.local(self.total, self.out.at[here, :]).wait()
            else:
                last = self.links.local(sources[4].at[here, :], spots[0])
                self.links.local(self.total, self.out.at[here, rows_at(parity, width)]).wait()
                last.wait()
                self.total[...] = spots[3][...].astype(F32) + spots[0][...].astype(F32)
                self.links.local(self.total, self.out.at[here, rows_at(1 - parity, width)]).wait()
        self.links.finish(list(self.y_moves.values()) + list(self.z_moves.values()))


def backward_kernel(links, r):
    links.greet(ALL_MASKS)
    row, seq, y = links.row, links.seq, links.y
    tok, width = r.grad.shape
    cols = r.left.shape[1]
    half = r.gate.shape[1]
    part, grad = r.part, r.grad
    everything = pl.ds(0, 8 * tok)
    outs = []
    stages = [r.stage_0, r.stage_1]
    small_stages = [ref.at[part_of(0, 2 * r.total_q.shape[0]), part_of(0, cols)] for ref in stages]
    far_y = [2 * z + 1 - y for z in range(4)]
    own_y = [2 * z + y for z in range(4)]

    spread = Spread(links, r.cot, True, tok)
    r.cot[spread.own(), :] = r.cotangent[...]
    spread.start()
    loads = [
        links.local(r.rows_d, r.rows),
        links.local(r.f2_gate_w, r.gate_v),
        links.local(r.f2_up_w, r.up_v),
        links.local(r.f2_down_w, r.down_v),
        links.local(r.x_three, r.values),
    ]
    wait(loads)
    hidden_rows(r, r.rows, everything)
    spread.by_chip(lambda rows: hidden_back(r, rows))
    collect_d = Collect(links, part, r.core_b, r.far_b, True, tok)
    collect_d.run(turned_rows([(r.gate, r.gate_v), (r.up, r.up_v)], part))
    pairs = [(r.rows, r.gate), (r.rows, r.up), (r.cot, r.hidden)]
    weight_blocks(links, far_y, pairs, stages, r.blocks_2)
    stream_2 = Scatter(links, r.blocks_2, r.land_y_2, r.land_z_2, *stages, r.total_2, r.sum_2, 2)
    stream_2.over_y(2)
    dx, gain_grad = norm_back(r.values[...], r.gain_d[...], collect_d.result())
    r.gains[pl.ds(3, 1), :] = gain_grad
    grad[...] = r.cotangent[...].astype(F32) + dx

    spread_a = Spread(links, r.cot_a, False, tok)
    r.cot_a[spread_a.own(), :] = grad[...].astype(BF)
    spread_a.start()
    weight_blocks(links, own_y, pairs, stages, r.blocks_2)
    in_v = r.gate_v.at[:, pl.ds(0, cols)]
    heads = r.q_heads.shape[1]
    q_v, k_v, v_v = (r.gate.at[:, part_of(k, heads)] for k in range(3))
    dout_v = r.dout_v
    dq_v, dk_v, dv_v = (r.up.at[:, part_of(k, heads)] for k in range(3))
    loads = [
        links.local(r.attn_out_w, r.out_w),
        links.local(r.query_w, in_v),
        links.local(r.attended, r.left),
        links.local(r.q_heads, q_v),
        links.local(r.k_heads, k_v),
        links.local(r.v_heads, v_v),
    ]
    spread_a.forward()
    for k in range(4):
        plain_rows(r.hidden, r.down_v, r.rows)(part_of(k, 2 * tok))
    spread.finish()
    collect_d.finish()
    wait(loads)
    spread_a.wait()

    def back_step(at):
        r.dcols[:, at] = dot_right_t(r.cot_a[...], r.out_w[at, :]).astype(BF)

    columns_loop(cols, 512, back_step)
    dout_moves = to_heads(links, r.dcols, dout_v, tok)
    landed(dout_moves)
    attend_back(
        q_v, k_v, v_v, dout_v, r.docs_col, r.docs_row, dq_v, dk_v, dv_v, r.dk_acc, r.dv_acc
    )
    dq_moves = from_heads(links, dq_v, r.dq_cols, tok)
    dk_moves = from_heads(links, dk_v, r.k_cols, tok)
    dv_moves = from_heads(links, dv_v, r.v_cols, tok)
    stream_2.over_y(3, 1, 0)
    rows_c = part.at[pl.ds(4 * tok, 4 * tok), :]
    load = links.local(r.rows_c, rows_c)
    collect_m = Collect(links, r.rows, r.core_m, r.far_m, True, tok)
    collect_m.run(lambda rows: None)
    stream_2.over_z(2)
    load.wait()
    landed(dq_moves)
    collect_c = Collect(links, part, r.core_c, r.far_c, False, tok)
    collect_c.run(turned_rows([(r.dq_cols, in_v)], part))
    weight_blocks(links, range(8), [(rows_c, r.dq_cols), (r.cot_a, r.left)], small_stages, r.blocks_q)
    stream_q = Scatter(links, r.blocks_q, r.land_y_q, r.land_z_q, *small_stages, r.total_q, r.sum_q, 1)
    stream_q.over_y(3, 1, 2, 0)
    r.values[...] = r.values[...] + collect_m.result()
    links.local(r.values, r.mixed).wait()
    links.local(r.x_two, r.values).wait()
    dx, gain_grad = norm_back(r.values[...], r.gain_c[...], collect_c.result())
    r.gains[pl.ds(2, 1), :] = gain_grad
    grad[...] = grad[...] + dx

    spread_b = Spread(links, r.cot, True, tok)
    r.cot[spread_b.own(), :] = grad[...].astype(BF)
    spread_b.start()
    landed(dk_moves)
    landed(dv_moves)
    links.finish(dout_moves[0] + dq_moves[0] + dk_moves[0] + dv_moves[0])
    collect_m.finish()
    loads = [
        links.local(r.f1_down_w, r.down_v),
        links.local(r.gate_1, r.gate),
        links.local(r.up_1, r.up),
        links.local(r.f1_gate_w, r.gate_v),
        links.local(r.f1_up_w, r.up_v),
        links.local(r.hidden_1, r.hidden),
        links.local(r.rows_b, r.rows),
        links.local(r.x_one, r.values),
    ]
    home = [
        from_columns(links, r.k_cols, r.key_grad, tok, cols),
        from_columns(links, r.v_cols, r.value_grad, tok, cols),
    ]
    stream_2.over_z(3)
    wait(loads)
    spread_b.by_chip(lambda rows: hidden_back(r, rows))
    collect_c.finish()
    spread_a.finish()
    collect_b = Collect(links, part, r.core_b, r.far_b, True, tok)
    collect_b.run(turned_rows([(r.gate, r.gate_v), (r.up, r.up_v)], part))
    weight_blocks(links, far_y, pairs, stages, r.blocks_1)
    stream_1 = Scatter(links, r.blocks_1, r.land_y_1, r.land_z_1, *stages, r.total_2, r.sum_1, 2)
    stream_1.over_y(2, 3)
    weight_blocks(links, own_y, pairs, stages, r.blocks_1)
    stream_2.over_z(1)
    dx, gain_grad = norm_back(r.values[...], r.gain_b[...], collect_b.result())
    r.gains[pl.ds(1, 1), :] = gain_grad
    grad[...] = grad[...] + dx

    spread_g = Spread(links, r.cot_a, False, tok)
    r.cot_a[spread_g.own(), :] = grad[...].astype(BF)
    spread_g.start()
    spread_b.finish()
    collect_b.finish()
    rows_a = part.at[pl.ds(4 * tok, 4 * tok), :]
    loads = [
        links.local(r.gmu_out_w, r.out_w),
        links.local(r.gmu_gate_w, in_v),
        links.local(r.pre, r.dcols),
        links.local(r.mem, r.dq_cols),
        links.local(r.act, r.left),
        links.local(r.rows_a, rows_a),
    ]
    spread_g.forward()
    stream_q.over_z(3, 1)
    wait(loads)
    spread_g.wait()

    def gmu_back(at):
        dact = dot_right_t(r.cot_a[...], r.out_w[at, :])
        pre, mem = r.dcols[:, at].astype(F32), r.dq_cols[:, at].astype(F32)
        sigmoid = jax.nn.sigmoid(pre)
        r.dcols[:, at] = (dact * (pre * sigmoid)).astype(BF)
        r.dq_cols[:, at] = (dact * mem * (sigmoid * (1.0 + pre * (1.0 - sigmoid)))).astype(BF)

    columns_loop(cols, 256, gmu_back)
    collect_g = Collect(links, part, r.core_c, r.far_c, False, tok)
    collect_g.run(turned_rows([(r.dq_cols, in_v)], part))
    home.append(from_columns(links, r.dcols, r.mem_grad, tok, cols))
    weight_blocks(links, range(8), [(rows_a, r.dq_cols), (r.cot_a, r.left)], small_stages, r.blocks_g)
    stream_g = Scatter(links, r.blocks_g, r.land_y_g, r.land_z_g, *small_stages, r.total_q, r.sum_g, 1)
    stream_g.over_y(3, 1, 2, 0)
    stream_1.over_y(1, 0)
    stream_q.over_z(2)
    stream_1.over_z(2)
    dx, gain_grad = norm_back(r.x[...].astype(F32), r.gain_a[...], collect_g.result())
    grad[...] = grad[...] + dx
    outs.append(links.local(grad, r.input_grad))

    r.gains[pl.ds(0, 1), :] = gain_grad
    r.row_sums[row] = r.gains[...]
    for move in [links.copy(r.gains, r.row_sums.at[row], mask, 0) for mask in (1, 2, 3)]:
        move.wait_recv()
    r.seq_sums[seq] = r.row_sums[0] + r.row_sums[1] + r.row_sums[2] + r.row_sums[3]
    gain_moves = [links.copy(r.seq_sums.at[seq], r.seq_sums.at[seq], 0, mask) for mask in range(1, 8)]
    for moves in home:
        landed(moves)

    stream_1.over_z(3)
    stream_2.finish()
    stream_g.over_z(3, 1, 2)
    stream_1.over_z(1)
    stream_q.finish()
    for move in gain_moves:
        move.wait_recv()
    total = r.seq_sums[0]
    for k in range(1, 8):
        total = total + r.seq_sums[k]
    r.gain_total[...] = total
    outs.append(links.local(r.gain_total, r.gain_grads))
    stream_g.finish()
    stream_1.finish()
    wait(outs)
    links.finish()


def backward_pass(large, small):
    tok, width = small["x"].shape
    tokens, cols = large["mem"].shape
    wide, half = large["gate_1"].shape
    depth = width // 8
    ffn, unit = (3 * depth, half), (2 * depth, cols)

    def times(count, shape):
        return (count * shape[0], shape[1])

    outs = typed(
        F32,
        mixed=(tok, width),
        input_grad=(tok, width),
        gain_grads=(4, width),
        sum_2=(3 * depth, 2 * half),
        sum_1=(3 * depth, 2 * half),
        sum_q=unit,
        sum_g=unit,
    ) | typed(
        BF,
        key_grad=(tok, width),
        value_grad=(tok, width),
        mem_grad=(tok, width),
        blocks_2=times(8, ffn),
        blocks_1=times(8, ffn),
        blocks_q=times(8, unit),
        blocks_g=times(8, unit),
        land_y_2=times(4, ffn),
        land_y_1=times(4, ffn),
        land_y_q=times(4, unit),
        land_y_g=times(4, unit),
        land_z_2=times(3, ffn),
        land_z_1=times(3, ffn),
        land_z_q=times(3, unit),
        land_z_g=times(3, unit),
    )
    scratch = typed(
        BF,
        rows=(wide, width),
        cot=(wide, width),
        cot_a=(tokens, width),
        gate_v=(width, half),
        up_v=(width, half),
        down_v=(half, width),
        out_w=(cols, width),
        gate=(wide, half),
        up=(wide, half),
        hidden=(wide, half),
        part=(wide, width),
        left=(tokens, cols),
        dcols=(tokens, cols),
        dq_cols=(tokens, cols),
        k_cols=(tokens, cols),
        v_cols=(tokens, cols),
        dout_v=(small["docs_col"].shape[0], cols // 2),
        core_b=(4 * tok, width),
        far_b=(3 * tok, width),
        core_m=(4 * tok, width),
        far_m=(3 * tok, width),
        core_c=(2 * tok, width),
        far_c=(tok, width),
        stage_0=ffn,
        stage_1=ffn,
    ) | typed(
        F32,
        values=(tok, width),
        grad=(tok, width),
        dk_acc=(small["docs_col"].shape[0], HEAD_DIM),
        dv_acc=(small["docs_col"].shape[0], HEAD_DIM),
        total_2=(depth, half),
        total_q=(depth, cols),
        gains=(4, width),
        gain_total=(4, width),
        row_sums=(4, 4, width),
        seq_sums=(8, 4, width),
    )
    return run_kernel(backward_kernel, 1, 384, large, small, outs, scratch)


def body_general(
    block_input,
    memory,
    key_cache,
    value_cache,
    doc_lengths,
    gmu_gate,
    gmu_out,
    ffn1_gate,
    ffn1_up,
    ffn1_down,
    query_weight,
    attn_out,
    ffn2_gate,
    ffn2_up,
    ffn2_down,
    gain_a,
    gain_b,
    gain_c,
    gain_d,
    cotangent,
):
    seq_count = lax.axis_size("seq")
    row_count = lax.axis_size("row")
    seq_index = lax.axis_index("seq")
    tok_len = block_input.shape[1]
    width = block_input.shape[2]
    head_count = query_weight.shape[1] // HEAD_DIM
    depth = ffn1_gate.shape[0]
    half = ffn1_gate.shape[1] // 2
    z_count = seq_count // 2
    z_index, y_index = seq_index // 2, seq_index % 2
    parity = z_index % 2

    def spread(normed):
        return lax.all_gather(normed[None], "row", axis=0, tiled=True).reshape(
            row_count * tok_len, width
        )

    def collect(partial_value):
        return lax.psum_scatter(
            partial_value.reshape(row_count, tok_len, width).astype(BF),
            "row",
            scatter_dimension=0,
            tiled=True,
        ).astype(F32)[0]

    def spread_wide(normed):
        both = jnp.stack([normed, swapped(normed, "seq", 2)])
        return lax.all_gather(both[None], "row", axis=0, tiled=True).reshape(
            2 * row_count * tok_len, width
        )

    def collect_wide(partial_value):
        parts = partial_value.reshape(row_count, 2, tok_len, width).astype(BF)
        summed = lax.psum_scatter(parts, "row", scatter_dimension=0, tiled=True)[0]
        other = swapped(summed[1], "seq", 2)
        return summed[0].astype(F32) + other.astype(F32)

    def gather_ffn(gate, up, down):
        shard = jnp.stack([gate, up, down.T])
        whole = jnp.zeros((z_count, 2, 3, depth, half), BF)
        for step in range(z_count):
            want = (parity + step) % 2
            piece = lax.dynamic_slice_in_dim(shard, want * half, half, axis=2)
            if step:
                piece = swapped(piece, "seq", 2 * step)
            over = swapped(piece, "seq", 1)
            source = z_index ^ step
            whole = lax.dynamic_update_slice(whole, piece[None, None], (source, y_index, 0, 0, 0))
            whole = lax.dynamic_update_slice(whole, over[None, None], (source, 1 - y_index, 0, 0, 0))
        whole = whole.transpose(2, 0, 1, 3, 4).reshape(3, seq_count * depth, half)
        return whole[0], whole[1], whole[2]

    def scatter_ffn(gate_grad, up_grad, down_grad_t):
        whole = jnp.stack([gate_grad.astype(BF), up_grad.astype(BF), down_grad_t.astype(BF)])
        whole = whole.reshape(3, z_count, 2, depth, half)
        sums = [None, None]
        for step in range(z_count):
            target = z_index ^ step
            there = lax.dynamic_slice(
                whole, (0, target, 1 - y_index, 0, 0), (3, 1, 1, depth, half)
            )[:, 0, 0]
            here = lax.dynamic_slice(whole, (0, target, y_index, 0, 0), (3, 1, 1, depth, half))[:, 0, 0]
            total = here.astype(F32) + swapped(there, "seq", 1).astype(F32)
            if step:
                total = swapped(total.astype(BF), "seq", 2 * step).astype(F32)
            kind = step % 2
            sums[kind] = total if sums[kind] is None else sums[kind] + total
        pair = jnp.stack(sums)
        lower = lax.dynamic_index_in_dim(pair, parity, 0, keepdims=False)
        upper = lax.dynamic_index_in_dim(pair, 1 - parity, 0, keepdims=False)
        full = jnp.concatenate([lower, upper], axis=2)
        return full[0], full[1], full[2].T

    gmu_gate_full = lax.all_gather(gmu_gate, "seq", axis=0, tiled=True)
    gmu_out_full = lax.all_gather(gmu_out, "seq", axis=1, tiled=True)
    gate_one_w, up_one_w, down_one_t = gather_ffn(ffn1_gate, ffn1_up, ffn1_down)
    query_full = lax.all_gather(query_weight, "seq", axis=0, tiled=True)
    aout_full = lax.all_gather(attn_out, "seq", axis=1, tiled=True)
    gate_two_w, up_two_w, down_two_t = gather_ffn(ffn2_gate, ffn2_up, ffn2_down)

    def ffn_forward(rows_in, gate_weight, up_weight, down_weight_t):
        gate_val = dot_plain(rows_in, gate_weight)
        up_val = dot_plain(rows_in, up_weight)
        hidden = (jax.nn.silu(gate_val) * up_val).astype(BF)
        return (dot_right_t(hidden, down_weight_t), gate_val, up_val, hidden)

    def ffn_backward(cot_rows, rows_in, gate_val, up_val, hidden, gate_weight, up_weight, down_weight_t):
        dhid = dot_plain(cot_rows, down_weight_t)
        dgate = (dhid * up_val * silu_slope(gate_val)).astype(BF)
        dup = (dhid * jax.nn.silu(gate_val)).astype(BF)
        drows = dot_right_t(dgate, gate_weight) + dot_right_t(dup, up_weight)
        down_grad_t = dot_left_t(cot_rows, hidden)
        gate_grad = dot_left_t(rows_in, dgate)
        up_grad = dot_left_t(rows_in, dup)
        return (drows, gate_grad, up_grad, down_grad_t)

    mem_cols = lax.all_to_all(memory, "row", split_axis=2, concat_axis=0, tiled=True)
    mem_cols = mem_cols.reshape(row_count * tok_len, -1).astype(F32)
    kv_here = lax.all_to_all(
        jnp.concatenate([key_cache, value_cache], axis=0)[:, None], "row", split_axis=3, concat_axis=1, tiled=True
    )

    x_zero = block_input[0].astype(F32)
    normed_a, inv_a = rms_forward(x_zero, gain_a)
    rows_a = spread(normed_a.astype(BF))
    gmu_pre = dot_plain(rows_a, gmu_gate_full)
    gmu_act = (mem_cols * jax.nn.silu(gmu_pre)).astype(BF)
    x_one = x_zero + collect(dot_plain(gmu_act, gmu_out_full))
    normed_b, inv_b = rms_forward(x_one, gain_b)
    rows_b = spread_wide(normed_b.astype(BF))
    part_one, gate_one, up_one, hidden_one = ffn_forward(rows_b, gate_one_w, up_one_w, down_one_t)
    x_two = x_one + collect_wide(part_one)
    normed_c, inv_c = rms_forward(x_two, gain_c)
    rows_c = spread(normed_c.astype(BF))
    queries = dot_plain(rows_c, query_full).astype(BF)
    head_shape = (row_count, tok_len, head_count, HEAD_DIM)
    attended, ring_grad = ring_attention(
        queries.reshape(head_shape), kv_here.reshape((2,) + head_shape), doc_lengths, tok_len, head_count
    )

    def attention_grad(dout):
        return ring_grad(dout.reshape(head_shape))

    attended = attended.reshape(row_count * tok_len, head_count * HEAD_DIM)
    x_three = x_two + collect(dot_plain(attended, aout_full))
    normed_d, inv_d = rms_forward(x_three, gain_d)
    rows_d = spread_wide(normed_d.astype(BF))
    part_two, gate_two, up_two, hidden_two = ffn_forward(rows_d, gate_two_w, up_two_w, down_two_t)
    mixed = x_three + collect_wide(part_two)

    grad_y = cotangent[0].astype(F32)
    drows_d, gate_two_grad, up_two_grad, down_two_grad = ffn_backward(
        spread_wide(cotangent[0]), rows_d, gate_two, up_two, hidden_two, gate_two_w, up_two_w, down_two_t
    )
    dx_d, gain_d_grad = rms_backward(x_three, inv_d, gain_d, collect_wide(drows_d))
    grad_three = grad_y + dx_d
    cot_three = spread(grad_three.astype(BF))
    dattended = dot_right_t(cot_three, aout_full)
    aout_grad = dot_left_t(attended, cot_three)
    dqueries, kv_grad = attention_grad(dattended.astype(BF))
    dqueries = dqueries.reshape(row_count * tok_len, head_count * HEAD_DIM)
    query_grad = dot_left_t(rows_c, dqueries)
    dx_c, gain_c_grad = rms_backward(x_two, inv_c, gain_c, collect(dot_right_t(dqueries, query_full)))
    grad_two = grad_three + dx_c
    drows_b, gate_one_grad, up_one_grad, down_one_grad = ffn_backward(
        spread_wide(grad_two.astype(BF)), rows_b, gate_one, up_one, hidden_one, gate_one_w, up_one_w, down_one_t
    )
    dx_b, gain_b_grad = rms_backward(x_one, inv_b, gain_b, collect_wide(drows_b))
    grad_one = grad_two + dx_b
    cot_one = spread(grad_one.astype(BF))
    dact = dot_right_t(cot_one, gmu_out_full)
    gout_grad = dot_left_t(gmu_act, cot_one)
    mem_grad_cols = dact * jax.nn.silu(gmu_pre)
    dpre = (dact * mem_cols * silu_slope(gmu_pre)).astype(BF)
    gate_a_grad = dot_left_t(rows_a, dpre)
    dx_a, gain_a_grad = rms_backward(x_zero, inv_a, gain_a, collect(dot_right_t(dpre, gmu_gate_full)))
    input_grad = grad_one + dx_a

    mem_grad = lax.all_to_all(
        mem_grad_cols.reshape(row_count, tok_len, -1).astype(BF), "row", split_axis=0, concat_axis=2, tiled=True
    ).astype(F32)
    kv_home = lax.all_to_all(
        kv_grad.reshape(2, row_count, tok_len, -1), "row", split_axis=1, concat_axis=3, tiled=True
    ).astype(F32)

    def scatter(grad, dim):
        return lax.psum_scatter(grad.astype(BF), "seq", scatter_dimension=dim, tiled=True).astype(F32)

    gate_two_out, up_two_out, down_two_out = scatter_ffn(gate_two_grad, up_two_grad, down_two_grad)
    aout_out = scatter(aout_grad, 1)
    query_out = scatter(query_grad, 0)
    gate_one_out, up_one_out, down_one_out = scatter_ffn(gate_one_grad, up_one_grad, down_one_grad)
    gout_out = scatter(gout_grad, 1)
    gate_a_out = scatter(gate_a_grad, 0)
    gain_grads = lax.psum((gain_a_grad, gain_b_grad, gain_c_grad, gain_d_grad), ("seq", "row"))
    return (
        mixed[None],
        input_grad[None],
        mem_grad,
        kv_home[0],
        kv_home[1],
        gate_a_out,
        gout_out,
        gate_one_out,
        up_one_out,
        down_one_out,
        query_out,
        aout_out,
        gate_two_out,
        up_two_out,
        down_two_out,
        gain_grads[0],
        gain_grads[1],
        gain_grads[2],
        gain_grads[3],
    )


def body_fast(
    block_input,
    memory,
    key_cache,
    value_cache,
    doc_lengths,
    gmu_gate,
    gmu_out,
    ffn1_gate,
    ffn1_up,
    ffn1_down,
    query_weight,
    attn_out,
    ffn2_gate,
    ffn2_up,
    ffn2_down,
    gain_a,
    gain_b,
    gain_c,
    gain_d,
    cotangent,
):
    seq_count = lax.axis_size("seq")
    row_count = lax.axis_size("row")
    seq_index = lax.axis_index("seq")
    positions = jnp.arange(seq_count * block_input.shape[1], dtype=jnp.int32)
    docs = lax.dynamic_index_in_dim(
        doc_numbers(doc_lengths, positions), seq_index // (seq_count // row_count), 0, keepdims=False
    )
    shared = dict(x=block_input[0], docs_col=docs[:, None], docs_row=docs[None, :])
    shared |= dict(gain_a=gain_a[None], gain_b=gain_b[None], gain_c=gain_c[None], gain_d=gain_d[None])
    kept = forward_pass(
        dict(
            memory=memory[0],
            keys=key_cache[0],
            values=value_cache[0],
            gmu_gate=gmu_gate,
            gmu_out=gmu_out,
            f1_gate=ffn1_gate,
            f1_up=ffn1_up,
            f1_down=ffn1_down,
            query=query_weight,
            attn_out=attn_out,
            f2_gate=ffn2_gate,
            f2_up=ffn2_up,
            f2_down=ffn2_down,
        ),
        shared,
    )
    back = backward_pass(
        dict(
            rows_a=kept.rows_a_out,
            rows_b=kept.rows_b_out,
            rows_c=kept.rows_c_out,
            rows_d=kept.rows_d_out,
            q_heads=kept.q_heads_out,
            k_heads=kept.k_heads_out,
            v_heads=kept.v_heads_out,
            attended=kept.attended_out,
            mem=kept.mem_out,
            pre=kept.pre_out,
            act=kept.act_out,
            gate_1=kept.gate_out,
            up_1=kept.up_out,
            hidden_1=kept.hidden_out,
            x_one=kept.x_one_out,
            x_two=kept.x_two_out,
            x_three=kept.x_three_out,
            gmu_gate_w=kept.gmu_gate_w,
            gmu_out_w=kept.gmu_out_w,
            query_w=kept.query_w,
            attn_out_w=kept.attn_out_w,
            f1_gate_w=kept.f1_gate_w,
            f1_up_w=kept.f1_up_w,
            f1_down_w=kept.f1_down_w,
            f2_gate_w=kept.f2_gate_w,
            f2_up_w=kept.f2_up_w,
            f2_down_w=kept.f2_down_w,
        ),
        shared | dict(cotangent=cotangent[0]),
    )
    depth = gmu_gate.shape[0]

    def shards(sums):
        parts = [sums[k * depth : (k + 1) * depth] for k in range(sums.shape[0] // depth)]
        return parts[:-1] + [parts[-1].T]

    gate_a_out, gout_out = shards(back.sum_g)
    query_out, aout_out = shards(back.sum_q)
    gate_one_out, up_one_out, down_one_out = shards(back.sum_1)
    gate_two_out, up_two_out, down_two_out = shards(back.sum_2)
    return (
        back.mixed[None],
        back.input_grad[None],
        back.mem_grad.astype(F32)[None],
        back.key_grad.astype(F32)[None],
        back.value_grad.astype(F32)[None],
        gate_a_out,
        gout_out,
        gate_one_out,
        up_one_out,
        down_one_out,
        query_out,
        aout_out,
        gate_two_out,
        up_two_out,
        down_two_out,
        *(back.gain_grads[k] for k in range(4)),
    )


def solution(mesh):
    tokens = P("row", "seq", None)
    inner, outer = P("seq", "row"), P("row", "seq")
    in_specs = (
        (tokens,) * 4
        + (P(), inner, outer, inner, inner, outer, inner, outer, inner, inner, outer)
        + (P(),) * 4
        + (tokens,)
    )
    out_specs = (
        (tokens,) * 5
        + (inner, outer, inner, inner, outer, inner, outer, inner, inner, outer)
        + (P(),) * 4
    )
    seq_count, row_count = mesh.shape["seq"], mesh.shape["row"]
    body = body_fast if seq_count == 8 and row_count == 4 else body_general
    return jax.shard_map(body, mesh=mesh, in_specs=in_specs, out_specs=out_specs, check_vma=False)
```

```python
from types import SimpleNamespace

import jax
import jax.numpy as jnp
from jax import lax
from jax.experimental import pallas as pl
from jax.experimental.pallas import tpu as pltpu
from jax.sharding import PartitionSpec as P

HEAD_DIM = 128


EPSILON = 1e-05
MASKED = -1e30
BF = jnp.bfloat16
F32 = jnp.float32


def passed_along(value, axis, steps):
    count = lax.axis_size(axis)
    first, last = (max(0, -steps), min(count, count - steps))
    return lax.ppermute(value, axis, [(source, source + steps) for source in range(first, last)])


def shifted(value, axis, steps):
    count = lax.axis_size(axis)
    pairs = [(source, (source + steps) % count) for source in range(count)]
    return lax.ppermute(value, axis, pairs)


def swapped(value, axis, mask):
    count = lax.axis_size(axis)
    return lax.ppermute(value, axis, [(source, source ^ mask) for source in range(count)])


def silu_slope(values):
    sigmoid = jax.nn.sigmoid(values)
    return sigmoid * (1.0 + values * (1.0 - sigmoid))


def rms_forward(values, gain_vec):
    inverse = lax.rsqrt(jnp.mean(values * values, axis=-1, keepdims=True) + EPSILON)
    return (values * inverse * gain_vec, inverse)


def rms_backward(values, inverse, gain_vec, grad_normed):
    scaled = grad_normed * gain_vec
    gain_grad = jnp.sum(grad_normed * values * inverse, axis=0)
    inner_sum = jnp.mean(scaled * values, axis=-1, keepdims=True)
    return (inverse * scaled - values * inverse * inverse * inverse * inner_sum, gain_grad)


def doc_numbers(doc_lengths, positions):
    doc_ends = jnp.cumsum(doc_lengths, axis=1, dtype=jnp.int32)
    return jnp.sum((positions[None, :, None] >= doc_ends[:, None, :]).astype(jnp.int32), axis=-1)


def dot_plain(left, right):
    return jnp.dot(left, right, preferred_element_type=F32)


def dot_left_t(left, right):
    return lax.dot_general(left, right, (((0,), (0,)), ((), ())), preferred_element_type=F32)


def dot_right_t(left, right):
    return lax.dot_general(left, right, (((1,), (1,)), ((), ())), preferred_element_type=F32)


def ring_attention(queries, kv_here, doc_lengths, tok_len, head_count):
    seq_count = lax.axis_size("seq")
    seq_index = lax.axis_index("seq")
    row_count = queries.shape[0]
    score_scale = HEAD_DIM ** (-0.5)
    local_pos = jnp.arange(tok_len, dtype=jnp.int32)

    def allowed_pairs(source):
        q_positions = seq_index * tok_len + local_pos
        key_pos = source * tok_len + local_pos
        q_docs = doc_numbers(doc_lengths, q_positions)
        key_docs = doc_numbers(doc_lengths, key_pos)
        causal = key_pos[None, :] <= q_positions[:, None]
        same_doc = q_docs[:, :, None] == key_docs[:, None, :]
        return (causal[None] & same_doc)[:, :, None, :]

    def absorb(softmax_state, kv_block, source):
        run_max, totals, accum = softmax_state
        scores = jnp.einsum("rihd,rjhd->rihj", queries, kv_block[0], preferred_element_type=F32)
        allowed = allowed_pairs(source)
        scores = jnp.where(allowed, scores * score_scale, MASKED)
        new_max = jnp.maximum(run_max, jnp.max(scores, axis=-1, keepdims=True))
        weights = jnp.where(allowed, jnp.exp(scores - new_max), 0.0)
        shrink = jnp.exp(run_max - new_max)
        totals = totals * shrink + jnp.sum(weights, axis=-1, keepdims=True)
        accum = accum * shrink + jnp.einsum(
            "rihj,rjhd->rihd", weights.astype(BF), kv_block[1], preferred_element_type=F32
        )
        return (new_max, totals, accum)

    stat_shape = (row_count, tok_len, head_count, 1)
    start_state = (
        jnp.full(stat_shape, MASKED, F32),
        jnp.zeros(stat_shape, F32),
        jnp.zeros((row_count, tok_len, head_count, HEAD_DIM), F32),
    )
    first_state = absorb(start_state, kv_here, seq_index)

    def cycle_forward(section_num, carry):
        softmax_state, kv_block = carry
        kv_block = passed_along(kv_block, "seq", 1)
        source = (seq_index - section_num) % seq_count
        return (absorb(softmax_state, kv_block, source), kv_block)

    final_state, _ = lax.fori_loop(1, seq_count, cycle_forward, (first_state, kv_here))
    run_max, totals, accum = final_state
    outputs = accum / totals
    log_sums = run_max + jnp.log(totals)

    def backward(dout):
        row_delta = jnp.sum(dout.astype(F32) * outputs, axis=-1, keepdims=True)
        head_shape = (row_count, tok_len, head_count, HEAD_DIM)

        def cycle_backward(section_num, carry):
            query_acc, kv_block, grad_block = carry
            source = (seq_index - section_num) % seq_count
            scores = jnp.einsum("rihd,rjhd->rihj", queries, kv_block[0], preferred_element_type=F32)
            allowed = allowed_pairs(source)
            probs = jnp.where(allowed, jnp.exp(scores * score_scale - log_sums), 0.0)
            dprob = jnp.einsum("rihd,rjhd->rihj", dout, kv_block[1], preferred_element_type=F32)
            dscores = (probs * (dprob - row_delta)).astype(BF)
            query_acc = (
                query_acc
                + jnp.einsum("rihj,rjhd->rihd", dscores, kv_block[0], preferred_element_type=F32)
                * score_scale
            )
            key_part = (
                jnp.einsum("rihj,rihd->rjhd", dscores, queries, preferred_element_type=F32)
                * score_scale
            )
            value_part = jnp.einsum(
                "rihj,rihd->rjhd", probs.astype(BF), dout, preferred_element_type=F32
            )
            grad_block = grad_block + jnp.stack([key_part, value_part])
            kv_block = passed_along(kv_block, "seq", 1)
            grad_block = shifted(grad_block.astype(BF), "seq", 1).astype(grad_block.dtype)
            return (query_acc, kv_block, grad_block)

        query_acc, _, grad_block = lax.fori_loop(
            0,
            seq_count,
            cycle_backward,
            (jnp.zeros(head_shape, F32), kv_here, jnp.zeros((2,) + head_shape, F32)),
        )
        return query_acc.astype(BF), grad_block.astype(BF)

    return outputs.astype(BF), backward


MESH = pl.DeviceIdType.MESH
VMEM_LIMIT = 62 * 2**20


def flipped(value, mask):
    bit = 1
    while bit <= mask:
        if mask & bit:
            value = value + bit - 2 * bit * lax.rem(lax.div(value, bit), 2)
        bit *= 2
    return value


def rows_at(index, size):
    return pl.ds(pl.multiple_of(index * size, size), size)


def part_of(index, size):
    return pl.ds(index * size, size)


class Links:
    def __init__(self, send, recv):
        self.send, self.recv, self.used, self.sent = send, recv, 0, []
        self.row, self.seq = lax.axis_index("row"), lax.axis_index("seq")
        self.z, self.y = lax.div(self.seq, 2), lax.rem(self.seq, 2)
        self.parity = lax.rem(self.z, 2)

    def device(self, row_mask, seq_mask):
        return {"row": flipped(self.row, row_mask), "seq": flipped(self.seq, seq_mask)}

    def greet(self, masks):
        barrier = pltpu.get_barrier_semaphore()
        for mask in masks:
            pl.semaphore_signal(barrier, inc=1, device_id=self.device(*mask), device_id_type=MESH)
        pl.semaphore_wait(barrier, len(masks))

    def slot(self):
        self.used += 1
        assert self.used <= self.send.shape[0]
        return self.used - 1

    def copy(self, src, dst, row_mask, seq_mask):
        slot = self.slot()
        move = pltpu.make_async_remote_copy(
            src_ref=src,
            dst_ref=dst,
            send_sem=self.send.at[slot],
            recv_sem=self.recv.at[slot],
            device_id=self.device(row_mask, seq_mask),
            device_id_type=MESH,
        )
        move.start()
        self.sent.append(move)
        return move

    def local(self, src, dst):
        move = pltpu.make_async_copy(src, dst, self.send.at[self.slot()])
        move.start()
        return move

    def finish(self, moves=None):
        moves = list(self.sent if moves is None else moves)
        for move in moves:
            move.wait_send()
        done = {id(move) for move in moves}
        self.sent = [move for move in self.sent if id(move) not in done]


def wait(moves):
    for move in moves:
        move.wait()


def landed(moves):
    for move in moves[0]:
        move.wait_recv()
    moves[1].wait()


class Gather:
    def __init__(self, links, shard, whole, outer, parts):
        self.links, self.shard, self.whole, self.outer, self.parts = links, shard, whole, outer, parts
        self.z_moves, self.y_moves = {}, {}

    def piece(self, step):
        if self.parts == 1:
            return self.shard
        part = lax.rem(self.links.parity + step, 2)
        if self.outer:
            return self.shard.at[rows_at(part, self.shard.shape[0] // 2), :]
        return self.shard.at[:, rows_at(part, self.shard.shape[1] // 2)]

    def place(self, source):
        if self.outer:
            return self.whole.at[:, rows_at(source, self.shard.shape[1])]
        return self.whole.at[rows_at(source, self.shard.shape[0]), :]

    def own(self):
        self.keep = self.links.local(self.piece(0), self.place(self.links.seq))
        self.y_moves[0] = self.links.copy(self.piece(0), self.place(self.links.seq), 0, 1)

    def over_z(self, *steps):
        for step in steps:
            if step == 3 and self.parts == 1:
                self.z_moves[2].wait_recv()
                here = self.place(flipped(self.links.seq, 4))
                self.z_moves[3] = self.links.copy(here, here, 0, 2)
            else:
                self.z_moves[step] = self.links.copy(self.piece(step), self.place(self.links.seq), 0, 2 * step)

    def over_y(self, *steps):
        for step in steps:
            if not (step == 2 and 3 in self.z_moves and self.parts == 1):
                self.z_moves[step].wait_recv()
            here = self.place(flipped(self.links.seq, 2 * step))
            self.y_moves[step] = self.links.copy(here, here, 0, 1)

    def arrived(self):
        self.keep.wait()
        for step in range(4):
            self.y_moves[step].wait_recv()


def each(weights, action, *steps):
    for step in steps:
        for weight in weights:
            action(weight, step)


def chip_masks(wide):
    return [(0, 0), (2, 0)] + ([(0, 2), (2, 2)] if wide else [])


def chip_rows(links, mask, wide, tok):
    chip = lax.div(flipped(links.row, mask[0]), 2)
    if wide:
        chip = chip * 2 + lax.rem(links.parity + mask[1] // 2, 2)
    return rows_at(chip, 2 * tok)


def block_rows(links, mask, wide, tok, other=0):
    chip = lax.div(flipped(links.row, mask[0]), 2)
    if wide:
        chip = chip * 2 + lax.rem(links.parity + mask[1] // 2, 2)
    return rows_at(chip * 2 + lax.rem(links.row + other, 2), tok)


class Spread:
    def __init__(self, links, whole, wide, tok):
        self.links, self.whole, self.wide, self.tok = links, whole, wide, tok
        self.masks = chip_masks(wide)

    def place(self, mask):
        return self.whole.at[block_rows(self.links, mask, self.wide, self.tok), :]

    def own(self):
        return block_rows(self.links, (0, 0), self.wide, self.tok)

    def start(self):
        here = self.place((0, 0))
        self.far = [self.links.copy(here, here, *mask) for mask in self.masks[1:]]
        self.near = [self.links.copy(here, here, 1, 0)]

    def forward(self):
        for mask, move in zip(self.masks[1:], self.far):
            move.wait_recv()
            there = self.place(mask)
            self.near.append(self.links.copy(there, there, 1, 0))

    def wait(self):
        for move in self.near:
            move.wait_recv()

    def by_chip(self, compute):
        for k, mask in enumerate(self.masks):
            if k:
                self.far[k - 1].wait_recv()
                there = self.place(mask)
                self.near.append(self.links.copy(there, there, 1, 0))
            self.near[k].wait_recv()
            compute(chip_rows(self.links, mask, self.wide, self.tok))

    def finish(self):
        self.links.finish(self.far + self.near)


class Collect:
    def __init__(self, links, parts, from_core, from_far, wide, tok):
        self.links, self.parts, self.wide, self.tok = links, parts, wide, tok
        self.from_core, self.from_far = from_core, from_far
        self.masks = chip_masks(wide)
        self.near, self.far = {}, {}

    def block(self, mask, other=0):
        return self.parts.at[block_rows(self.links, mask, self.wide, self.tok, other), :]

    def slot(self, ref, k):
        return ref.at[part_of(k, self.tok), :]

    def forward(self, k):
        self.near[k].wait_recv()
        mine = self.block(self.masks[k])
        mine[...] = (mine[...].astype(F32) + self.slot(self.from_core, k)[...].astype(F32)).astype(BF)
        self.far[k] = self.links.copy(mine, self.slot(self.from_far, k - 1), *self.masks[k])

    def run(self, compute):
        last = len(self.masks) - 1
        for k in range(last, -1, -1):
            compute(chip_rows(self.links, self.masks[k], self.wide, self.tok))
            self.near[k] = self.links.copy(self.block(self.masks[k], 1), self.slot(self.from_core, k), 1, 0)
            if k < last:
                self.forward(k + 1)

    def result(self):
        self.near[0].wait_recv()
        total = self.block((0, 0))[...].astype(F32) + self.slot(self.from_core, 0)[...].astype(F32)
        for k in range(1, len(self.masks)):
            self.far[k].wait_recv()
            total = total + self.slot(self.from_far, k - 1)[...].astype(F32)
        return total

    def finish(self):
        self.links.finish(list(self.near.values()) + list(self.far.values()))


def normed_block(values, gain):
    inverse = lax.rsqrt(jnp.mean(values * values, axis=-1, keepdims=True) + EPSILON)
    return (values * inverse * gain).astype(BF)


def norm_back(values, gain, grad_normed):
    inverse = lax.rsqrt(jnp.mean(values * values, axis=-1, keepdims=True) + EPSILON)
    scaled = grad_normed * gain
    gain_grad = jnp.sum(grad_normed * values * inverse, axis=0, keepdims=True)
    inner_sum = jnp.mean(scaled * values, axis=-1, keepdims=True)
    return inverse * scaled - values * inverse * inverse * inverse * inner_sum, gain_grad


def silu(values):
    return values * jax.nn.sigmoid(values)


def columns_loop(columns, tile, step):
    @pl.loop(0, columns // tile)
    def _(index):
        step(rows_at(index, tile))


def to_heads(links, src, dst, tok):
    wide = dst.shape[1]

    def block(seq):
        return src.at[rows_at(lax.div(seq, 2), tok), rows_at(lax.rem(seq, 2), wide)]

    here = dst.at[rows_at(links.seq, tok), :]
    moves = [links.copy(block(flipped(links.seq, mask)), here, 0, mask) for mask in range(1, 8)]
    return moves, links.local(block(links.seq), here)


def from_heads(links, src, dst, tok):
    wide = src.shape[1]
    here = dst.at[rows_at(links.z, tok), rows_at(links.y, wide)]
    moves = [links.copy(src.at[rows_at(flipped(links.seq, mask), tok), :], here, 0, mask) for mask in range(1, 8)]
    return moves, links.local(src.at[rows_at(links.seq, tok), :], here)


def to_columns(links, src, dst, tok, cols):
    here = dst.at[rows_at(links.row, tok), :]
    moves = [links.copy(src.at[:, rows_at(flipped(links.row, mask), cols)], here, mask, 0) for mask in (1, 2, 3)]
    return moves, links.local(src.at[:, rows_at(links.row, cols)], here)


def from_columns(links, src, dst, tok, cols):
    here = dst.at[:, rows_at(links.row, cols)]
    moves = [links.copy(src.at[rows_at(flipped(links.row, mask), tok), :], here, mask, 0) for mask in (1, 2, 3)]
    return moves, links.local(src.at[rows_at(links.row, tok), :], here)


def tile_mask(docs_col, docs_row, start, tile):
    keys = start + tile
    q_pos = lax.broadcasted_iota(jnp.int32, (tile, keys), 0) + start
    k_pos = lax.broadcasted_iota(jnp.int32, (tile, keys), 1)
    return (k_pos <= q_pos) & (docs_col[pl.ds(start, tile), :] == docs_row[:, pl.ds(0, keys)])


def softmax_tile(q, k, docs_col, docs_row, start, tile):
    scores = dot_right_t(q, k) * (HEAD_DIM ** (-0.5))
    scores = jnp.where(tile_mask(docs_col, docs_row, start, tile), scores, MASKED)
    expo = jnp.exp(scores - jnp.max(scores, axis=1, keepdims=True))
    return expo * (1.0 / jnp.sum(expo, axis=1, keepdims=True))


def attend(q_ref, k_ref, v_ref, docs_col, docs_row, out_ref):
    length = q_ref.shape[0]
    tile = min(256, length)

    @pl.loop(0, q_ref.shape[1] // HEAD_DIM)
    def _(head):
        lanes = rows_at(head, HEAD_DIM)
        for start in range(0, length, tile):
            keys, here = pl.ds(0, start + tile), pl.ds(start, tile)
            probs = softmax_tile(q_ref[here, lanes], k_ref[keys, lanes], docs_col, docs_row, start, tile)
            out_ref[here, lanes] = dot_plain(probs.astype(BF), v_ref[keys, lanes]).astype(BF)


def attend_back(q_ref, k_ref, v_ref, dout_ref, docs_col, docs_row, dq_ref, dk_ref, dv_ref, dk_acc, dv_acc):
    length = q_ref.shape[0]
    tile = min(256, length)
    scale = HEAD_DIM ** (-0.5)

    @pl.loop(0, q_ref.shape[1] // HEAD_DIM)
    def _(head):
        lanes = rows_at(head, HEAD_DIM)
        for start in reversed(range(0, length, tile)):
            keys, here = pl.ds(0, start + tile), pl.ds(start, tile)
            q, k, dout = q_ref[here, lanes], k_ref[keys, lanes], dout_ref[here, lanes]
            probs = softmax_tile(q, k, docs_col, docs_row, start, tile)
            dprob = dot_right_t(dout, v_ref[keys, lanes])
            delta = jnp.sum(probs * dprob, axis=1, keepdims=True)
            dscores = (probs * (dprob - delta)).astype(BF)
            dq_ref[here, lanes] = (dot_plain(dscores, k) * scale).astype(BF)
            dk, dv = dot_left_t(dscores, q), dot_left_t(probs.astype(BF), dout)
            if start + tile == length:
                dk_acc[...] = dk
                dv_acc[...] = dv
            else:
                dk_acc[keys, :] += dk
                dv_acc[keys, :] += dv
        dk_ref[:, lanes] = (dk_acc[...] * scale).astype(BF)
        dv_ref[:, lanes] = dv_acc[...].astype(BF)


def hidden_rows(r, rows_in, rows):
    def step(at):
        gate_val = dot_plain(rows_in[rows, :], r.gate_v[:, at])
        up_val = dot_plain(rows_in[rows, :], r.up_v[:, at])
        r.gate[rows, at] = gate_val.astype(BF)
        r.up[rows, at] = up_val.astype(BF)
        r.hidden[rows, at] = (silu(gate_val) * up_val).astype(BF)

    columns_loop(r.gate.shape[1], 256, step)


def hidden_back(r, rows):
    def step(at):
        dhid = dot_right_t(r.cot[rows, :], r.down_v[at, :])
        gate_val, up_val = r.gate[rows, at].astype(F32), r.up[rows, at].astype(F32)
        sigmoid = jax.nn.sigmoid(gate_val)
        r.gate[rows, at] = (dhid * up_val * (sigmoid * (1.0 + gate_val * (1.0 - sigmoid)))).astype(BF)
        r.up[rows, at] = (dhid * (gate_val * sigmoid)).astype(BF)

    columns_loop(r.gate.shape[1], 512, step)


def plain_rows(left, right, out):
    def compute(rows):
        def step(at):
            out[rows, at] = dot_plain(left[rows, :], right[:, at]).astype(BF)

        columns_loop(right.shape[1], 1024, step)

    return compute


def turned_rows(pairs, out):
    def compute(rows):
        def step(at):
            value = dot_right_t(pairs[0][0][rows, :], pairs[0][1][at, :])
            for left, right in pairs[1:]:
                value = value + dot_right_t(left[rows, :], right[at, :])
            out[rows, at] = value.astype(BF)

        columns_loop(pairs[0][1].shape[0], 512, step)

    return compute


def run_kernel(kernel, ident, moves, large, small, outs, scratch):
    anywhere = pl.BlockSpec(memory_space=pl.ANY)
    whole = pl.BlockSpec(memory_space=pltpu.VMEM)
    names = [*large, *small, *outs, *scratch]

    def body(*refs):
        kernel(Links(*refs[-2:]), SimpleNamespace(**dict(zip(names, refs[:-2], strict=True))))

    results = pl.pallas_call(
        body,
        out_shape=[jax.ShapeDtypeStruct(*item) for item in outs.values()],
        in_specs=[anywhere] * len(large) + [whole] * len(small),
        out_specs=[anywhere] * len(outs),
        scratch_shapes=[pltpu.VMEM(*item) for item in scratch.values()] + [pltpu.SemaphoreType.DMA((moves,))] * 2,
        compiler_params=pltpu.CompilerParams(
            collective_id=ident, has_side_effects=True, vmem_limit_bytes=VMEM_LIMIT
        ),
    )(*large.values(), *small.values())
    return SimpleNamespace(**dict(zip(outs, results, strict=True)))


def typed(kind, **shapes):
    return {name: (dims, kind) for name, dims in shapes.items()}


ALL_MASKS = [(1, 0), (2, 0), (3, 0), (0, 2), (2, 2)] + [(0, mask) for mask in (1, 3, 4, 5, 6, 7)]


def forward_kernel(links, r):
    links.greet(ALL_MASKS)
    row = links.row
    tok, width = r.x.shape
    cols = r.gmu_gate.shape[1]
    part = r.part
    outs = []

    def keep(ref, out):
        outs.append(links.local(ref, out))

    gmu_in, gmu_to = Gather(links, r.gmu_gate, r.gmu_gate_w, False, 1), Gather(links, r.gmu_out, r.gmu_out_w, True, 1)
    weights_g = [gmu_in, gmu_to]
    weights_1 = [
        Gather(links, r.f1_gate, r.f1_gate_w, False, 2),
        Gather(links, r.f1_up, r.f1_up_w, False, 2),
        Gather(links, r.f1_down, r.f1_down_w, True, 2),
    ]
    weights_q = [Gather(links, r.query, r.query_w, False, 1), Gather(links, r.attn_out, r.attn_out_w, True, 1)]
    weights_2 = [
        Gather(links, r.f2_gate, r.f2_gate_w, False, 2),
        Gather(links, r.f2_up, r.f2_up_w, False, 2),
        Gather(links, r.f2_down, r.f2_down_w, True, 2),
    ]
    gate_2, up_2, down_2 = weights_2

    each(weights_g, Gather.over_z, 2, 1)
    for weight in weights_g:
        weight.own()

    spread_a = Spread(links, r.rows_a, False, tok)
    r.rows_a[spread_a.own(), :] = normed_block(r.x[...].astype(F32), r.gain_a[...])
    spread_a.start()
    k_cols = to_columns(links, r.keys, r.k_cols, tok, cols)
    v_cols = to_columns(links, r.values, r.v_cols, tok, cols)
    mem_moves = to_columns(links, r.memory, r.mem, tok, cols)
    spread_a.forward()
    landed(k_cols)
    landed(v_cols)
    k_moves = to_heads(links, r.k_cols, r.k_heads, tok)
    v_moves = to_heads(links, r.v_cols, r.v_heads, tok)
    each(weights_g, Gather.over_z, 3)
    each(weights_1, Gather.over_z, 2, 1, 3)
    each(weights_g, Gather.over_y, 2, 1, 3)
    for weight in weights_1 + weights_q + [gate_2]:
        weight.own()
    spread_a.wait()
    landed(mem_moves)
    keep(r.rows_a, r.rows_a_out)
    keep(r.mem, r.mem_out)
    gmu_in.arrived()
    load_in = links.local(r.gmu_gate_w, r.in_v)
    gmu_to.arrived()
    load_out = links.local(r.gmu_out_w, r.out_v)
    load_in.wait()

    def gmu_step(at):
        value = dot_plain(r.rows_a[...], r.in_v[:, at])
        r.pre[:, at] = value.astype(BF)
        r.act[:, at] = (r.mem[:, at].astype(F32) * silu(value)).astype(BF)

    columns_loop(cols, 256, gmu_step)
    load_out.wait()
    collect_a = Collect(links, part, r.core_a, r.far_a, False, tok)
    collect_a.run(plain_rows(r.act, r.out_v, part))
    keep(r.pre, r.pre_out)
    keep(r.act, r.act_out)
    r.x_one[...] = r.x[...].astype(F32) + collect_a.result()
    keep(r.x_one, r.x_one_out)

    spread_b = Spread(links, r.rows_b, True, tok)
    r.rows_b[spread_b.own(), :] = normed_block(r.x_one[...], r.gain_b[...])
    spread_b.start()
    each(weights_q, Gather.over_z, 2, 1)
    each(weights_1, Gather.over_y, 2, 1, 3)
    spread_b.forward()
    spread_b.wait()
    keep(r.rows_b, r.rows_b_out)
    each(weights_q, Gather.over_z, 3)
    gate_2.over_z(2, 1, 3)
    each(weights_q, Gather.over_y, 2, 1, 3)
    loads = []
    for weight, place in zip(weights_1, (r.gate_v, r.up_v, r.down_v)):
        weight.arrived()
        loads.append(links.local(weight.whole, place))
    collect_a.finish()
    wait(loads)
    hidden_rows(r, r.rows_b, pl.ds(0, 8 * tok))
    spread_a.finish()
    outs[0].wait()
    del outs[0]
    collect_b = Collect(links, part, r.core_b, r.far_b, True, tok)
    collect_b.run(plain_rows(r.hidden, r.down_v, part))
    up_2.over_z(2, 1, 3)
    gate_2.over_y(2, 1, 3)
    landed(k_moves)
    landed(v_moves)
    keep(r.k_heads, r.k_heads_out)
    keep(r.v_heads, r.v_heads_out)
    keep(r.gate, r.gate_out)
    keep(r.up, r.up_out)
    keep(r.hidden, r.hidden_out)
    r.x_two[...] = r.x_one[...] + collect_b.result()
    keep(r.x_two, r.x_two_out)

    spread_c = Spread(links, r.rows_a, False, tok)
    r.rows_a[spread_c.own(), :] = normed_block(r.x_two[...], r.gain_c[...])
    spread_c.start()
    loads = []
    for weight, place in zip(weights_q, (r.in_v, r.out_v)):
        weight.arrived()
        loads.append(links.local(weight.whole, place))
    spread_c.forward()
    wait(loads)
    spread_c.wait()
    keep(r.rows_a, r.rows_c_out)

    def query_step(at):
        r.q_cols[:, at] = dot_plain(r.rows_a[...], r.in_v[:, at]).astype(BF)

    columns_loop(cols, 512, query_step)
    q_moves = to_heads(links, r.q_cols, r.q_heads, tok)
    down_2.over_z(2, 1)
    up_2.own()
    up_2.over_y(2, 1)
    landed(q_moves)
    keep(r.q_heads, r.q_heads_out)
    attend(r.q_heads, r.k_heads, r.v_heads, r.docs_col, r.docs_row, r.out_heads)
    spread_b.finish()
    wait(outs)
    outs.clear()
    out_moves = from_heads(links, r.out_heads, r.attended, tok)
    down_2.over_z(3)
    up_2.over_y(3)
    down_2.own()
    landed(out_moves)
    keep(r.attended, r.attended_out)
    collect_b.finish()
    collect_c = Collect(links, part, r.core_c, r.far_c, False, tok)
    collect_c.run(plain_rows(r.attended, r.out_v, part))
    r.x_three[...] = r.x_two[...] + collect_c.result()
    keep(r.x_three, r.x_three_out)
    spread_d = Spread(links, r.rows_b, True, tok)
    r.rows_b[spread_d.own(), :] = normed_block(r.x_three[...], r.gain_d[...])
    spread_d.start()
    spread_d.forward()
    down_2.over_y(2, 1, 3)
    spread_d.wait()
    keep(r.rows_b, r.rows_d_out)
    for weight in weights_2:
        weight.arrived()
    wait(outs)
    links.finish()


def forward_pass(large, small):
    tok, width = small["x"].shape
    cols = large["gmu_gate"].shape[1]
    half = large["f1_gate"].shape[1] // 2
    tokens = 4 * tok
    positions = small["docs_col"].shape[0]
    heads = (positions, cols * tokens // positions)
    inner, outer = (width, half), (half, width)
    outs = typed(
        BF,
        gmu_gate_w=(width, cols),
        gmu_out_w=(cols, width),
        f1_gate_w=inner,
        f1_up_w=inner,
        f1_down_w=outer,
        query_w=(width, cols),
        attn_out_w=(cols, width),
        f2_gate_w=inner,
        f2_up_w=inner,
        f2_down_w=outer,
        rows_a_out=(tokens, width),
        mem_out=(tokens, cols),
        pre_out=(tokens, cols),
        act_out=(tokens, cols),
        rows_b_out=(2 * tokens, width),
        gate_out=(2 * tokens, half),
        up_out=(2 * tokens, half),
        hidden_out=(2 * tokens, half),
        rows_c_out=(tokens, width),
        q_heads_out=heads,
        k_heads_out=heads,
        v_heads_out=heads,
        attended_out=(tokens, cols),
        rows_d_out=(2 * tokens, width),
    ) | typed(F32, x_one_out=(tok, width), x_two_out=(tok, width), x_three_out=(tok, width))
    scratch = typed(
        BF,
        rows_a=(tokens, width),
        mem=(tokens, cols),
        k_cols=(tokens, cols),
        v_cols=(tokens, cols),
        in_v=(width, cols),
        out_v=(cols, width),
        pre=(tokens, cols),
        act=(tokens, cols),
        part=(2 * tokens, width),
        core_a=(2 * tok, width),
        far_a=(tok, width),
        core_b=(4 * tok, width),
        far_b=(3 * tok, width),
        core_c=(2 * tok, width),
        far_c=(tok, width),
        rows_b=(2 * tokens, width),
        gate_v=inner,
        up_v=inner,
        down_v=outer,
        gate=(2 * tokens, half),
        up=(2 * tokens, half),
        hidden=(2 * tokens, half),
        q_cols=(tokens, cols),
        q_heads=heads,
        k_heads=heads,
        v_heads=heads,
        out_heads=heads,
        attended=(tokens, cols),
    ) | typed(F32, x_one=(tok, width), x_two=(tok, width), x_three=(tok, width))
    return run_kernel(forward_kernel, 0, 256, large, small, outs, scratch)


def weight_blocks(links, order, pairs, stages, blocks):
    size = stages[0].shape[0]
    depth = size // len(pairs)
    moves = [None, None]
    for count, block in enumerate(order):
        stage, kind = stages[count % 2], count % 2
        if moves[kind] is not None:
            moves[kind].wait()
        at = rows_at(block, depth)
        for k, (left, right) in enumerate(pairs):
            stage[part_of(k, depth), :] = dot_left_t(left[:, at], right[...]).astype(BF)
        moves[kind] = links.local(stage, blocks.at[rows_at(block, size), :])
    for move in moves:
        if move is not None:
            move.wait()


class Scatter:
    def __init__(self, links, blocks, land_y, land_z, here, there, total, turned, parts, *outs):
        self.links, self.blocks, self.land_y, self.land_z = links, blocks, land_y, land_z
        self.here, self.there, self.total, self.turned, self.parts, self.outs = here, there, total, turned, parts, outs
        self.size = blocks.shape[0] // 8
        self.y_moves, self.z_moves = {}, {}

    def slot(self, ref, k):
        return ref.at[part_of(k, self.size), :]

    def block(self, step, y):
        return self.blocks.at[rows_at(2 * flipped(self.links.z, step) + y, self.size), :]

    def over_y(self, *steps):
        for step in steps:
            self.y_moves[step] = self.links.copy(
                self.block(step, 1 - self.links.y), self.slot(self.land_y, step), 0, 1
            )

    def over_z(self, *steps):
        for step in steps:
            first = self.links.local(self.block(step, self.links.y), self.here)
            self.y_moves[step].wait_recv()
            mine = self.slot(self.land_y, step)
            second = self.links.local(mine, self.there)
            first.wait()
            second.wait()
            total = self.here[...].astype(F32) + self.there[...].astype(F32)
            mask = 2 * step
            if self.parts == 1 and step == 2:
                self.z_moves[3].wait_recv()
                self.links.local(self.slot(self.land_z, 2), self.there).wait()
                total = total + self.there[...].astype(F32)
            elif self.parts == 1 and step == 3:
                mask = 2
            self.here[...] = total.astype(BF)
            self.links.local(self.here, mine).wait()
            self.z_moves[step] = self.links.copy(mine, self.slot(self.land_z, step - 1), 0, mask)

    def store(self, k, half):
        rows, width = self.total.shape
        if k < len(self.outs) - 1:
            self.links.local(self.total, self.outs[k].at[:, rows_at(half, width)]).wait()
        else:
            self.turned[...] = self.total[...].T
            self.links.local(self.turned, self.outs[k].at[rows_at(half, width), :]).wait()

    def spots(self):
        rows = self.total.shape[0]
        return [ref.at[part_of(n, rows), :] for ref in (self.here, self.there) for n in range(2)]

    def add(self, sources, half):
        rows, spots = self.total.shape[0], self.spots()
        for k in range(len(self.outs)):
            wait([self.links.local(source.at[part_of(k, rows), :], spot) for source, spot in zip(sources, spots)])
            total = spots[0][...].astype(F32)
            for spot in spots[1 : len(sources)]:
                total = total + spot[...].astype(F32)
            self.total[...] = total
            self.store(k, half)

    def finish_other(self):
        for step in (1, 3):
            self.z_moves[step].wait_recv()
        self.add([self.slot(self.land_z, 0), self.slot(self.land_z, 2)], 1 - self.links.parity)

    def finish(self):
        self.y_moves[0].wait_recv()
        self.z_moves[2].wait_recv()
        sources = [self.block(0, self.links.y), self.slot(self.land_y, 0), self.slot(self.land_z, 1)]
        if self.parts == 1:
            self.z_moves[1].wait_recv()
            self.add([*sources, self.slot(self.land_z, 0)], 0)
        else:
            self.add(sources, self.links.parity)


def backward_kernel(links, r):
    links.greet(ALL_MASKS)
    row, seq, y = links.row, links.seq, links.y
    tok, width = r.grad.shape
    cols = r.left.shape[1]
    half = r.gate.shape[1]
    part, grad = r.part, r.grad
    everything = pl.ds(0, 8 * tok)
    outs = []
    stages = [r.stage_0, r.stage_1]
    depth = r.total.shape[0]
    small_stages = [ref.at[part_of(0, 2 * depth), part_of(0, cols)] for ref in stages]
    totals = [r.total, r.turned]
    small_totals = [r.total.at[:, part_of(0, cols)], r.turned.at[part_of(0, cols), :]]
    far_y = [2 * z + 1 - y for z in range(4)]
    own_y = [2 * z + y for z in range(4)]

    spread = Spread(links, r.cot, True, tok)
    r.cot[spread.own(), :] = r.cotangent[...]
    spread.start()
    loads = [
        links.local(r.rows_d, r.rows),
        links.local(r.f2_gate_w, r.gate_v),
        links.local(r.f2_up_w, r.up_v),
        links.local(r.f2_down_w, r.down_v),
        links.local(r.x_three, r.values),
    ]
    wait(loads)
    hidden_rows(r, r.rows, everything)
    spread.by_chip(lambda rows: hidden_back(r, rows))
    pairs = [(r.rows, r.gate), (r.rows, r.up), (r.cot, r.hidden)]
    collect_d = Collect(links, part, r.core_b, r.far_b, True, tok)
    collect_d.run(turned_rows([(r.gate, r.gate_v), (r.up, r.up_v)], part))
    weight_blocks(links, far_y, pairs, stages, r.blocks_2)
    stream_2 = Scatter(links, r.blocks_2, r.land_y_2, r.land_z_2, *stages, *totals, 2, r.f2_gate_g, r.f2_up_g, r.f2_down_g)
    stream_2.over_y(2)
    dx, gain_grad = norm_back(r.values[...], r.gain_d[...], collect_d.result())
    r.gains[pl.ds(3, 1), :] = gain_grad
    grad[...] = r.cotangent[...].astype(F32) + dx

    spread_a = Spread(links, r.cot_a, False, tok)
    r.cot_a[spread_a.own(), :] = grad[...].astype(BF)
    spread_a.start()
    weight_blocks(links, own_y, pairs, stages, r.blocks_2)
    in_v = r.gate_v.at[:, pl.ds(0, cols)]
    heads = r.q_heads.shape[1]
    q_v, k_v, v_v = (r.gate.at[:, part_of(k, heads)] for k in range(3))
    dout_v = r.dout_v
    dq_v, dk_v, dv_v = (r.up.at[:, part_of(k, heads)] for k in range(3))
    loads = [
        links.local(r.attn_out_w, r.out_w),
        links.local(r.query_w, in_v),
        links.local(r.attended, r.left),
        links.local(r.q_heads, q_v),
        links.local(r.k_heads, k_v),
        links.local(r.v_heads, v_v),
    ]
    spread_a.forward()
    for k in range(4):
        plain_rows(r.hidden, r.down_v, r.rows)(part_of(k, 2 * tok))
    spread.finish()
    collect_d.finish()
    wait(loads)
    spread_a.wait()

    def back_step(at):
        r.dcols[:, at] = dot_right_t(r.cot_a[...], r.out_w[at, :]).astype(BF)

    columns_loop(cols, 512, back_step)
    dout_moves = to_heads(links, r.dcols, dout_v, tok)
    landed(dout_moves)
    attend_back(
        q_v, k_v, v_v, dout_v, r.docs_col, r.docs_row, dq_v, dk_v, dv_v, r.dk_acc, r.dv_acc
    )
    dq_moves = from_heads(links, dq_v, r.dq_cols, tok)
    dk_moves = from_heads(links, dk_v, r.k_cols, tok)
    dv_moves = from_heads(links, dv_v, r.v_cols, tok)
    stream_2.over_y(3, 1, 0)
    rows_c = part.at[pl.ds(4 * tok, 4 * tok), :]
    load = links.local(r.rows_c, rows_c)
    collect_m = Collect(links, r.rows, r.core_m, r.far_m, True, tok)
    collect_m.run(lambda rows: None)
    stream_2.over_z(2)
    load.wait()
    landed(dq_moves)
    collect_c = Collect(links, part, r.core_c, r.far_c, False, tok)
    collect_c.run(turned_rows([(r.dq_cols, in_v)], part))
    weight_blocks(links, range(8), [(rows_c, r.dq_cols), (r.cot_a, r.left)], small_stages, r.blocks_q)
    stream_q = Scatter(links, r.blocks_q, r.land_y_q, r.land_z_q, *small_stages, *small_totals, 1, r.query_g, r.attn_out_g)
    stream_q.over_y(3, 1, 2, 0)
    r.values[...] = r.values[...] + collect_m.result()
    links.local(r.values, r.mixed).wait()
    links.local(r.x_two, r.values).wait()
    dx, gain_grad = norm_back(r.values[...], r.gain_c[...], collect_c.result())
    r.gains[pl.ds(2, 1), :] = gain_grad
    grad[...] = grad[...] + dx

    spread_b = Spread(links, r.cot, True, tok)
    r.cot[spread_b.own(), :] = grad[...].astype(BF)
    spread_b.start()
    landed(dk_moves)
    landed(dv_moves)
    links.finish(dout_moves[0] + dq_moves[0] + dk_moves[0] + dv_moves[0])
    collect_m.finish()
    loads = [
        links.local(r.f1_down_w, r.down_v),
        links.local(r.gate_1, r.gate),
        links.local(r.up_1, r.up),
        links.local(r.f1_gate_w, r.gate_v),
        links.local(r.f1_up_w, r.up_v),
        links.local(r.hidden_1, r.hidden),
        links.local(r.rows_b, r.rows),
        links.local(r.x_one, r.values),
    ]
    home = [
        from_columns(links, r.k_cols, r.key_grad, tok, cols),
        from_columns(links, r.v_cols, r.value_grad, tok, cols),
    ]
    stream_2.over_z(3)
    wait(loads)
    spread_b.by_chip(lambda rows: hidden_back(r, rows))
    collect_c.finish()
    spread_a.finish()
    collect_b = Collect(links, part, r.core_b, r.far_b, True, tok)
    collect_b.run(turned_rows([(r.gate, r.gate_v), (r.up, r.up_v)], part))
    weight_blocks(links, far_y, pairs, stages, r.blocks_1)
    stream_1 = Scatter(links, r.blocks_1, r.land_y_1, r.land_z_1, *stages, *totals, 2, r.f1_gate_g, r.f1_up_g, r.f1_down_g)
    stream_1.over_y(2, 1, 3)
    weight_blocks(links, own_y, pairs, stages, r.blocks_1)
    stream_2.over_z(1)
    dx, gain_grad = norm_back(r.values[...], r.gain_b[...], collect_b.result())
    r.gains[pl.ds(1, 1), :] = gain_grad
    grad[...] = grad[...] + dx

    spread_g = Spread(links, r.cot_a, False, tok)
    r.cot_a[spread_g.own(), :] = grad[...].astype(BF)
    spread_g.start()
    spread_b.finish()
    collect_b.finish()
    rows_a = part.at[pl.ds(4 * tok, 4 * tok), :]
    loads = [
        links.local(r.gmu_out_w, r.out_w),
        links.local(r.gmu_gate_w, in_v),
        links.local(r.pre, r.dcols),
        links.local(r.mem, r.dq_cols),
        links.local(r.act, r.left),
        links.local(r.rows_a, rows_a),
    ]
    spread_g.forward()
    stream_q.over_z(3, 1)
    wait(loads)
    spread_g.wait()

    def gmu_back(at):
        dact = dot_right_t(r.cot_a[...], r.out_w[at, :])
        pre, mem = r.dcols[:, at].astype(F32), r.dq_cols[:, at].astype(F32)
        sigmoid = jax.nn.sigmoid(pre)
        r.dcols[:, at] = (dact * (pre * sigmoid)).astype(BF)
        r.dq_cols[:, at] = (dact * mem * (sigmoid * (1.0 + pre * (1.0 - sigmoid)))).astype(BF)

    columns_loop(cols, 256, gmu_back)
    collect_g = Collect(links, part, r.core_c, r.far_c, False, tok)
    collect_g.run(turned_rows([(r.dq_cols, in_v)], part))
    stream_1.over_z(2)
    home.append(from_columns(links, r.dcols, r.mem_grad, tok, cols))
    weight_blocks(links, range(8), [(rows_a, r.dq_cols), (r.cot_a, r.left)], small_stages, r.blocks_g)
    stream_g = Scatter(links, r.blocks_g, r.land_y_g, r.land_z_g, *small_stages, *small_totals, 1, r.gmu_gate_g, r.gmu_out_g)
    stream_g.over_y(3, 1, 2, 0)
    stream_1.over_y(0)
    stream_q.over_z(2)
    stream_1.over_z(1)
    dx, gain_grad = norm_back(r.x[...].astype(F32), r.gain_a[...], collect_g.result())
    grad[...] = grad[...] + dx
    outs.append(links.local(grad, r.input_grad))

    r.gains[pl.ds(0, 1), :] = gain_grad
    r.row_sums[row] = r.gains[...]
    for move in [links.copy(r.gains, r.row_sums.at[row], mask, 0) for mask in (1, 2, 3)]:
        move.wait_recv()
    r.seq_sums[seq] = r.row_sums[0] + r.row_sums[1] + r.row_sums[2] + r.row_sums[3]
    gain_moves = [links.copy(r.seq_sums.at[seq], r.seq_sums.at[seq], 0, mask) for mask in range(1, 8)]
    for moves in home:
        landed(moves)

    stream_1.over_z(3)
    stream_2.finish()
    stream_2.finish_other()
    stream_g.over_z(3, 1, 2)
    stream_q.finish()
    for move in gain_moves:
        move.wait_recv()
    total = r.seq_sums[0]
    for k in range(1, 8):
        total = total + r.seq_sums[k]
    r.gain_total[...] = total
    outs.append(links.local(r.gain_total, r.gain_grads))
    stream_1.finish_other()
    stream_g.finish()
    stream_1.finish()
    wait(outs)
    links.finish()


def backward_pass(large, small):
    tok, width = small["x"].shape
    tokens, cols = large["mem"].shape
    wide, half = large["gate_1"].shape
    depth = width // 8
    ffn, unit = (3 * depth, half), (2 * depth, cols)

    def times(count, shape):
        return (count * shape[0], shape[1])

    outs = typed(
        F32,
        mixed=(tok, width),
        input_grad=(tok, width),
        gain_grads=(4, width),
        f2_gate_g=(depth, 2 * half),
        f2_up_g=(depth, 2 * half),
        f2_down_g=(2 * half, depth),
        f1_gate_g=(depth, 2 * half),
        f1_up_g=(depth, 2 * half),
        f1_down_g=(2 * half, depth),
        query_g=(depth, cols),
        attn_out_g=(cols, depth),
        gmu_gate_g=(depth, cols),
        gmu_out_g=(cols, depth),
    ) | typed(
        BF,
        key_grad=(tok, width),
        value_grad=(tok, width),
        mem_grad=(tok, width),
        blocks_2=times(8, ffn),
        blocks_1=times(8, ffn),
        blocks_q=times(8, unit),
        blocks_g=times(8, unit),
        land_y_2=times(4, ffn),
        land_y_1=times(4, ffn),
        land_y_q=times(4, unit),
        land_y_g=times(4, unit),
        land_z_2=times(3, ffn),
        land_z_1=times(3, ffn),
        land_z_q=times(3, unit),
        land_z_g=times(3, unit),
    )
    scratch = typed(
        BF,
        rows=(wide, width),
        cot=(wide, width),
        cot_a=(tokens, width),
        gate_v=(width, half),
        up_v=(width, half),
        down_v=(half, width),
        out_w=(cols, width),
        gate=(wide, half),
        up=(wide, half),
        hidden=(wide, half),
        part=(wide, width),
        left=(tokens, cols),
        dcols=(tokens, cols),
        dq_cols=(tokens, cols),
        k_cols=(tokens, cols),
        v_cols=(tokens, cols),
        dout_v=(small["docs_col"].shape[0], cols // 2),
        core_b=(4 * tok, width),
        far_b=(3 * tok, width),
        core_m=(4 * tok, width),
        far_m=(3 * tok, width),
        core_c=(2 * tok, width),
        far_c=(tok, width),
        stage_0=ffn,
        stage_1=ffn,
    ) | typed(
        F32,
        values=(tok, width),
        grad=(tok, width),
        dk_acc=(small["docs_col"].shape[0], HEAD_DIM),
        dv_acc=(small["docs_col"].shape[0], HEAD_DIM),
        total=(depth, half),
        turned=(half, depth),
        gains=(4, width),
        gain_total=(4, width),
        row_sums=(4, 4, width),
        seq_sums=(8, 4, width),
    )
    return run_kernel(backward_kernel, 1, 384, large, small, outs, scratch)


def body_general(
    block_input,
    memory,
    key_cache,
    value_cache,
    doc_lengths,
    gmu_gate,
    gmu_out,
    ffn1_gate,
    ffn1_up,
    ffn1_down,
    query_weight,
    attn_out,
    ffn2_gate,
    ffn2_up,
    ffn2_down,
    gain_a,
    gain_b,
    gain_c,
    gain_d,
    cotangent,
):
    seq_count = lax.axis_size("seq")
    row_count = lax.axis_size("row")
    seq_index = lax.axis_index("seq")
    tok_len = block_input.shape[1]
    width = block_input.shape[2]
    head_count = query_weight.shape[1] // HEAD_DIM
    depth = ffn1_gate.shape[0]
    half = ffn1_gate.shape[1] // 2
    z_count = seq_count // 2
    z_index, y_index = seq_index // 2, seq_index % 2
    parity = z_index % 2

    def spread(normed):
        return lax.all_gather(normed[None], "row", axis=0, tiled=True).reshape(
            row_count * tok_len, width
        )

    def collect(partial_value):
        return lax.psum_scatter(
            partial_value.reshape(row_count, tok_len, width).astype(BF),
            "row",
            scatter_dimension=0,
            tiled=True,
        ).astype(F32)[0]

    def spread_wide(normed):
        both = jnp.stack([normed, swapped(normed, "seq", 2)])
        return lax.all_gather(both[None], "row", axis=0, tiled=True).reshape(
            2 * row_count * tok_len, width
        )

    def collect_wide(partial_value):
        parts = partial_value.reshape(row_count, 2, tok_len, width).astype(BF)
        summed = lax.psum_scatter(parts, "row", scatter_dimension=0, tiled=True)[0]
        other = swapped(summed[1], "seq", 2)
        return summed[0].astype(F32) + other.astype(F32)

    def gather_ffn(gate, up, down):
        shard = jnp.stack([gate, up, down.T])
        whole = jnp.zeros((z_count, 2, 3, depth, half), BF)
        for step in range(z_count):
            want = (parity + step) % 2
            piece = lax.dynamic_slice_in_dim(shard, want * half, half, axis=2)
            if step:
                piece = swapped(piece, "seq", 2 * step)
            over = swapped(piece, "seq", 1)
            source = z_index ^ step
            whole = lax.dynamic_update_slice(whole, piece[None, None], (source, y_index, 0, 0, 0))
            whole = lax.dynamic_update_slice(whole, over[None, None], (source, 1 - y_index, 0, 0, 0))
        whole = whole.transpose(2, 0, 1, 3, 4).reshape(3, seq_count * depth, half)
        return whole[0], whole[1], whole[2]

    def scatter_ffn(gate_grad, up_grad, down_grad_t):
        whole = jnp.stack([gate_grad.astype(BF), up_grad.astype(BF), down_grad_t.astype(BF)])
        whole = whole.reshape(3, z_count, 2, depth, half)
        sums = [None, None]
        for step in range(z_count):
            target = z_index ^ step
            there = lax.dynamic_slice(
                whole, (0, target, 1 - y_index, 0, 0), (3, 1, 1, depth, half)
            )[:, 0, 0]
            here = lax.dynamic_slice(whole, (0, target, y_index, 0, 0), (3, 1, 1, depth, half))[:, 0, 0]
            total = here.astype(F32) + swapped(there, "seq", 1).astype(F32)
            if step:
                total = swapped(total.astype(BF), "seq", 2 * step).astype(F32)
            kind = step % 2
            sums[kind] = total if sums[kind] is None else sums[kind] + total
        pair = jnp.stack(sums)
        lower = lax.dynamic_index_in_dim(pair, parity, 0, keepdims=False)
        upper = lax.dynamic_index_in_dim(pair, 1 - parity, 0, keepdims=False)
        full = jnp.concatenate([lower, upper], axis=2)
        return full[0], full[1], full[2].T

    gmu_gate_full = lax.all_gather(gmu_gate, "seq", axis=0, tiled=True)
    gmu_out_full = lax.all_gather(gmu_out, "seq", axis=1, tiled=True)
    gate_one_w, up_one_w, down_one_t = gather_ffn(ffn1_gate, ffn1_up, ffn1_down)
    query_full = lax.all_gather(query_weight, "seq", axis=0, tiled=True)
    aout_full = lax.all_gather(attn_out, "seq", axis=1, tiled=True)
    gate_two_w, up_two_w, down_two_t = gather_ffn(ffn2_gate, ffn2_up, ffn2_down)

    def ffn_forward(rows_in, gate_weight, up_weight, down_weight_t):
        gate_val = dot_plain(rows_in, gate_weight)
        up_val = dot_plain(rows_in, up_weight)
        hidden = (jax.nn.silu(gate_val) * up_val).astype(BF)
        return (dot_right_t(hidden, down_weight_t), gate_val, up_val, hidden)

    def ffn_backward(cot_rows, rows_in, gate_val, up_val, hidden, gate_weight, up_weight, down_weight_t):
        dhid = dot_plain(cot_rows, down_weight_t)
        dgate = (dhid * up_val * silu_slope(gate_val)).astype(BF)
        dup = (dhid * jax.nn.silu(gate_val)).astype(BF)
        drows = dot_right_t(dgate, gate_weight) + dot_right_t(dup, up_weight)
        down_grad_t = dot_left_t(cot_rows, hidden)
        gate_grad = dot_left_t(rows_in, dgate)
        up_grad = dot_left_t(rows_in, dup)
        return (drows, gate_grad, up_grad, down_grad_t)

    mem_cols = lax.all_to_all(memory, "row", split_axis=2, concat_axis=0, tiled=True)
    mem_cols = mem_cols.reshape(row_count * tok_len, -1).astype(F32)
    kv_here = lax.all_to_all(
        jnp.concatenate([key_cache, value_cache], axis=0)[:, None], "row", split_axis=3, concat_axis=1, tiled=True
    )

    x_zero = block_input[0].astype(F32)
    normed_a, inv_a = rms_forward(x_zero, gain_a)
    rows_a = spread(normed_a.astype(BF))
    gmu_pre = dot_plain(rows_a, gmu_gate_full)
    gmu_act = (mem_cols * jax.nn.silu(gmu_pre)).astype(BF)
    x_one = x_zero + collect(dot_plain(gmu_act, gmu_out_full))
    normed_b, inv_b = rms_forward(x_one, gain_b)
    rows_b = spread_wide(normed_b.astype(BF))
    part_one, gate_one, up_one, hidden_one = ffn_forward(rows_b, gate_one_w, up_one_w, down_one_t)
    x_two = x_one + collect_wide(part_one)
    normed_c, inv_c = rms_forward(x_two, gain_c)
    rows_c = spread(normed_c.astype(BF))
    queries = dot_plain(rows_c, query_full).astype(BF)
    head_shape = (row_count, tok_len, head_count, HEAD_DIM)
    attended, ring_grad = ring_attention(
        queries.reshape(head_shape), kv_here.reshape((2,) + head_shape), doc_lengths, tok_len, head_count
    )

    def attention_grad(dout):
        return ring_grad(dout.reshape(head_shape))

    attended = attended.reshape(row_count * tok_len, head_count * HEAD_DIM)
    x_three = x_two + collect(dot_plain(attended, aout_full))
    normed_d, inv_d = rms_forward(x_three, gain_d)
    rows_d = spread_wide(normed_d.astype(BF))
    part_two, gate_two, up_two, hidden_two = ffn_forward(rows_d, gate_two_w, up_two_w, down_two_t)
    mixed = x_three + collect_wide(part_two)

    grad_y = cotangent[0].astype(F32)
    drows_d, gate_two_grad, up_two_grad, down_two_grad = ffn_backward(
        spread_wide(cotangent[0]), rows_d, gate_two, up_two, hidden_two, gate_two_w, up_two_w, down_two_t
    )
    dx_d, gain_d_grad = rms_backward(x_three, inv_d, gain_d, collect_wide(drows_d))
    grad_three = grad_y + dx_d
    cot_three = spread(grad_three.astype(BF))
    dattended = dot_right_t(cot_three, aout_full)
    aout_grad = dot_left_t(attended, cot_three)
    dqueries, kv_grad = attention_grad(dattended.astype(BF))
    dqueries = dqueries.reshape(row_count * tok_len, head_count * HEAD_DIM)
    query_grad = dot_left_t(rows_c, dqueries)
    dx_c, gain_c_grad = rms_backward(x_two, inv_c, gain_c, collect(dot_right_t(dqueries, query_full)))
    grad_two = grad_three + dx_c
    drows_b, gate_one_grad, up_one_grad, down_one_grad = ffn_backward(
        spread_wide(grad_two.astype(BF)), rows_b, gate_one, up_one, hidden_one, gate_one_w, up_one_w, down_one_t
    )
    dx_b, gain_b_grad = rms_backward(x_one, inv_b, gain_b, collect_wide(drows_b))
    grad_one = grad_two + dx_b
    cot_one = spread(grad_one.astype(BF))
    dact = dot_right_t(cot_one, gmu_out_full)
    gout_grad = dot_left_t(gmu_act, cot_one)
    mem_grad_cols = dact * jax.nn.silu(gmu_pre)
    dpre = (dact * mem_cols * silu_slope(gmu_pre)).astype(BF)
    gate_a_grad = dot_left_t(rows_a, dpre)
    dx_a, gain_a_grad = rms_backward(x_zero, inv_a, gain_a, collect(dot_right_t(dpre, gmu_gate_full)))
    input_grad = grad_one + dx_a

    mem_grad = lax.all_to_all(
        mem_grad_cols.reshape(row_count, tok_len, -1).astype(BF), "row", split_axis=0, concat_axis=2, tiled=True
    ).astype(F32)
    kv_home = lax.all_to_all(
        kv_grad.reshape(2, row_count, tok_len, -1), "row", split_axis=1, concat_axis=3, tiled=True
    ).astype(F32)

    def scatter(grad, dim):
        return lax.psum_scatter(grad.astype(BF), "seq", scatter_dimension=dim, tiled=True).astype(F32)

    gate_two_out, up_two_out, down_two_out = scatter_ffn(gate_two_grad, up_two_grad, down_two_grad)
    aout_out = scatter(aout_grad, 1)
    query_out = scatter(query_grad, 0)
    gate_one_out, up_one_out, down_one_out = scatter_ffn(gate_one_grad, up_one_grad, down_one_grad)
    gout_out = scatter(gout_grad, 1)
    gate_a_out = scatter(gate_a_grad, 0)
    gain_grads = lax.psum((gain_a_grad, gain_b_grad, gain_c_grad, gain_d_grad), ("seq", "row"))
    return (
        mixed[None],
        input_grad[None],
        mem_grad,
        kv_home[0],
        kv_home[1],
        gate_a_out,
        gout_out,
        gate_one_out,
        up_one_out,
        down_one_out,
        query_out,
        aout_out,
        gate_two_out,
        up_two_out,
        down_two_out,
        gain_grads[0],
        gain_grads[1],
        gain_grads[2],
        gain_grads[3],
    )


def body_fast(
    block_input,
    memory,
    key_cache,
    value_cache,
    doc_lengths,
    gmu_gate,
    gmu_out,
    ffn1_gate,
    ffn1_up,
    ffn1_down,
    query_weight,
    attn_out,
    ffn2_gate,
    ffn2_up,
    ffn2_down,
    gain_a,
    gain_b,
    gain_c,
    gain_d,
    cotangent,
):
    seq_count = lax.axis_size("seq")
    row_count = lax.axis_size("row")
    seq_index = lax.axis_index("seq")
    positions = jnp.arange(seq_count * block_input.shape[1], dtype=jnp.int32)
    docs = lax.dynamic_index_in_dim(
        doc_numbers(doc_lengths, positions), seq_index // (seq_count // row_count), 0, keepdims=False
    )
    shared = dict(x=block_input[0], docs_col=docs[:, None], docs_row=docs[None, :])
    shared |= dict(gain_a=gain_a[None], gain_b=gain_b[None], gain_c=gain_c[None], gain_d=gain_d[None])
    kept = forward_pass(
        dict(
            memory=memory[0],
            keys=key_cache[0],
            values=value_cache[0],
            gmu_gate=gmu_gate,
            gmu_out=gmu_out,
            f1_gate=ffn1_gate,
            f1_up=ffn1_up,
            f1_down=ffn1_down,
            query=query_weight,
            attn_out=attn_out,
            f2_gate=ffn2_gate,
            f2_up=ffn2_up,
            f2_down=ffn2_down,
        ),
        shared,
    )
    back = backward_pass(
        dict(
            rows_a=kept.rows_a_out,
            rows_b=kept.rows_b_out,
            rows_c=kept.rows_c_out,
            rows_d=kept.rows_d_out,
            q_heads=kept.q_heads_out,
            k_heads=kept.k_heads_out,
            v_heads=kept.v_heads_out,
            attended=kept.attended_out,
            mem=kept.mem_out,
            pre=kept.pre_out,
            act=kept.act_out,
            gate_1=kept.gate_out,
            up_1=kept.up_out,
            hidden_1=kept.hidden_out,
            x_one=kept.x_one_out,
            x_two=kept.x_two_out,
            x_three=kept.x_three_out,
            gmu_gate_w=kept.gmu_gate_w,
            gmu_out_w=kept.gmu_out_w,
            query_w=kept.query_w,
            attn_out_w=kept.attn_out_w,
            f1_gate_w=kept.f1_gate_w,
            f1_up_w=kept.f1_up_w,
            f1_down_w=kept.f1_down_w,
            f2_gate_w=kept.f2_gate_w,
            f2_up_w=kept.f2_up_w,
            f2_down_w=kept.f2_down_w,
        ),
        shared | dict(cotangent=cotangent[0]),
    )
    return (
        back.mixed[None],
        back.input_grad[None],
        back.mem_grad.astype(F32)[None],
        back.key_grad.astype(F32)[None],
        back.value_grad.astype(F32)[None],
        back.gmu_gate_g,
        back.gmu_out_g,
        back.f1_gate_g,
        back.f1_up_g,
        back.f1_down_g,
        back.query_g,
        back.attn_out_g,
        back.f2_gate_g,
        back.f2_up_g,
        back.f2_down_g,
        *(back.gain_grads[k] for k in range(4)),
    )


def solution(mesh):
    tokens = P("row", "seq", None)
    inner, outer = P("seq", "row"), P("row", "seq")
    in_specs = (
        (tokens,) * 4
        + (P(), inner, outer, inner, inner, outer, inner, outer, inner, inner, outer)
        + (P(),) * 4
        + (tokens,)
    )
    out_specs = (
        (tokens,) * 5
        + (inner, outer, inner, inner, outer, inner, outer, inner, inner, outer)
        + (P(),) * 4
    )
    seq_count, row_count = mesh.shape["seq"], mesh.shape["row"]
    body = body_fast if seq_count == 8 and row_count == 4 else body_general
    return jax.shard_map(body, mesh=mesh, in_specs=in_specs, out_specs=out_specs, check_vma=False)
```

```python
from types import SimpleNamespace

import jax
import jax.numpy as jnp
from jax import lax
from jax.experimental import pallas as pl
from jax.experimental.pallas import tpu as pltpu
from jax.sharding import PartitionSpec as P

HEAD_DIM = 128


EPSILON = 1e-05
MASKED = -1e30
BF = jnp.bfloat16
F32 = jnp.float32


def passed_along(value, axis, steps):
    count = lax.axis_size(axis)
    first, last = (max(0, -steps), min(count, count - steps))
    return lax.ppermute(value, axis, [(source, source + steps) for source in range(first, last)])


def shifted(value, axis, steps):
    count = lax.axis_size(axis)
    pairs = [(source, (source + steps) % count) for source in range(count)]
    return lax.ppermute(value, axis, pairs)


def swapped(value, axis, mask):
    count = lax.axis_size(axis)
    return lax.ppermute(value, axis, [(source, source ^ mask) for source in range(count)])


def silu_slope(values):
    sigmoid = jax.nn.sigmoid(values)
    return sigmoid * (1.0 + values * (1.0 - sigmoid))


def rms_forward(values, gain_vec):
    inverse = lax.rsqrt(jnp.mean(values * values, axis=-1, keepdims=True) + EPSILON)
    return (values * inverse * gain_vec, inverse)


def rms_backward(values, inverse, gain_vec, grad_normed):
    scaled = grad_normed * gain_vec
    gain_grad = jnp.sum(grad_normed * values * inverse, axis=0)
    inner_sum = jnp.mean(scaled * values, axis=-1, keepdims=True)
    return (inverse * scaled - values * inverse * inverse * inverse * inner_sum, gain_grad)


def doc_numbers(doc_lengths, positions):
    doc_ends = jnp.cumsum(doc_lengths, axis=1, dtype=jnp.int32)
    return jnp.sum((positions[None, :, None] >= doc_ends[:, None, :]).astype(jnp.int32), axis=-1)


def dot_plain(left, right):
    return jnp.dot(left, right, preferred_element_type=F32)


def dot_left_t(left, right):
    return lax.dot_general(left, right, (((0,), (0,)), ((), ())), preferred_element_type=F32)


def dot_right_t(left, right):
    return lax.dot_general(left, right, (((1,), (1,)), ((), ())), preferred_element_type=F32)


def ring_attention(queries, kv_here, doc_lengths, tok_len, head_count):
    seq_count = lax.axis_size("seq")
    seq_index = lax.axis_index("seq")
    row_count = queries.shape[0]
    score_scale = HEAD_DIM ** (-0.5)
    local_pos = jnp.arange(tok_len, dtype=jnp.int32)

    def allowed_pairs(source):
        q_positions = seq_index * tok_len + local_pos
        key_pos = source * tok_len + local_pos
        q_docs = doc_numbers(doc_lengths, q_positions)
        key_docs = doc_numbers(doc_lengths, key_pos)
        causal = key_pos[None, :] <= q_positions[:, None]
        same_doc = q_docs[:, :, None] == key_docs[:, None, :]
        return (causal[None] & same_doc)[:, :, None, :]

    def absorb(softmax_state, kv_block, source):
        run_max, totals, accum = softmax_state
        scores = jnp.einsum("rihd,rjhd->rihj", queries, kv_block[0], preferred_element_type=F32)
        allowed = allowed_pairs(source)
        scores = jnp.where(allowed, scores * score_scale, MASKED)
        new_max = jnp.maximum(run_max, jnp.max(scores, axis=-1, keepdims=True))
        weights = jnp.where(allowed, jnp.exp(scores - new_max), 0.0)
        shrink = jnp.exp(run_max - new_max)
        totals = totals * shrink + jnp.sum(weights, axis=-1, keepdims=True)
        accum = accum * shrink + jnp.einsum(
            "rihj,rjhd->rihd", weights.astype(BF), kv_block[1], preferred_element_type=F32
        )
        return (new_max, totals, accum)

    stat_shape = (row_count, tok_len, head_count, 1)
    start_state = (
        jnp.full(stat_shape, MASKED, F32),
        jnp.zeros(stat_shape, F32),
        jnp.zeros((row_count, tok_len, head_count, HEAD_DIM), F32),
    )
    first_state = absorb(start_state, kv_here, seq_index)

    def cycle_forward(section_num, carry):
        softmax_state, kv_block = carry
        kv_block = passed_along(kv_block, "seq", 1)
        source = (seq_index - section_num) % seq_count
        return (absorb(softmax_state, kv_block, source), kv_block)

    final_state, _ = lax.fori_loop(1, seq_count, cycle_forward, (first_state, kv_here))
    run_max, totals, accum = final_state
    outputs = accum / totals
    log_sums = run_max + jnp.log(totals)

    def backward(dout):
        row_delta = jnp.sum(dout.astype(F32) * outputs, axis=-1, keepdims=True)
        head_shape = (row_count, tok_len, head_count, HEAD_DIM)

        def cycle_backward(section_num, carry):
            query_acc, kv_block, grad_block = carry
            source = (seq_index - section_num) % seq_count
            scores = jnp.einsum("rihd,rjhd->rihj", queries, kv_block[0], preferred_element_type=F32)
            allowed = allowed_pairs(source)
            probs = jnp.where(allowed, jnp.exp(scores * score_scale - log_sums), 0.0)
            dprob = jnp.einsum("rihd,rjhd->rihj", dout, kv_block[1], preferred_element_type=F32)
            dscores = (probs * (dprob - row_delta)).astype(BF)
            query_acc = (
                query_acc
                + jnp.einsum("rihj,rjhd->rihd", dscores, kv_block[0], preferred_element_type=F32)
                * score_scale
            )
            key_part = (
                jnp.einsum("rihj,rihd->rjhd", dscores, queries, preferred_element_type=F32)
                * score_scale
            )
            value_part = jnp.einsum(
                "rihj,rihd->rjhd", probs.astype(BF), dout, preferred_element_type=F32
            )
            grad_block = grad_block + jnp.stack([key_part, value_part])
            kv_block = passed_along(kv_block, "seq", 1)
            grad_block = shifted(grad_block.astype(BF), "seq", 1).astype(grad_block.dtype)
            return (query_acc, kv_block, grad_block)

        query_acc, _, grad_block = lax.fori_loop(
            0,
            seq_count,
            cycle_backward,
            (jnp.zeros(head_shape, F32), kv_here, jnp.zeros((2,) + head_shape, F32)),
        )
        return query_acc.astype(BF), grad_block.astype(BF)

    return outputs.astype(BF), backward


MESH = pl.DeviceIdType.MESH
VMEM_LIMIT = 62 * 2**20


def flipped(value, mask):
    bit = 1
    while bit <= mask:
        if mask & bit:
            value = value + bit - 2 * bit * lax.rem(lax.div(value, bit), 2)
        bit *= 2
    return value


def rows_at(index, size):
    return pl.ds(pl.multiple_of(index * size, size), size)


def part_of(index, size):
    return pl.ds(index * size, size)


class Links:
    def __init__(self, send, recv):
        self.send, self.recv, self.used, self.sent = send, recv, 0, []
        self.row, self.seq = lax.axis_index("row"), lax.axis_index("seq")
        self.z, self.y = lax.div(self.seq, 2), lax.rem(self.seq, 2)
        self.parity = lax.rem(self.z, 2)

    def device(self, row_mask, seq_mask):
        return {"row": flipped(self.row, row_mask), "seq": flipped(self.seq, seq_mask)}

    def greet(self, masks):
        barrier = pltpu.get_barrier_semaphore()
        for mask in masks:
            pl.semaphore_signal(barrier, inc=1, device_id=self.device(*mask), device_id_type=MESH)
        pl.semaphore_wait(barrier, len(masks))

    def slot(self):
        self.used += 1
        assert self.used <= self.send.shape[0]
        return self.used - 1

    def copy(self, src, dst, row_mask, seq_mask):
        slot = self.slot()
        move = pltpu.make_async_remote_copy(
            src_ref=src,
            dst_ref=dst,
            send_sem=self.send.at[slot],
            recv_sem=self.recv.at[slot],
            device_id=self.device(row_mask, seq_mask),
            device_id_type=MESH,
        )
        move.start()
        self.sent.append(move)
        return move

    def local(self, src, dst):
        move = pltpu.make_async_copy(src, dst, self.send.at[self.slot()])
        move.start()
        return move

    def finish(self, moves=None):
        moves = list(self.sent if moves is None else moves)
        for move in moves:
            move.wait_send()
        done = {id(move) for move in moves}
        self.sent = [move for move in self.sent if id(move) not in done]


def wait(moves):
    for move in moves:
        move.wait()


def landed(moves):
    for move in moves[0]:
        move.wait_recv()
    moves[1].wait()


class Gather:
    def __init__(self, links, shard, whole, outer, parts):
        self.links, self.shard, self.whole, self.outer, self.parts = links, shard, whole, outer, parts
        self.z_moves, self.y_moves = {}, {}

    def piece(self, step):
        if self.parts == 1:
            return self.shard
        part = lax.rem(self.links.parity + step, 2)
        if self.outer:
            return self.shard.at[rows_at(part, self.shard.shape[0] // 2), :]
        return self.shard.at[:, rows_at(part, self.shard.shape[1] // 2)]

    def place(self, source):
        if self.outer:
            return self.whole.at[:, rows_at(source, self.shard.shape[1])]
        return self.whole.at[rows_at(source, self.shard.shape[0]), :]

    def own(self):
        self.keep = self.links.local(self.piece(0), self.place(self.links.seq))
        self.y_moves[0] = self.links.copy(self.piece(0), self.place(self.links.seq), 0, 1)

    def over_z(self, *steps):
        for step in steps:
            if step == 3 and self.parts == 1:
                self.z_moves[2].wait_recv()
                here = self.place(flipped(self.links.seq, 4))
                self.z_moves[3] = self.links.copy(here, here, 0, 2)
            else:
                self.z_moves[step] = self.links.copy(self.piece(step), self.place(self.links.seq), 0, 2 * step)

    def over_y(self, *steps):
        for step in steps:
            if not (step == 2 and 3 in self.z_moves and self.parts == 1):
                self.z_moves[step].wait_recv()
            here = self.place(flipped(self.links.seq, 2 * step))
            self.y_moves[step] = self.links.copy(here, here, 0, 1)

    def arrived(self):
        self.keep.wait()
        for step in range(4):
            self.y_moves[step].wait_recv()


def each(weights, action, *steps):
    for step in steps:
        for weight in weights:
            action(weight, step)


def chip_masks(wide):
    return [(0, 0), (2, 0)] + ([(0, 2), (2, 2)] if wide else [])


def chip_rows(links, mask, wide, tok):
    chip = lax.div(flipped(links.row, mask[0]), 2)
    if wide:
        chip = chip * 2 + lax.rem(links.parity + mask[1] // 2, 2)
    return rows_at(chip, 2 * tok)


def block_rows(links, mask, wide, tok, other=0):
    chip = lax.div(flipped(links.row, mask[0]), 2)
    if wide:
        chip = chip * 2 + lax.rem(links.parity + mask[1] // 2, 2)
    return rows_at(chip * 2 + lax.rem(links.row + other, 2), tok)


class Spread:
    def __init__(self, links, whole, wide, tok):
        self.links, self.whole, self.wide, self.tok = links, whole, wide, tok
        self.masks = chip_masks(wide)

    def place(self, mask):
        return self.whole.at[block_rows(self.links, mask, self.wide, self.tok), :]

    def own(self):
        return block_rows(self.links, (0, 0), self.wide, self.tok)

    def start(self):
        here = self.place((0, 0))
        self.far = [self.links.copy(here, here, *mask) for mask in self.masks[1:]]
        self.near = [self.links.copy(here, here, 1, 0)]

    def forward(self):
        for mask, move in zip(self.masks[1:], self.far):
            move.wait_recv()
            there = self.place(mask)
            self.near.append(self.links.copy(there, there, 1, 0))

    def wait(self):
        for move in self.near:
            move.wait_recv()

    def by_chip(self, compute):
        for k, mask in enumerate(self.masks):
            if k:
                self.far[k - 1].wait_recv()
                there = self.place(mask)
                self.near.append(self.links.copy(there, there, 1, 0))
            self.near[k].wait_recv()
            compute(chip_rows(self.links, mask, self.wide, self.tok))

    def finish(self):
        self.links.finish(self.far + self.near)


class Collect:
    def __init__(self, links, parts, from_core, from_far, wide, tok):
        self.links, self.parts, self.wide, self.tok = links, parts, wide, tok
        self.from_core, self.from_far = from_core, from_far
        self.masks = chip_masks(wide)
        self.near, self.far = {}, {}

    def block(self, mask, other=0):
        return self.parts.at[block_rows(self.links, mask, self.wide, self.tok, other), :]

    def slot(self, ref, k):
        return ref.at[part_of(k, self.tok), :]

    def forward(self, k):
        self.near[k].wait_recv()
        mine = self.block(self.masks[k])
        mine[...] = (mine[...].astype(F32) + self.slot(self.from_core, k)[...].astype(F32)).astype(BF)
        self.far[k] = self.links.copy(mine, self.slot(self.from_far, k - 1), *self.masks[k])

    def run(self, compute):
        last = len(self.masks) - 1
        for k in range(last, -1, -1):
            compute(chip_rows(self.links, self.masks[k], self.wide, self.tok))
            self.near[k] = self.links.copy(self.block(self.masks[k], 1), self.slot(self.from_core, k), 1, 0)
            if k < last:
                self.forward(k + 1)

    def result(self):
        self.near[0].wait_recv()
        total = self.block((0, 0))[...].astype(F32) + self.slot(self.from_core, 0)[...].astype(F32)
        for k in range(1, len(self.masks)):
            self.far[k].wait_recv()
            total = total + self.slot(self.from_far, k - 1)[...].astype(F32)
        return total

    def finish(self):
        self.links.finish(list(self.near.values()) + list(self.far.values()))


def normed_block(values, gain):
    inverse = lax.rsqrt(jnp.mean(values * values, axis=-1, keepdims=True) + EPSILON)
    return (values * inverse * gain).astype(BF)


def norm_back(values, gain, grad_normed):
    inverse = lax.rsqrt(jnp.mean(values * values, axis=-1, keepdims=True) + EPSILON)
    scaled = grad_normed * gain
    gain_grad = jnp.sum(grad_normed * values * inverse, axis=0, keepdims=True)
    inner_sum = jnp.mean(scaled * values, axis=-1, keepdims=True)
    return inverse * scaled - values * inverse * inverse * inverse * inner_sum, gain_grad


def silu(values):
    return values * jax.nn.sigmoid(values)


def columns_loop(columns, tile, step):
    @pl.loop(0, columns // tile)
    def _(index):
        step(rows_at(index, tile))


def to_heads(links, src, dst, tok):
    wide = dst.shape[1]

    def block(seq):
        return src.at[rows_at(lax.div(seq, 2), tok), rows_at(lax.rem(seq, 2), wide)]

    here = dst.at[rows_at(links.seq, tok), :]
    moves = [links.copy(block(flipped(links.seq, mask)), here, 0, mask) for mask in range(1, 8)]
    return moves, links.local(block(links.seq), here)


def from_heads(links, src, dst, tok):
    wide = src.shape[1]
    here = dst.at[rows_at(links.z, tok), rows_at(links.y, wide)]
    moves = [links.copy(src.at[rows_at(flipped(links.seq, mask), tok), :], here, 0, mask) for mask in range(1, 8)]
    return moves, links.local(src.at[rows_at(links.seq, tok), :], here)


def to_columns(links, src, dst, tok, cols):
    here = dst.at[rows_at(links.row, tok), :]
    moves = [links.copy(src.at[:, rows_at(flipped(links.row, mask), cols)], here, mask, 0) for mask in (1, 2, 3)]
    return moves, links.local(src.at[:, rows_at(links.row, cols)], here)


def from_columns(links, src, dst, tok, cols):
    here = dst.at[:, rows_at(links.row, cols)]
    moves = [links.copy(src.at[rows_at(flipped(links.row, mask), tok), :], here, mask, 0) for mask in (1, 2, 3)]
    return moves, links.local(src.at[rows_at(links.row, tok), :], here)


def tile_mask(docs_col, docs_row, start, tile):
    keys = start + tile
    q_pos = lax.broadcasted_iota(jnp.int32, (tile, keys), 0) + start
    k_pos = lax.broadcasted_iota(jnp.int32, (tile, keys), 1)
    return (k_pos <= q_pos) & (docs_col[pl.ds(start, tile), :] == docs_row[:, pl.ds(0, keys)])


def softmax_tile(q, k, docs_col, docs_row, start, tile):
    scores = dot_right_t(q, k) * (HEAD_DIM ** (-0.5))
    scores = jnp.where(tile_mask(docs_col, docs_row, start, tile), scores, MASKED)
    expo = jnp.exp(scores - jnp.max(scores, axis=1, keepdims=True))
    return expo * (1.0 / jnp.sum(expo, axis=1, keepdims=True))


def attend(q_ref, k_ref, v_ref, docs_col, docs_row, out_ref):
    length = q_ref.shape[0]
    tile = min(256, length)

    @pl.loop(0, q_ref.shape[1] // HEAD_DIM)
    def _(head):
        lanes = rows_at(head, HEAD_DIM)
        for start in range(0, length, tile):
            keys, here = pl.ds(0, start + tile), pl.ds(start, tile)
            probs = softmax_tile(q_ref[here, lanes], k_ref[keys, lanes], docs_col, docs_row, start, tile)
            out_ref[here, lanes] = dot_plain(probs.astype(BF), v_ref[keys, lanes]).astype(BF)


def attend_back(q_ref, k_ref, v_ref, dout_ref, docs_col, docs_row, dq_ref, dk_ref, dv_ref, dk_acc, dv_acc):
    length = q_ref.shape[0]
    tile = min(256, length)
    scale = HEAD_DIM ** (-0.5)

    @pl.loop(0, q_ref.shape[1] // HEAD_DIM)
    def _(head):
        lanes = rows_at(head, HEAD_DIM)
        for start in reversed(range(0, length, tile)):
            keys, here = pl.ds(0, start + tile), pl.ds(start, tile)
            q, k, dout = q_ref[here, lanes], k_ref[keys, lanes], dout_ref[here, lanes]
            probs = softmax_tile(q, k, docs_col, docs_row, start, tile)
            dprob = dot_right_t(dout, v_ref[keys, lanes])
            delta = jnp.sum(probs * dprob, axis=1, keepdims=True)
            dscores = (probs * (dprob - delta)).astype(BF)
            dq_ref[here, lanes] = (dot_plain(dscores, k) * scale).astype(BF)
            dk, dv = dot_left_t(dscores, q), dot_left_t(probs.astype(BF), dout)
            if start + tile == length:
                dk_acc[...] = dk
                dv_acc[...] = dv
            else:
                dk_acc[keys, :] += dk
                dv_acc[keys, :] += dv
        dk_ref[:, lanes] = (dk_acc[...] * scale).astype(BF)
        dv_ref[:, lanes] = dv_acc[...].astype(BF)


def hidden_rows(r, rows_in, rows):
    def step(at):
        gate_val = dot_plain(rows_in[rows, :], r.gate_v[:, at])
        up_val = dot_plain(rows_in[rows, :], r.up_v[:, at])
        r.gate[rows, at] = gate_val.astype(BF)
        r.up[rows, at] = up_val.astype(BF)
        r.hidden[rows, at] = (silu(gate_val) * up_val).astype(BF)

    columns_loop(r.gate.shape[1], 256, step)


def hidden_back(r, rows):
    def step(at):
        dhid = dot_right_t(r.cot[rows, :], r.down_v[at, :])
        gate_val, up_val = r.gate[rows, at].astype(F32), r.up[rows, at].astype(F32)
        sigmoid = jax.nn.sigmoid(gate_val)
        r.gate[rows, at] = (dhid * up_val * (sigmoid * (1.0 + gate_val * (1.0 - sigmoid)))).astype(BF)
        r.up[rows, at] = (dhid * (gate_val * sigmoid)).astype(BF)

    columns_loop(r.gate.shape[1], 512, step)


def plain_rows(left, right, out):
    def compute(rows):
        def step(at):
            out[rows, at] = dot_plain(left[rows, :], right[:, at]).astype(BF)

        columns_loop(right.shape[1], 1024, step)

    return compute


def turned_rows(pairs, out):
    def compute(rows):
        def step(at):
            value = dot_right_t(pairs[0][0][rows, :], pairs[0][1][at, :])
            for left, right in pairs[1:]:
                value = value + dot_right_t(left[rows, :], right[at, :])
            out[rows, at] = value.astype(BF)

        columns_loop(pairs[0][1].shape[0], 512, step)

    return compute


def run_kernel(kernel, ident, moves, large, small, outs, scratch):
    anywhere = pl.BlockSpec(memory_space=pl.ANY)
    whole = pl.BlockSpec(memory_space=pltpu.VMEM)
    names = [*large, *small, *outs, *scratch]

    def body(*refs):
        kernel(Links(*refs[-2:]), SimpleNamespace(**dict(zip(names, refs[:-2], strict=True))))

    results = pl.pallas_call(
        body,
        out_shape=[jax.ShapeDtypeStruct(*item) for item in outs.values()],
        in_specs=[anywhere] * len(large) + [whole] * len(small),
        out_specs=[anywhere] * len(outs),
        scratch_shapes=[pltpu.VMEM(*item) for item in scratch.values()] + [pltpu.SemaphoreType.DMA((moves,))] * 2,
        compiler_params=pltpu.CompilerParams(
            collective_id=ident, has_side_effects=True, vmem_limit_bytes=VMEM_LIMIT
        ),
    )(*large.values(), *small.values())
    return SimpleNamespace(**dict(zip(outs, results, strict=True)))


def typed(kind, **shapes):
    return {name: (dims, kind) for name, dims in shapes.items()}


ALL_MASKS = [(1, 0), (2, 0), (3, 0), (0, 2), (2, 2)] + [(0, mask) for mask in (1, 3, 4, 5, 6, 7)]


def forward_kernel(links, r):
    links.greet(ALL_MASKS)
    row = links.row
    tok, width = r.x.shape
    cols = r.gmu_gate.shape[1]
    part = r.part
    outs = []

    def keep(ref, out):
        outs.append(links.local(ref, out))

    gmu_in, gmu_to = Gather(links, r.gmu_gate, r.gmu_gate_w, False, 1), Gather(links, r.gmu_out, r.gmu_out_w, True, 1)
    weights_g = [gmu_in, gmu_to]
    weights_1 = [
        Gather(links, r.f1_gate, r.f1_gate_w, False, 2),
        Gather(links, r.f1_up, r.f1_up_w, False, 2),
        Gather(links, r.f1_down, r.f1_down_w, True, 2),
    ]
    weights_q = [Gather(links, r.query, r.query_w, False, 1), Gather(links, r.attn_out, r.attn_out_w, True, 1)]
    weights_2 = [
        Gather(links, r.f2_gate, r.f2_gate_w, False, 2),
        Gather(links, r.f2_up, r.f2_up_w, False, 2),
        Gather(links, r.f2_down, r.f2_down_w, True, 2),
    ]
    gate_2, up_2, down_2 = weights_2

    each(weights_g, Gather.over_z, 2, 1)
    for weight in weights_g:
        weight.own()

    spread_a = Spread(links, r.rows_a, False, tok)
    r.rows_a[spread_a.own(), :] = normed_block(r.x[...].astype(F32), r.gain_a[...])
    spread_a.start()
    spread_y = Spread(links, r.cot_rows, True, tok)
    own_y = links.local(r.cotangent, r.cot_rows.at[spread_y.own(), :])
    k_cols = to_columns(links, r.keys, r.k_cols, tok, cols)
    v_cols = to_columns(links, r.values, r.v_cols, tok, cols)
    mem_moves = to_columns(links, r.memory, r.mem, tok, cols)
    spread_a.forward()
    landed(k_cols)
    landed(v_cols)
    k_moves = to_heads(links, r.k_cols, r.k_heads, tok)
    v_moves = to_heads(links, r.v_cols, r.v_heads, tok)
    each(weights_g, Gather.over_z, 3)
    own_y.wait()
    spread_y.start()
    each(weights_1, Gather.over_z, 2, 1, 3)
    each(weights_g, Gather.over_y, 2, 1, 3)
    for weight in weights_1 + weights_q + [gate_2]:
        weight.own()
    spread_a.wait()
    landed(mem_moves)
    keep(r.rows_a, r.rows_a_out)
    keep(r.mem, r.mem_out)
    spread_y.forward()
    gmu_in.arrived()
    load_in = links.local(r.gmu_gate_w, r.in_v)
    gmu_to.arrived()
    load_out = links.local(r.gmu_out_w, r.out_v)
    load_in.wait()

    def gmu_step(at):
        value = dot_plain(r.rows_a[...], r.in_v[:, at])
        r.pre[:, at] = value.astype(BF)
        r.act[:, at] = (r.mem[:, at].astype(F32) * silu(value)).astype(BF)

    columns_loop(cols, 256, gmu_step)
    load_out.wait()
    collect_a = Collect(links, part, r.core_a, r.far_a, False, tok)
    collect_a.run(plain_rows(r.act, r.out_v, part))
    keep(r.pre, r.pre_out)
    keep(r.act, r.act_out)
    r.x_one[...] = r.x[...].astype(F32) + collect_a.result()
    keep(r.x_one, r.x_one_out)

    spread_b = Spread(links, r.rows_b, True, tok)
    r.rows_b[spread_b.own(), :] = normed_block(r.x_one[...], r.gain_b[...])
    spread_b.start()
    each(weights_q, Gather.over_z, 2, 1)
    each(weights_1, Gather.over_y, 2, 1, 3)
    spread_b.forward()
    spread_b.wait()
    keep(r.rows_b, r.rows_b_out)
    each(weights_q, Gather.over_z, 3)
    gate_2.over_z(2, 1, 3)
    each(weights_q, Gather.over_y, 2, 1)
    loads = []
    for weight, place in zip(weights_1, (r.gate_v, r.up_v, r.down_v)):
        weight.arrived()
        loads.append(links.local(weight.whole, place))
    collect_a.finish()
    wait(loads)
    hidden_rows(r, r.rows_b, pl.ds(0, 8 * tok))
    spread_a.finish()
    outs[0].wait()
    del outs[0]
    collect_b = Collect(links, part, r.core_b, r.far_b, True, tok)
    collect_b.run(plain_rows(r.hidden, r.down_v, part))
    up_2.over_z(2, 1, 3)
    each(weights_q, Gather.over_y, 3)
    gate_2.over_y(2, 1, 3)
    landed(k_moves)
    landed(v_moves)
    keep(r.k_heads, r.k_heads_out)
    keep(r.v_heads, r.v_heads_out)
    keep(r.gate, r.gate_out)
    keep(r.up, r.up_out)
    keep(r.hidden, r.hidden_out)
    r.x_two[...] = r.x_one[...] + collect_b.result()
    keep(r.x_two, r.x_two_out)

    spread_c = Spread(links, r.rows_a, False, tok)
    r.rows_a[spread_c.own(), :] = normed_block(r.x_two[...], r.gain_c[...])
    spread_c.start()
    loads = []
    for weight, place in zip(weights_q, (r.in_v, r.out_v)):
        weight.arrived()
        loads.append(links.local(weight.whole, place))
    spread_c.forward()
    wait(loads)
    spread_c.wait()
    keep(r.rows_a, r.rows_c_out)

    def query_step(at):
        r.q_cols[:, at] = dot_plain(r.rows_a[...], r.in_v[:, at]).astype(BF)

    columns_loop(cols, 512, query_step)
    q_moves = to_heads(links, r.q_cols, r.q_heads, tok)
    up_2.own()
    up_2.over_y(2, 1)
    landed(q_moves)
    keep(r.q_heads, r.q_heads_out)
    attend(r.q_heads, r.k_heads, r.v_heads, r.docs_col, r.docs_row, r.out_heads)
    spread_b.finish()
    wait(outs)
    outs.clear()
    out_moves = from_heads(links, r.out_heads, r.attended, tok)
    down_2.over_z(2, 1, 3)
    up_2.over_y(3)
    down_2.own()
    landed(out_moves)
    keep(r.attended, r.attended_out)
    collect_b.finish()
    collect_c = Collect(links, part, r.core_c, r.far_c, False, tok)
    collect_c.run(plain_rows(r.attended, r.out_v, part))
    down_2.over_y(2, 1)
    r.x_three[...] = r.x_two[...] + collect_c.result()
    keep(r.x_three, r.x_three_out)
    spread_d = Spread(links, r.rows_b, True, tok)
    r.rows_b[spread_d.own(), :] = normed_block(r.x_three[...], r.gain_d[...])
    spread_d.start()
    spread_d.forward()
    down_2.over_y(3)
    spread_d.wait()
    keep(r.rows_b, r.rows_d_out)
    for weight in weights_2:
        weight.arrived()
    spread_y.wait()
    wait(outs)
    links.finish()


def forward_pass(large, small):
    tok, width = small["x"].shape
    cols = large["gmu_gate"].shape[1]
    half = large["f1_gate"].shape[1] // 2
    tokens = 4 * tok
    positions = small["docs_col"].shape[0]
    heads = (positions, cols * tokens // positions)
    inner, outer = (width, half), (half, width)
    outs = typed(
        BF,
        gmu_gate_w=(width, cols),
        gmu_out_w=(cols, width),
        f1_gate_w=inner,
        f1_up_w=inner,
        f1_down_w=outer,
        query_w=(width, cols),
        attn_out_w=(cols, width),
        f2_gate_w=inner,
        f2_up_w=inner,
        f2_down_w=outer,
        rows_a_out=(tokens, width),
        mem_out=(tokens, cols),
        pre_out=(tokens, cols),
        act_out=(tokens, cols),
        rows_b_out=(2 * tokens, width),
        gate_out=(2 * tokens, half),
        up_out=(2 * tokens, half),
        hidden_out=(2 * tokens, half),
        rows_c_out=(tokens, width),
        q_heads_out=heads,
        k_heads_out=heads,
        v_heads_out=heads,
        attended_out=(tokens, cols),
        rows_d_out=(2 * tokens, width),
        cot_rows=(2 * tokens, width),
    ) | typed(F32, x_one_out=(tok, width), x_two_out=(tok, width), x_three_out=(tok, width))
    scratch = typed(
        BF,
        rows_a=(tokens, width),
        mem=(tokens, cols),
        k_cols=(tokens, cols),
        v_cols=(tokens, cols),
        in_v=(width, cols),
        out_v=(cols, width),
        pre=(tokens, cols),
        act=(tokens, cols),
        part=(2 * tokens, width),
        core_a=(2 * tok, width),
        far_a=(tok, width),
        core_b=(4 * tok, width),
        far_b=(3 * tok, width),
        core_c=(2 * tok, width),
        far_c=(tok, width),
        rows_b=(2 * tokens, width),
        gate_v=inner,
        up_v=inner,
        down_v=outer,
        gate=(2 * tokens, half),
        up=(2 * tokens, half),
        hidden=(2 * tokens, half),
        q_cols=(tokens, cols),
        q_heads=heads,
        k_heads=heads,
        v_heads=heads,
        out_heads=heads,
        attended=(tokens, cols),
    ) | typed(F32, x_one=(tok, width), x_two=(tok, width), x_three=(tok, width))
    return run_kernel(forward_kernel, 0, 256, large, small, outs, scratch)


def weight_blocks(links, order, pairs, stages, blocks):
    size = stages[0].shape[0]
    depth = size // len(pairs)
    moves = [None, None]
    for count, block in enumerate(order):
        stage, kind = stages[count % 2], count % 2
        if moves[kind] is not None:
            moves[kind].wait()
        at = rows_at(block, depth)
        for k, (left, right) in enumerate(pairs):
            stage[part_of(k, depth), :] = dot_left_t(left[:, at], right[...]).astype(BF)
        moves[kind] = links.local(stage, blocks.at[rows_at(block, size), :])
    for move in moves:
        if move is not None:
            move.wait()


class Scatter:
    def __init__(self, links, blocks, land_y, land_z, here, there, total, turned, parts, *outs):
        self.links, self.blocks, self.land_y, self.land_z = links, blocks, land_y, land_z
        self.here, self.there, self.total, self.turned, self.parts, self.outs = here, there, total, turned, parts, outs
        self.size = blocks.shape[0] // 8
        self.y_moves, self.z_moves = {}, {}

    def slot(self, ref, k):
        return ref.at[part_of(k, self.size), :]

    def block(self, step, y):
        return self.blocks.at[rows_at(2 * flipped(self.links.z, step) + y, self.size), :]

    def over_y(self, *steps):
        for step in steps:
            self.y_moves[step] = self.links.copy(
                self.block(step, 1 - self.links.y), self.slot(self.land_y, step), 0, 1
            )

    def over_z(self, *steps):
        for step in steps:
            first = self.links.local(self.block(step, self.links.y), self.here)
            self.y_moves[step].wait_recv()
            mine = self.slot(self.land_y, step)
            second = self.links.local(mine, self.there)
            first.wait()
            second.wait()
            total = self.here[...].astype(F32) + self.there[...].astype(F32)
            mask = 2 * step
            if self.parts == 1 and step == 2:
                self.z_moves[3].wait_recv()
                self.links.local(self.slot(self.land_z, 2), self.there).wait()
                total = total + self.there[...].astype(F32)
            elif self.parts == 1 and step == 3:
                mask = 2
            self.here[...] = total.astype(BF)
            self.links.local(self.here, mine).wait()
            self.z_moves[step] = self.links.copy(mine, self.slot(self.land_z, step - 1), 0, mask)

    def store(self, k, half):
        rows, width = self.total.shape
        if k < len(self.outs) - 1:
            self.links.local(self.total, self.outs[k].at[:, rows_at(half, width)]).wait()
        else:
            self.turned[...] = self.total[...].T
            self.links.local(self.turned, self.outs[k].at[rows_at(half, width), :]).wait()

    def spots(self):
        rows = self.total.shape[0]
        return [ref.at[part_of(n, rows), :] for ref in (self.here, self.there) for n in range(2)]

    def add(self, sources, half):
        rows, spots = self.total.shape[0], self.spots()
        for k in range(len(self.outs)):
            wait([self.links.local(source.at[part_of(k, rows), :], spot) for source, spot in zip(sources, spots)])
            total = spots[0][...].astype(F32)
            for spot in spots[1 : len(sources)]:
                total = total + spot[...].astype(F32)
            self.total[...] = total
            self.store(k, half)

    def finish_other(self):
        for step in (1, 3):
            self.z_moves[step].wait_recv()
        self.add([self.slot(self.land_z, 0), self.slot(self.land_z, 2)], 1 - self.links.parity)

    def finish(self):
        self.y_moves[0].wait_recv()
        self.z_moves[2].wait_recv()
        sources = [self.block(0, self.links.y), self.slot(self.land_y, 0), self.slot(self.land_z, 1)]
        if self.parts == 1:
            self.z_moves[1].wait_recv()
            self.add([*sources, self.slot(self.land_z, 0)], 0)
        else:
            self.add(sources, self.links.parity)


def backward_kernel(links, r):
    links.greet(ALL_MASKS)
    row, seq, y = links.row, links.seq, links.y
    tok, width = r.grad.shape
    cols = r.left.shape[1]
    half = r.gate.shape[1]
    part, grad = r.part, r.grad
    everything = pl.ds(0, 8 * tok)
    outs = []
    stages = [r.stage_0, r.stage_1]
    depth = r.total.shape[0]
    small_stages = [ref.at[part_of(0, 2 * depth), part_of(0, cols)] for ref in stages]
    totals = [r.total, r.turned]
    small_totals = [r.total.at[:, part_of(0, cols)], r.turned.at[part_of(0, cols), :]]
    far_y = [2 * z + 1 - y for z in range(4)]
    own_y = [2 * z + y for z in range(4)]

    loads = [
        links.local(r.cot_rows, r.cot),
        links.local(r.rows_d, r.rows),
        links.local(r.f2_gate_w, r.gate_v),
        links.local(r.f2_up_w, r.up_v),
        links.local(r.f2_down_w, r.down_v),
        links.local(r.x_three, r.values),
    ]
    wait(loads)
    hidden_rows(r, r.rows, everything)
    for k in range(2):
        hidden_back(r, part_of(k, 4 * tok))
    pairs = [(r.rows, r.gate), (r.rows, r.up), (r.cot, r.hidden)]
    collect_d = Collect(links, part, r.core_b, r.far_b, True, tok)
    collect_d.run(turned_rows([(r.gate, r.gate_v), (r.up, r.up_v)], part))
    weight_blocks(links, far_y, pairs, stages, r.blocks_2)
    stream_2 = Scatter(links, r.blocks_2, r.land_y_2, r.land_z_2, *stages, *totals, 2, r.f2_gate_g, r.f2_up_g, r.f2_down_g)
    stream_2.over_y(2)
    dx, gain_grad = norm_back(r.values[...], r.gain_d[...], collect_d.result())
    r.gains[pl.ds(3, 1), :] = gain_grad
    grad[...] = r.cotangent[...].astype(F32) + dx

    spread_a = Spread(links, r.cot_a, False, tok)
    r.cot_a[spread_a.own(), :] = grad[...].astype(BF)
    spread_a.start()
    weight_blocks(links, own_y, pairs, stages, r.blocks_2)
    in_v = r.gate_v.at[:, pl.ds(0, cols)]
    heads = r.q_heads.shape[1]
    q_v, k_v, v_v = (r.gate.at[:, part_of(k, heads)] for k in range(3))
    dout_v = r.dout_v
    dq_v, dk_v, dv_v = (r.up.at[:, part_of(k, heads)] for k in range(3))
    loads = [
        links.local(r.attn_out_w, r.out_w),
        links.local(r.query_w, in_v),
        links.local(r.attended, r.left),
        links.local(r.q_heads, q_v),
        links.local(r.k_heads, k_v),
        links.local(r.v_heads, v_v),
    ]
    spread_a.forward()
    for k in range(4):
        plain_rows(r.hidden, r.down_v, r.rows)(part_of(k, 2 * tok))
    collect_d.finish()
    wait(loads)
    spread_a.wait()

    def back_step(at):
        r.dcols[:, at] = dot_right_t(r.cot_a[...], r.out_w[at, :]).astype(BF)

    columns_loop(cols, 512, back_step)
    dout_moves = to_heads(links, r.dcols, dout_v, tok)
    landed(dout_moves)
    attend_back(
        q_v, k_v, v_v, dout_v, r.docs_col, r.docs_row, dq_v, dk_v, dv_v, r.dk_acc, r.dv_acc
    )
    dq_moves = from_heads(links, dq_v, r.dq_cols, tok)
    dk_moves = from_heads(links, dk_v, r.k_cols, tok)
    dv_moves = from_heads(links, dv_v, r.v_cols, tok)
    stream_2.over_y(3, 1, 0)
    rows_c = part.at[pl.ds(4 * tok, 4 * tok), :]
    load = links.local(r.rows_c, rows_c)
    collect_m = Collect(links, r.rows, r.core_m, r.far_m, True, tok)
    collect_m.run(lambda rows: None)
    stream_2.over_z(2)
    load.wait()
    landed(dq_moves)
    collect_c = Collect(links, part, r.core_c, r.far_c, False, tok)
    collect_c.run(turned_rows([(r.dq_cols, in_v)], part))
    weight_blocks(links, range(8), [(rows_c, r.dq_cols), (r.cot_a, r.left)], small_stages, r.blocks_q)
    stream_q = Scatter(links, r.blocks_q, r.land_y_q, r.land_z_q, *small_stages, *small_totals, 1, r.query_g, r.attn_out_g)
    stream_q.over_y(3, 1, 2, 0)
    r.values[...] = r.values[...] + collect_m.result()
    links.local(r.values, r.mixed).wait()
    links.local(r.x_two, r.values).wait()
    dx, gain_grad = norm_back(r.values[...], r.gain_c[...], collect_c.result())
    r.gains[pl.ds(2, 1), :] = gain_grad
    grad[...] = grad[...] + dx

    spread_b = Spread(links, r.cot, True, tok)
    r.cot[spread_b.own(), :] = grad[...].astype(BF)
    spread_b.start()
    landed(dk_moves)
    landed(dv_moves)
    links.finish(dout_moves[0] + dq_moves[0] + dk_moves[0] + dv_moves[0])
    collect_m.finish()
    loads = [
        links.local(r.f1_down_w, r.down_v),
        links.local(r.gate_1, r.gate),
        links.local(r.up_1, r.up),
        links.local(r.f1_gate_w, r.gate_v),
        links.local(r.f1_up_w, r.up_v),
        links.local(r.hidden_1, r.hidden),
        links.local(r.rows_b, r.rows),
        links.local(r.x_one, r.values),
    ]
    home = [
        from_columns(links, r.k_cols, r.key_grad, tok, cols),
        from_columns(links, r.v_cols, r.value_grad, tok, cols),
    ]
    stream_2.over_z(3)
    wait(loads)
    spread_b.by_chip(lambda rows: hidden_back(r, rows))
    collect_c.finish()
    spread_a.finish()
    collect_b = Collect(links, part, r.core_b, r.far_b, True, tok)
    collect_b.run(turned_rows([(r.gate, r.gate_v), (r.up, r.up_v)], part))
    weight_blocks(links, far_y, pairs, stages, r.blocks_1)
    stream_1 = Scatter(links, r.blocks_1, r.land_y_1, r.land_z_1, *stages, *totals, 2, r.f1_gate_g, r.f1_up_g, r.f1_down_g)
    stream_1.over_y(2, 1, 3)
    weight_blocks(links, own_y, pairs, stages, r.blocks_1)
    stream_2.over_z(1)
    dx, gain_grad = norm_back(r.values[...], r.gain_b[...], collect_b.result())
    r.gains[pl.ds(1, 1), :] = gain_grad
    grad[...] = grad[...] + dx

    spread_g = Spread(links, r.cot_a, False, tok)
    r.cot_a[spread_g.own(), :] = grad[...].astype(BF)
    spread_g.start()
    spread_b.finish()
    collect_b.finish()
    rows_a = part.at[pl.ds(4 * tok, 4 * tok), :]
    loads = [
        links.local(r.gmu_out_w, r.out_w),
        links.local(r.gmu_gate_w, in_v),
        links.local(r.pre, r.dcols),
        links.local(r.mem, r.dq_cols),
        links.local(r.act, r.left),
        links.local(r.rows_a, rows_a),
    ]
    spread_g.forward()
    stream_q.over_z(3, 1)
    stream_1.over_z(2)
    wait(loads)
    spread_g.wait()

    def gmu_back(at):
        dact = dot_right_t(r.cot_a[...], r.out_w[at, :])
        pre, mem = r.dcols[:, at].astype(F32), r.dq_cols[:, at].astype(F32)
        sigmoid = jax.nn.sigmoid(pre)
        r.dcols[:, at] = (dact * (pre * sigmoid)).astype(BF)
        r.dq_cols[:, at] = (dact * mem * (sigmoid * (1.0 + pre * (1.0 - sigmoid)))).astype(BF)

    columns_loop(cols, 256, gmu_back)
    collect_g = Collect(links, part, r.core_c, r.far_c, False, tok)
    collect_g.run(turned_rows([(r.dq_cols, in_v)], part))
    home.append(from_columns(links, r.dcols, r.mem_grad, tok, cols))
    weight_blocks(links, range(8), [(rows_a, r.dq_cols), (r.cot_a, r.left)], small_stages, r.blocks_g)
    stream_g = Scatter(links, r.blocks_g, r.land_y_g, r.land_z_g, *small_stages, *small_totals, 1, r.gmu_gate_g, r.gmu_out_g)
    stream_g.over_y(3, 1, 2, 0)
    stream_1.over_y(0)
    stream_q.over_z(2)
    stream_1.over_z(1)
    dx, gain_grad = norm_back(r.x[...].astype(F32), r.gain_a[...], collect_g.result())
    grad[...] = grad[...] + dx
    outs.append(links.local(grad, r.input_grad))

    r.gains[pl.ds(0, 1), :] = gain_grad
    r.row_sums[row] = r.gains[...]
    for move in [links.copy(r.gains, r.row_sums.at[row], mask, 0) for mask in (1, 2, 3)]:
        move.wait_recv()
    r.seq_sums[seq] = r.row_sums[0] + r.row_sums[1] + r.row_sums[2] + r.row_sums[3]
    gain_moves = [links.copy(r.seq_sums.at[seq], r.seq_sums.at[seq], 0, mask) for mask in range(1, 8)]
    for moves in home:
        landed(moves)

    stream_1.over_z(3)
    stream_2.finish()
    stream_2.finish_other()
    stream_g.over_z(3, 1, 2)
    stream_q.finish()
    for move in gain_moves:
        move.wait_recv()
    total = r.seq_sums[0]
    for k in range(1, 8):
        total = total + r.seq_sums[k]
    r.gain_total[...] = total
    outs.append(links.local(r.gain_total, r.gain_grads))
    stream_1.finish()
    stream_1.finish_other()
    stream_g.finish()
    wait(outs)
    links.finish()


def backward_pass(large, small):
    tok, width = small["x"].shape
    tokens, cols = large["mem"].shape
    wide, half = large["gate_1"].shape
    depth = width // 8
    ffn, unit = (3 * depth, half), (2 * depth, cols)

    def times(count, shape):
        return (count * shape[0], shape[1])

    outs = typed(
        F32,
        mixed=(tok, width),
        input_grad=(tok, width),
        gain_grads=(4, width),
        f2_gate_g=(depth, 2 * half),
        f2_up_g=(depth, 2 * half),
        f2_down_g=(2 * half, depth),
        f1_gate_g=(depth, 2 * half),
        f1_up_g=(depth, 2 * half),
        f1_down_g=(2 * half, depth),
        query_g=(depth, cols),
        attn_out_g=(cols, depth),
        gmu_gate_g=(depth, cols),
        gmu_out_g=(cols, depth),
    ) | typed(
        BF,
        key_grad=(tok, width),
        value_grad=(tok, width),
        mem_grad=(tok, width),
        blocks_2=times(8, ffn),
        blocks_1=times(8, ffn),
        blocks_q=times(8, unit),
        blocks_g=times(8, unit),
        land_y_2=times(4, ffn),
        land_y_1=times(4, ffn),
        land_y_q=times(4, unit),
        land_y_g=times(4, unit),
        land_z_2=times(3, ffn),
        land_z_1=times(3, ffn),
        land_z_q=times(3, unit),
        land_z_g=times(3, unit),
    )
    scratch = typed(
        BF,
        rows=(wide, width),
        cot=(wide, width),
        cot_a=(tokens, width),
        gate_v=(width, half),
        up_v=(width, half),
        down_v=(half, width),
        out_w=(cols, width),
        gate=(wide, half),
        up=(wide, half),
        hidden=(wide, half),
        part=(wide, width),
        left=(tokens, cols),
        dcols=(tokens, cols),
        dq_cols=(tokens, cols),
        k_cols=(tokens, cols),
        v_cols=(tokens, cols),
        dout_v=(small["docs_col"].shape[0], cols // 2),
        core_b=(4 * tok, width),
        far_b=(3 * tok, width),
        core_m=(4 * tok, width),
        far_m=(3 * tok, width),
        core_c=(2 * tok, width),
        far_c=(tok, width),
        stage_0=ffn,
        stage_1=ffn,
    ) | typed(
        F32,
        values=(tok, width),
        grad=(tok, width),
        dk_acc=(small["docs_col"].shape[0], HEAD_DIM),
        dv_acc=(small["docs_col"].shape[0], HEAD_DIM),
        total=(depth, half),
        turned=(half, depth),
        gains=(4, width),
        gain_total=(4, width),
        row_sums=(4, 4, width),
        seq_sums=(8, 4, width),
    )
    return run_kernel(backward_kernel, 1, 384, large, small, outs, scratch)


def body_general(
    block_input,
    memory,
    key_cache,
    value_cache,
    doc_lengths,
    gmu_gate,
    gmu_out,
    ffn1_gate,
    ffn1_up,
    ffn1_down,
    query_weight,
    attn_out,
    ffn2_gate,
    ffn2_up,
    ffn2_down,
    gain_a,
    gain_b,
    gain_c,
    gain_d,
    cotangent,
):
    seq_count = lax.axis_size("seq")
    row_count = lax.axis_size("row")
    seq_index = lax.axis_index("seq")
    tok_len = block_input.shape[1]
    width = block_input.shape[2]
    head_count = query_weight.shape[1] // HEAD_DIM
    depth = ffn1_gate.shape[0]
    half = ffn1_gate.shape[1] // 2
    z_count = seq_count // 2
    z_index, y_index = seq_index // 2, seq_index % 2
    parity = z_index % 2

    def spread(normed):
        return lax.all_gather(normed[None], "row", axis=0, tiled=True).reshape(
            row_count * tok_len, width
        )

    def collect(partial_value):
        return lax.psum_scatter(
            partial_value.reshape(row_count, tok_len, width).astype(BF),
            "row",
            scatter_dimension=0,
            tiled=True,
        ).astype(F32)[0]

    def spread_wide(normed):
        both = jnp.stack([normed, swapped(normed, "seq", 2)])
        return lax.all_gather(both[None], "row", axis=0, tiled=True).reshape(
            2 * row_count * tok_len, width
        )

    def collect_wide(partial_value):
        parts = partial_value.reshape(row_count, 2, tok_len, width).astype(BF)
        summed = lax.psum_scatter(parts, "row", scatter_dimension=0, tiled=True)[0]
        other = swapped(summed[1], "seq", 2)
        return summed[0].astype(F32) + other.astype(F32)

    def gather_ffn(gate, up, down):
        shard = jnp.stack([gate, up, down.T])
        whole = jnp.zeros((z_count, 2, 3, depth, half), BF)
        for step in range(z_count):
            want = (parity + step) % 2
            piece = lax.dynamic_slice_in_dim(shard, want * half, half, axis=2)
            if step:
                piece = swapped(piece, "seq", 2 * step)
            over = swapped(piece, "seq", 1)
            source = z_index ^ step
            whole = lax.dynamic_update_slice(whole, piece[None, None], (source, y_index, 0, 0, 0))
            whole = lax.dynamic_update_slice(whole, over[None, None], (source, 1 - y_index, 0, 0, 0))
        whole = whole.transpose(2, 0, 1, 3, 4).reshape(3, seq_count * depth, half)
        return whole[0], whole[1], whole[2]

    def scatter_ffn(gate_grad, up_grad, down_grad_t):
        whole = jnp.stack([gate_grad.astype(BF), up_grad.astype(BF), down_grad_t.astype(BF)])
        whole = whole.reshape(3, z_count, 2, depth, half)
        sums = [None, None]
        for step in range(z_count):
            target = z_index ^ step
            there = lax.dynamic_slice(
                whole, (0, target, 1 - y_index, 0, 0), (3, 1, 1, depth, half)
            )[:, 0, 0]
            here = lax.dynamic_slice(whole, (0, target, y_index, 0, 0), (3, 1, 1, depth, half))[:, 0, 0]
            total = here.astype(F32) + swapped(there, "seq", 1).astype(F32)
            if step:
                total = swapped(total.astype(BF), "seq", 2 * step).astype(F32)
            kind = step % 2
            sums[kind] = total if sums[kind] is None else sums[kind] + total
        pair = jnp.stack(sums)
        lower = lax.dynamic_index_in_dim(pair, parity, 0, keepdims=False)
        upper = lax.dynamic_index_in_dim(pair, 1 - parity, 0, keepdims=False)
        full = jnp.concatenate([lower, upper], axis=2)
        return full[0], full[1], full[2].T

    gmu_gate_full = lax.all_gather(gmu_gate, "seq", axis=0, tiled=True)
    gmu_out_full = lax.all_gather(gmu_out, "seq", axis=1, tiled=True)
    gate_one_w, up_one_w, down_one_t = gather_ffn(ffn1_gate, ffn1_up, ffn1_down)
    query_full = lax.all_gather(query_weight, "seq", axis=0, tiled=True)
    aout_full = lax.all_gather(attn_out, "seq", axis=1, tiled=True)
    gate_two_w, up_two_w, down_two_t = gather_ffn(ffn2_gate, ffn2_up, ffn2_down)

    def ffn_forward(rows_in, gate_weight, up_weight, down_weight_t):
        gate_val = dot_plain(rows_in, gate_weight)
        up_val = dot_plain(rows_in, up_weight)
        hidden = (jax.nn.silu(gate_val) * up_val).astype(BF)
        return (dot_right_t(hidden, down_weight_t), gate_val, up_val, hidden)

    def ffn_backward(cot_rows, rows_in, gate_val, up_val, hidden, gate_weight, up_weight, down_weight_t):
        dhid = dot_plain(cot_rows, down_weight_t)
        dgate = (dhid * up_val * silu_slope(gate_val)).astype(BF)
        dup = (dhid * jax.nn.silu(gate_val)).astype(BF)
        drows = dot_right_t(dgate, gate_weight) + dot_right_t(dup, up_weight)
        down_grad_t = dot_left_t(cot_rows, hidden)
        gate_grad = dot_left_t(rows_in, dgate)
        up_grad = dot_left_t(rows_in, dup)
        return (drows, gate_grad, up_grad, down_grad_t)

    mem_cols = lax.all_to_all(memory, "row", split_axis=2, concat_axis=0, tiled=True)
    mem_cols = mem_cols.reshape(row_count * tok_len, -1).astype(F32)
    kv_here = lax.all_to_all(
        jnp.concatenate([key_cache, value_cache], axis=0)[:, None], "row", split_axis=3, concat_axis=1, tiled=True
    )

    x_zero = block_input[0].astype(F32)
    normed_a, inv_a = rms_forward(x_zero, gain_a)
    rows_a = spread(normed_a.astype(BF))
    gmu_pre = dot_plain(rows_a, gmu_gate_full)
    gmu_act = (mem_cols * jax.nn.silu(gmu_pre)).astype(BF)
    x_one = x_zero + collect(dot_plain(gmu_act, gmu_out_full))
    normed_b, inv_b = rms_forward(x_one, gain_b)
    rows_b = spread_wide(normed_b.astype(BF))
    part_one, gate_one, up_one, hidden_one = ffn_forward(rows_b, gate_one_w, up_one_w, down_one_t)
    x_two = x_one + collect_wide(part_one)
    normed_c, inv_c = rms_forward(x_two, gain_c)
    rows_c = spread(normed_c.astype(BF))
    queries = dot_plain(rows_c, query_full).astype(BF)
    head_shape = (row_count, tok_len, head_count, HEAD_DIM)
    attended, ring_grad = ring_attention(
        queries.reshape(head_shape), kv_here.reshape((2,) + head_shape), doc_lengths, tok_len, head_count
    )

    def attention_grad(dout):
        return ring_grad(dout.reshape(head_shape))

    attended = attended.reshape(row_count * tok_len, head_count * HEAD_DIM)
    x_three = x_two + collect(dot_plain(attended, aout_full))
    normed_d, inv_d = rms_forward(x_three, gain_d)
    rows_d = spread_wide(normed_d.astype(BF))
    part_two, gate_two, up_two, hidden_two = ffn_forward(rows_d, gate_two_w, up_two_w, down_two_t)
    mixed = x_three + collect_wide(part_two)

    grad_y = cotangent[0].astype(F32)
    drows_d, gate_two_grad, up_two_grad, down_two_grad = ffn_backward(
        spread_wide(cotangent[0]), rows_d, gate_two, up_two, hidden_two, gate_two_w, up_two_w, down_two_t
    )
    dx_d, gain_d_grad = rms_backward(x_three, inv_d, gain_d, collect_wide(drows_d))
    grad_three = grad_y + dx_d
    cot_three = spread(grad_three.astype(BF))
    dattended = dot_right_t(cot_three, aout_full)
    aout_grad = dot_left_t(attended, cot_three)
    dqueries, kv_grad = attention_grad(dattended.astype(BF))
    dqueries = dqueries.reshape(row_count * tok_len, head_count * HEAD_DIM)
    query_grad = dot_left_t(rows_c, dqueries)
    dx_c, gain_c_grad = rms_backward(x_two, inv_c, gain_c, collect(dot_right_t(dqueries, query_full)))
    grad_two = grad_three + dx_c
    drows_b, gate_one_grad, up_one_grad, down_one_grad = ffn_backward(
        spread_wide(grad_two.astype(BF)), rows_b, gate_one, up_one, hidden_one, gate_one_w, up_one_w, down_one_t
    )
    dx_b, gain_b_grad = rms_backward(x_one, inv_b, gain_b, collect_wide(drows_b))
    grad_one = grad_two + dx_b
    cot_one = spread(grad_one.astype(BF))
    dact = dot_right_t(cot_one, gmu_out_full)
    gout_grad = dot_left_t(gmu_act, cot_one)
    mem_grad_cols = dact * jax.nn.silu(gmu_pre)
    dpre = (dact * mem_cols * silu_slope(gmu_pre)).astype(BF)
    gate_a_grad = dot_left_t(rows_a, dpre)
    dx_a, gain_a_grad = rms_backward(x_zero, inv_a, gain_a, collect(dot_right_t(dpre, gmu_gate_full)))
    input_grad = grad_one + dx_a

    mem_grad = lax.all_to_all(
        mem_grad_cols.reshape(row_count, tok_len, -1).astype(BF), "row", split_axis=0, concat_axis=2, tiled=True
    ).astype(F32)
    kv_home = lax.all_to_all(
        kv_grad.reshape(2, row_count, tok_len, -1), "row", split_axis=1, concat_axis=3, tiled=True
    ).astype(F32)

    def scatter(grad, dim):
        return lax.psum_scatter(grad.astype(BF), "seq", scatter_dimension=dim, tiled=True).astype(F32)

    gate_two_out, up_two_out, down_two_out = scatter_ffn(gate_two_grad, up_two_grad, down_two_grad)
    aout_out = scatter(aout_grad, 1)
    query_out = scatter(query_grad, 0)
    gate_one_out, up_one_out, down_one_out = scatter_ffn(gate_one_grad, up_one_grad, down_one_grad)
    gout_out = scatter(gout_grad, 1)
    gate_a_out = scatter(gate_a_grad, 0)
    gain_grads = lax.psum((gain_a_grad, gain_b_grad, gain_c_grad, gain_d_grad), ("seq", "row"))
    return (
        mixed[None],
        input_grad[None],
        mem_grad,
        kv_home[0],
        kv_home[1],
        gate_a_out,
        gout_out,
        gate_one_out,
        up_one_out,
        down_one_out,
        query_out,
        aout_out,
        gate_two_out,
        up_two_out,
        down_two_out,
        gain_grads[0],
        gain_grads[1],
        gain_grads[2],
        gain_grads[3],
    )


def body_fast(
    block_input,
    memory,
    key_cache,
    value_cache,
    doc_lengths,
    gmu_gate,
    gmu_out,
    ffn1_gate,
    ffn1_up,
    ffn1_down,
    query_weight,
    attn_out,
    ffn2_gate,
    ffn2_up,
    ffn2_down,
    gain_a,
    gain_b,
    gain_c,
    gain_d,
    cotangent,
):
    seq_count = lax.axis_size("seq")
    row_count = lax.axis_size("row")
    seq_index = lax.axis_index("seq")
    positions = jnp.arange(seq_count * block_input.shape[1], dtype=jnp.int32)
    docs = lax.dynamic_index_in_dim(
        doc_numbers(doc_lengths, positions), seq_index // (seq_count // row_count), 0, keepdims=False
    )
    shared = dict(x=block_input[0], docs_col=docs[:, None], docs_row=docs[None, :])
    shared |= dict(gain_a=gain_a[None], gain_b=gain_b[None], gain_c=gain_c[None], gain_d=gain_d[None])
    kept = forward_pass(
        dict(
            cotangent=cotangent[0],
            memory=memory[0],
            keys=key_cache[0],
            values=value_cache[0],
            gmu_gate=gmu_gate,
            gmu_out=gmu_out,
            f1_gate=ffn1_gate,
            f1_up=ffn1_up,
            f1_down=ffn1_down,
            query=query_weight,
            attn_out=attn_out,
            f2_gate=ffn2_gate,
            f2_up=ffn2_up,
            f2_down=ffn2_down,
        ),
        shared,
    )
    back = backward_pass(
        dict(
            cot_rows=kept.cot_rows,
            rows_a=kept.rows_a_out,
            rows_b=kept.rows_b_out,
            rows_c=kept.rows_c_out,
            rows_d=kept.rows_d_out,
            q_heads=kept.q_heads_out,
            k_heads=kept.k_heads_out,
            v_heads=kept.v_heads_out,
            attended=kept.attended_out,
            mem=kept.mem_out,
            pre=kept.pre_out,
            act=kept.act_out,
            gate_1=kept.gate_out,
            up_1=kept.up_out,
            hidden_1=kept.hidden_out,
            x_one=kept.x_one_out,
            x_two=kept.x_two_out,
            x_three=kept.x_three_out,
            gmu_gate_w=kept.gmu_gate_w,
            gmu_out_w=kept.gmu_out_w,
            query_w=kept.query_w,
            attn_out_w=kept.attn_out_w,
            f1_gate_w=kept.f1_gate_w,
            f1_up_w=kept.f1_up_w,
            f1_down_w=kept.f1_down_w,
            f2_gate_w=kept.f2_gate_w,
            f2_up_w=kept.f2_up_w,
            f2_down_w=kept.f2_down_w,
        ),
        shared | dict(cotangent=cotangent[0]),
    )
    return (
        back.mixed[None],
        back.input_grad[None],
        back.mem_grad.astype(F32)[None],
        back.key_grad.astype(F32)[None],
        back.value_grad.astype(F32)[None],
        back.gmu_gate_g,
        back.gmu_out_g,
        back.f1_gate_g,
        back.f1_up_g,
        back.f1_down_g,
        back.query_g,
        back.attn_out_g,
        back.f2_gate_g,
        back.f2_up_g,
        back.f2_down_g,
        *(back.gain_grads[k] for k in range(4)),
    )


def solution(mesh):
    tokens = P("row", "seq", None)
    inner, outer = P("seq", "row"), P("row", "seq")
    in_specs = (
        (tokens,) * 4
        + (P(), inner, outer, inner, inner, outer, inner, outer, inner, inner, outer)
        + (P(),) * 4
        + (tokens,)
    )
    out_specs = (
        (tokens,) * 5
        + (inner, outer, inner, inner, outer, inner, outer, inner, inner, outer)
        + (P(),) * 4
    )
    seq_count, row_count = mesh.shape["seq"], mesh.shape["row"]
    body = body_fast if seq_count == 8 and row_count == 4 else body_general
    return jax.shard_map(body, mesh=mesh, in_specs=in_specs, out_specs=out_specs, check_vma=False)
```

```python
from types import SimpleNamespace

import jax
import jax.numpy as jnp
from jax import lax
from jax.experimental import pallas as pl
from jax.experimental.pallas import tpu as pltpu
from jax.sharding import PartitionSpec as P

HEAD_DIM = 128


EPSILON = 1e-05
MASKED = -1e30
BF = jnp.bfloat16
F32 = jnp.float32


def passed_along(value, axis, steps):
    count = lax.axis_size(axis)
    first, last = (max(0, -steps), min(count, count - steps))
    return lax.ppermute(value, axis, [(source, source + steps) for source in range(first, last)])


def shifted(value, axis, steps):
    count = lax.axis_size(axis)
    pairs = [(source, (source + steps) % count) for source in range(count)]
    return lax.ppermute(value, axis, pairs)


def swapped(value, axis, mask):
    count = lax.axis_size(axis)
    return lax.ppermute(value, axis, [(source, source ^ mask) for source in range(count)])


def silu_slope(values):
    sigmoid = jax.nn.sigmoid(values)
    return sigmoid * (1.0 + values * (1.0 - sigmoid))


def rms_forward(values, gain_vec):
    inverse = lax.rsqrt(jnp.mean(values * values, axis=-1, keepdims=True) + EPSILON)
    return (values * inverse * gain_vec, inverse)


def rms_backward(values, inverse, gain_vec, grad_normed):
    scaled = grad_normed * gain_vec
    gain_grad = jnp.sum(grad_normed * values * inverse, axis=0)
    inner_sum = jnp.mean(scaled * values, axis=-1, keepdims=True)
    return (inverse * scaled - values * inverse * inverse * inverse * inner_sum, gain_grad)


def doc_numbers(doc_lengths, positions):
    doc_ends = jnp.cumsum(doc_lengths, axis=1, dtype=jnp.int32)
    return jnp.sum((positions[None, :, None] >= doc_ends[:, None, :]).astype(jnp.int32), axis=-1)


def dot_plain(left, right):
    return jnp.dot(left, right, preferred_element_type=F32)


def dot_left_t(left, right):
    return lax.dot_general(left, right, (((0,), (0,)), ((), ())), preferred_element_type=F32)


def dot_right_t(left, right):
    return lax.dot_general(left, right, (((1,), (1,)), ((), ())), preferred_element_type=F32)


def ring_attention(queries, kv_here, doc_lengths, tok_len, head_count):
    seq_count = lax.axis_size("seq")
    seq_index = lax.axis_index("seq")
    row_count = queries.shape[0]
    score_scale = HEAD_DIM ** (-0.5)
    local_pos = jnp.arange(tok_len, dtype=jnp.int32)

    def allowed_pairs(source):
        q_positions = seq_index * tok_len + local_pos
        key_pos = source * tok_len + local_pos
        q_docs = doc_numbers(doc_lengths, q_positions)
        key_docs = doc_numbers(doc_lengths, key_pos)
        causal = key_pos[None, :] <= q_positions[:, None]
        same_doc = q_docs[:, :, None] == key_docs[:, None, :]
        return (causal[None] & same_doc)[:, :, None, :]

    def absorb(softmax_state, kv_block, source):
        run_max, totals, accum = softmax_state
        scores = jnp.einsum("rihd,rjhd->rihj", queries, kv_block[0], preferred_element_type=F32)
        allowed = allowed_pairs(source)
        scores = jnp.where(allowed, scores * score_scale, MASKED)
        new_max = jnp.maximum(run_max, jnp.max(scores, axis=-1, keepdims=True))
        weights = jnp.where(allowed, jnp.exp(scores - new_max), 0.0)
        shrink = jnp.exp(run_max - new_max)
        totals = totals * shrink + jnp.sum(weights, axis=-1, keepdims=True)
        accum = accum * shrink + jnp.einsum(
            "rihj,rjhd->rihd", weights.astype(BF), kv_block[1], preferred_element_type=F32
        )
        return (new_max, totals, accum)

    stat_shape = (row_count, tok_len, head_count, 1)
    start_state = (
        jnp.full(stat_shape, MASKED, F32),
        jnp.zeros(stat_shape, F32),
        jnp.zeros((row_count, tok_len, head_count, HEAD_DIM), F32),
    )
    first_state = absorb(start_state, kv_here, seq_index)

    def cycle_forward(section_num, carry):
        softmax_state, kv_block = carry
        kv_block = passed_along(kv_block, "seq", 1)
        source = (seq_index - section_num) % seq_count
        return (absorb(softmax_state, kv_block, source), kv_block)

    final_state, _ = lax.fori_loop(1, seq_count, cycle_forward, (first_state, kv_here))
    run_max, totals, accum = final_state
    outputs = accum / totals
    log_sums = run_max + jnp.log(totals)

    def backward(dout):
        row_delta = jnp.sum(dout.astype(F32) * outputs, axis=-1, keepdims=True)
        head_shape = (row_count, tok_len, head_count, HEAD_DIM)

        def cycle_backward(section_num, carry):
            query_acc, kv_block, grad_block = carry
            source = (seq_index - section_num) % seq_count
            scores = jnp.einsum("rihd,rjhd->rihj", queries, kv_block[0], preferred_element_type=F32)
            allowed = allowed_pairs(source)
            probs = jnp.where(allowed, jnp.exp(scores * score_scale - log_sums), 0.0)
            dprob = jnp.einsum("rihd,rjhd->rihj", dout, kv_block[1], preferred_element_type=F32)
            dscores = (probs * (dprob - row_delta)).astype(BF)
            query_acc = (
                query_acc
                + jnp.einsum("rihj,rjhd->rihd", dscores, kv_block[0], preferred_element_type=F32)
                * score_scale
            )
            key_part = (
                jnp.einsum("rihj,rihd->rjhd", dscores, queries, preferred_element_type=F32)
                * score_scale
            )
            value_part = jnp.einsum(
                "rihj,rihd->rjhd", probs.astype(BF), dout, preferred_element_type=F32
            )
            grad_block = grad_block + jnp.stack([key_part, value_part])
            kv_block = passed_along(kv_block, "seq", 1)
            grad_block = shifted(grad_block.astype(BF), "seq", 1).astype(grad_block.dtype)
            return (query_acc, kv_block, grad_block)

        query_acc, _, grad_block = lax.fori_loop(
            0,
            seq_count,
            cycle_backward,
            (jnp.zeros(head_shape, F32), kv_here, jnp.zeros((2,) + head_shape, F32)),
        )
        return query_acc.astype(BF), grad_block.astype(BF)

    return outputs.astype(BF), backward


MESH = pl.DeviceIdType.MESH
VMEM_LIMIT = 62 * 2**20


def flipped(value, mask):
    bit = 1
    while bit <= mask:
        if mask & bit:
            value = value + bit - 2 * bit * lax.rem(lax.div(value, bit), 2)
        bit *= 2
    return value


def rows_at(index, size):
    return pl.ds(pl.multiple_of(index * size, size), size)


def part_of(index, size):
    return pl.ds(index * size, size)


class Links:
    def __init__(self, send, recv):
        self.send, self.recv, self.used, self.sent = send, recv, 0, []
        self.row, self.seq = lax.axis_index("row"), lax.axis_index("seq")
        self.z, self.y = lax.div(self.seq, 2), lax.rem(self.seq, 2)
        self.parity = lax.rem(self.z, 2)

    def device(self, row_mask, seq_mask):
        return {"row": flipped(self.row, row_mask), "seq": flipped(self.seq, seq_mask)}

    def greet(self, masks):
        barrier = pltpu.get_barrier_semaphore()
        for mask in masks:
            pl.semaphore_signal(barrier, inc=1, device_id=self.device(*mask), device_id_type=MESH)
        pl.semaphore_wait(barrier, len(masks))

    def slot(self):
        self.used += 1
        assert self.used <= self.send.shape[0]
        return self.used - 1

    def copy(self, src, dst, row_mask, seq_mask):
        slot = self.slot()
        move = pltpu.make_async_remote_copy(
            src_ref=src,
            dst_ref=dst,
            send_sem=self.send.at[slot],
            recv_sem=self.recv.at[slot],
            device_id=self.device(row_mask, seq_mask),
            device_id_type=MESH,
        )
        move.start()
        self.sent.append(move)
        return move

    def local(self, src, dst):
        move = pltpu.make_async_copy(src, dst, self.send.at[self.slot()])
        move.start()
        return move

    def finish(self, moves=None):
        moves = list(self.sent if moves is None else moves)
        for move in moves:
            move.wait_send()
        done = {id(move) for move in moves}
        self.sent = [move for move in self.sent if id(move) not in done]


def wait(moves):
    for move in moves:
        move.wait()


def landed(moves):
    for move in moves[0]:
        move.wait_recv()
    moves[1].wait()


class Gather:
    def __init__(self, links, shard, whole, outer, parts):
        self.links, self.shard, self.whole, self.outer, self.parts = links, shard, whole, outer, parts
        self.z_moves, self.y_moves = {}, {}

    def piece(self, step):
        if self.parts == 1:
            return self.shard
        part = lax.rem(self.links.parity + step, 2)
        if self.outer:
            return self.shard.at[rows_at(part, self.shard.shape[0] // 2), :]
        return self.shard.at[:, rows_at(part, self.shard.shape[1] // 2)]

    def place(self, source):
        if self.outer:
            return self.whole.at[:, rows_at(source, self.shard.shape[1])]
        return self.whole.at[rows_at(source, self.shard.shape[0]), :]

    def own(self):
        self.keep = self.links.local(self.piece(0), self.place(self.links.seq))
        self.y_moves[0] = self.links.copy(self.piece(0), self.place(self.links.seq), 0, 1)

    def over_z(self, *steps):
        for step in steps:
            if step == 3 and self.parts == 1:
                self.z_moves[2].wait_recv()
                here = self.place(flipped(self.links.seq, 4))
                self.z_moves[3] = self.links.copy(here, here, 0, 2)
            else:
                self.z_moves[step] = self.links.copy(self.piece(step), self.place(self.links.seq), 0, 2 * step)

    def over_y(self, *steps):
        for step in steps:
            if not (step == 2 and 3 in self.z_moves and self.parts == 1):
                self.z_moves[step].wait_recv()
            here = self.place(flipped(self.links.seq, 2 * step))
            self.y_moves[step] = self.links.copy(here, here, 0, 1)

    def arrived(self):
        self.keep.wait()
        for step in range(4):
            self.y_moves[step].wait_recv()


def each(weights, action, *steps):
    for step in steps:
        for weight in weights:
            action(weight, step)


def chip_masks(wide):
    return [(0, 0), (2, 0)] + ([(0, 2), (2, 2)] if wide else [])


def chip_rows(links, mask, wide, tok):
    chip = lax.div(flipped(links.row, mask[0]), 2)
    if wide:
        chip = chip * 2 + lax.rem(links.parity + mask[1] // 2, 2)
    return rows_at(chip, 2 * tok)


def block_rows(links, mask, wide, tok, other=0):
    chip = lax.div(flipped(links.row, mask[0]), 2)
    if wide:
        chip = chip * 2 + lax.rem(links.parity + mask[1] // 2, 2)
    return rows_at(chip * 2 + lax.rem(links.row + other, 2), tok)


class Spread:
    def __init__(self, links, whole, wide, tok):
        self.links, self.whole, self.wide, self.tok = links, whole, wide, tok
        self.masks = chip_masks(wide)

    def place(self, mask):
        return self.whole.at[block_rows(self.links, mask, self.wide, self.tok), :]

    def own(self):
        return block_rows(self.links, (0, 0), self.wide, self.tok)

    def start(self):
        here = self.place((0, 0))
        self.far = [self.links.copy(here, here, *mask) for mask in self.masks[1:]]
        self.near = [self.links.copy(here, here, 1, 0)]

    def forward(self):
        for mask, move in zip(self.masks[1:], self.far):
            move.wait_recv()
            there = self.place(mask)
            self.near.append(self.links.copy(there, there, 1, 0))

    def wait(self):
        for move in self.near:
            move.wait_recv()

    def by_chip(self, compute):
        for k, mask in enumerate(self.masks):
            if k:
                self.far[k - 1].wait_recv()
                there = self.place(mask)
                self.near.append(self.links.copy(there, there, 1, 0))
            self.near[k].wait_recv()
            compute(chip_rows(self.links, mask, self.wide, self.tok))

    def finish(self):
        self.links.finish(self.far + self.near)


class Collect:
    def __init__(self, links, parts, from_core, from_far, wide, tok):
        self.links, self.parts, self.wide, self.tok = links, parts, wide, tok
        self.from_core, self.from_far = from_core, from_far
        self.masks = chip_masks(wide)
        self.near, self.far = {}, {}

    def block(self, mask, other=0):
        return self.parts.at[block_rows(self.links, mask, self.wide, self.tok, other), :]

    def slot(self, ref, k):
        return ref.at[part_of(k, self.tok), :]

    def forward(self, k):
        self.near[k].wait_recv()
        mine = self.block(self.masks[k])
        mine[...] = (mine[...].astype(F32) + self.slot(self.from_core, k)[...].astype(F32)).astype(BF)
        self.far[k] = self.links.copy(mine, self.slot(self.from_far, k - 1), *self.masks[k])

    def run(self, compute):
        last = len(self.masks) - 1
        for k in range(last, -1, -1):
            compute(chip_rows(self.links, self.masks[k], self.wide, self.tok))
            self.near[k] = self.links.copy(self.block(self.masks[k], 1), self.slot(self.from_core, k), 1, 0)
            if k < last:
                self.forward(k + 1)

    def result(self):
        self.near[0].wait_recv()
        total = self.block((0, 0))[...].astype(F32) + self.slot(self.from_core, 0)[...].astype(F32)
        for k in range(1, len(self.masks)):
            self.far[k].wait_recv()
            total = total + self.slot(self.from_far, k - 1)[...].astype(F32)
        return total

    def finish(self):
        self.links.finish(list(self.near.values()) + list(self.far.values()))


def normed_block(values, gain):
    inverse = lax.rsqrt(jnp.mean(values * values, axis=-1, keepdims=True) + EPSILON)
    return (values * inverse * gain).astype(BF)


def norm_back(values, gain, grad_normed):
    inverse = lax.rsqrt(jnp.mean(values * values, axis=-1, keepdims=True) + EPSILON)
    scaled = grad_normed * gain
    gain_grad = jnp.sum(grad_normed * values * inverse, axis=0, keepdims=True)
    inner_sum = jnp.mean(scaled * values, axis=-1, keepdims=True)
    return inverse * scaled - values * inverse * inverse * inverse * inner_sum, gain_grad


def silu(values):
    return values * jax.nn.sigmoid(values)


def columns_loop(columns, tile, step):
    @pl.loop(0, columns // tile)
    def _(index):
        step(rows_at(index, tile))


def to_heads(links, src, dst, tok):
    wide = dst.shape[1]

    def block(seq):
        return src.at[rows_at(lax.div(seq, 2), tok), rows_at(lax.rem(seq, 2), wide)]

    here = dst.at[rows_at(links.seq, tok), :]
    moves = [links.copy(block(flipped(links.seq, mask)), here, 0, mask) for mask in range(1, 8)]
    return moves, links.local(block(links.seq), here)


def from_heads(links, src, dst, tok):
    wide = src.shape[1]
    here = dst.at[rows_at(links.z, tok), rows_at(links.y, wide)]
    moves = [links.copy(src.at[rows_at(flipped(links.seq, mask), tok), :], here, 0, mask) for mask in range(1, 8)]
    return moves, links.local(src.at[rows_at(links.seq, tok), :], here)


def to_columns(links, src, dst, tok, cols):
    here = dst.at[rows_at(links.row, tok), :]
    moves = [links.copy(src.at[:, rows_at(flipped(links.row, mask), cols)], here, mask, 0) for mask in (1, 2, 3)]
    return moves, links.local(src.at[:, rows_at(links.row, cols)], here)


def from_columns(links, src, dst, tok, cols):
    here = dst.at[:, rows_at(links.row, cols)]
    moves = [links.copy(src.at[rows_at(flipped(links.row, mask), tok), :], here, mask, 0) for mask in (1, 2, 3)]
    return moves, links.local(src.at[rows_at(links.row, tok), :], here)


def tile_mask(docs_col, docs_row, start, tile):
    keys = start + tile
    q_pos = lax.broadcasted_iota(jnp.int32, (tile, keys), 0) + start
    k_pos = lax.broadcasted_iota(jnp.int32, (tile, keys), 1)
    return (k_pos <= q_pos) & (docs_col[pl.ds(start, tile), :] == docs_row[:, pl.ds(0, keys)])


def softmax_tile(q, k, docs_col, docs_row, start, tile):
    scores = dot_right_t(q, k) * (HEAD_DIM ** (-0.5))
    scores = jnp.where(tile_mask(docs_col, docs_row, start, tile), scores, MASKED)
    expo = jnp.exp(scores - jnp.max(scores, axis=1, keepdims=True))
    return expo * (1.0 / jnp.sum(expo, axis=1, keepdims=True))


def attend(q_ref, k_ref, v_ref, docs_col, docs_row, out_ref):
    length = q_ref.shape[0]
    tile = min(256, length)

    @pl.loop(0, q_ref.shape[1] // HEAD_DIM)
    def _(head):
        lanes = rows_at(head, HEAD_DIM)
        for start in range(0, length, tile):
            keys, here = pl.ds(0, start + tile), pl.ds(start, tile)
            probs = softmax_tile(q_ref[here, lanes], k_ref[keys, lanes], docs_col, docs_row, start, tile)
            out_ref[here, lanes] = dot_plain(probs.astype(BF), v_ref[keys, lanes]).astype(BF)


def attend_back(q_ref, k_ref, v_ref, dout_ref, docs_col, docs_row, dq_ref, dk_ref, dv_ref, dk_acc, dv_acc):
    length = q_ref.shape[0]
    tile = min(256, length)
    scale = HEAD_DIM ** (-0.5)

    @pl.loop(0, q_ref.shape[1] // HEAD_DIM)
    def _(head):
        lanes = rows_at(head, HEAD_DIM)
        for start in reversed(range(0, length, tile)):
            keys, here = pl.ds(0, start + tile), pl.ds(start, tile)
            q, k, dout = q_ref[here, lanes], k_ref[keys, lanes], dout_ref[here, lanes]
            probs = softmax_tile(q, k, docs_col, docs_row, start, tile)
            dprob = dot_right_t(dout, v_ref[keys, lanes])
            delta = jnp.sum(probs * dprob, axis=1, keepdims=True)
            dscores = (probs * (dprob - delta)).astype(BF)
            dq_ref[here, lanes] = (dot_plain(dscores, k) * scale).astype(BF)
            dk, dv = dot_left_t(dscores, q), dot_left_t(probs.astype(BF), dout)
            if start + tile == length:
                dk_acc[...] = dk
                dv_acc[...] = dv
            else:
                dk_acc[keys, :] += dk
                dv_acc[keys, :] += dv
        dk_ref[:, lanes] = (dk_acc[...] * scale).astype(BF)
        dv_ref[:, lanes] = dv_acc[...].astype(BF)


def hidden_rows(r, rows_in, rows):
    def step(at):
        gate_val = dot_plain(rows_in[rows, :], r.gate_v[:, at])
        up_val = dot_plain(rows_in[rows, :], r.up_v[:, at])
        r.gate[rows, at] = gate_val.astype(BF)
        r.up[rows, at] = up_val.astype(BF)
        r.hidden[rows, at] = (silu(gate_val) * up_val).astype(BF)

    columns_loop(r.gate.shape[1], 256, step)


def hidden_back(r, rows):
    def step(at):
        dhid = dot_right_t(r.cot[rows, :], r.down_v[at, :])
        gate_val, up_val = r.gate[rows, at].astype(F32), r.up[rows, at].astype(F32)
        sigmoid = jax.nn.sigmoid(gate_val)
        r.gate[rows, at] = (dhid * up_val * (sigmoid * (1.0 + gate_val * (1.0 - sigmoid)))).astype(BF)
        r.up[rows, at] = (dhid * (gate_val * sigmoid)).astype(BF)

    columns_loop(r.gate.shape[1], 512, step)


def plain_rows(left, right, out):
    def compute(rows):
        def step(at):
            out[rows, at] = dot_plain(left[rows, :], right[:, at]).astype(BF)

        columns_loop(right.shape[1], 1024, step)

    return compute


def turned_rows(pairs, out):
    def compute(rows):
        def step(at):
            value = dot_right_t(pairs[0][0][rows, :], pairs[0][1][at, :])
            for left, right in pairs[1:]:
                value = value + dot_right_t(left[rows, :], right[at, :])
            out[rows, at] = value.astype(BF)

        columns_loop(pairs[0][1].shape[0], 512, step)

    return compute


def run_kernel(kernel, ident, moves, large, small, outs, scratch):
    anywhere = pl.BlockSpec(memory_space=pl.ANY)
    whole = pl.BlockSpec(memory_space=pltpu.VMEM)
    names = [*large, *small, *outs, *scratch]

    def body(*refs):
        kernel(Links(*refs[-2:]), SimpleNamespace(**dict(zip(names, refs[:-2], strict=True))))

    results = pl.pallas_call(
        body,
        out_shape=[jax.ShapeDtypeStruct(*item) for item in outs.values()],
        in_specs=[anywhere] * len(large) + [whole] * len(small),
        out_specs=[anywhere] * len(outs),
        scratch_shapes=[pltpu.VMEM(*item) for item in scratch.values()] + [pltpu.SemaphoreType.DMA((moves,))] * 2,
        compiler_params=pltpu.CompilerParams(
            collective_id=ident, has_side_effects=True, vmem_limit_bytes=VMEM_LIMIT
        ),
    )(*large.values(), *small.values())
    return SimpleNamespace(**dict(zip(outs, results, strict=True)))


def typed(kind, **shapes):
    return {name: (dims, kind) for name, dims in shapes.items()}


ALL_MASKS = [(1, 0), (2, 0), (3, 0), (0, 2), (2, 2)] + [(0, mask) for mask in (1, 3, 4, 5, 6, 7)]


def forward_kernel(links, r):
    links.greet(ALL_MASKS)
    row = links.row
    tok, width = r.x.shape
    cols = r.gmu_gate.shape[1]
    part = r.part
    outs = []

    def keep(ref, out):
        outs.append(links.local(ref, out))

    gmu_in, gmu_to = Gather(links, r.gmu_gate, r.gmu_gate_w, False, 1), Gather(links, r.gmu_out, r.gmu_out_w, True, 1)
    weights_g = [gmu_in, gmu_to]
    weights_1 = [
        Gather(links, r.f1_gate, r.f1_gate_w, False, 2),
        Gather(links, r.f1_up, r.f1_up_w, False, 2),
        Gather(links, r.f1_down, r.f1_down_w, True, 2),
    ]
    weights_q = [Gather(links, r.query, r.query_w, False, 1), Gather(links, r.attn_out, r.attn_out_w, True, 1)]
    weights_2 = [
        Gather(links, r.f2_gate, r.f2_gate_w, False, 2),
        Gather(links, r.f2_up, r.f2_up_w, False, 2),
        Gather(links, r.f2_down, r.f2_down_w, True, 2),
    ]
    gate_2, up_2, down_2 = weights_2

    each(weights_g, Gather.over_z, 2, 1)
    for weight in weights_g:
        weight.own()

    spread_a = Spread(links, r.rows_a, False, tok)
    r.rows_a[spread_a.own(), :] = normed_block(r.x[...].astype(F32), r.gain_a[...])
    spread_a.start()
    spread_y = Spread(links, r.cot_rows, True, tok)
    own_y = links.local(r.cotangent, r.cot_rows.at[spread_y.own(), :])
    k_cols = to_columns(links, r.keys, r.k_cols, tok, cols)
    v_cols = to_columns(links, r.values, r.v_cols, tok, cols)
    mem_moves = to_columns(links, r.memory, r.mem, tok, cols)
    spread_a.forward()
    landed(k_cols)
    landed(v_cols)
    k_moves = to_heads(links, r.k_cols, r.k_heads, tok)
    v_moves = to_heads(links, r.v_cols, r.v_heads, tok)
    each(weights_g, Gather.over_z, 3)
    own_y.wait()
    spread_y.start()
    each(weights_1, Gather.over_z, 2, 1, 3)
    each(weights_g, Gather.over_y, 2, 1, 3)
    for weight in weights_1 + weights_q + [gate_2]:
        weight.own()
    spread_a.wait()
    landed(mem_moves)
    keep(r.rows_a, r.rows_a_out)
    keep(r.mem, r.mem_out)
    spread_y.forward()
    gmu_in.arrived()
    load_in = links.local(r.gmu_gate_w, r.in_v)
    gmu_to.arrived()
    load_out = links.local(r.gmu_out_w, r.out_v)
    load_in.wait()

    def gmu_step(at):
        value = dot_plain(r.rows_a[...], r.in_v[:, at])
        r.pre[:, at] = value.astype(BF)
        r.act[:, at] = (r.mem[:, at].astype(F32) * silu(value)).astype(BF)

    columns_loop(cols, 256, gmu_step)
    load_out.wait()
    collect_a = Collect(links, part, r.core_a, r.far_a, False, tok)
    collect_a.run(plain_rows(r.act, r.out_v, part))
    keep(r.pre, r.pre_out)
    keep(r.act, r.act_out)
    r.x_one[...] = r.x[...].astype(F32) + collect_a.result()
    keep(r.x_one, r.x_one_out)

    spread_b = Spread(links, r.rows_b, True, tok)
    r.rows_b[spread_b.own(), :] = normed_block(r.x_one[...], r.gain_b[...])
    spread_b.start()
    each(weights_q, Gather.over_z, 2, 1)
    each(weights_1, Gather.over_y, 2, 1, 3)
    spread_b.forward()
    spread_b.wait()
    keep(r.rows_b, r.rows_b_out)
    each(weights_q, Gather.over_z, 3)
    gate_2.over_z(2, 1, 3)
    each(weights_q, Gather.over_y, 2, 1)
    loads = []
    for weight, place in zip(weights_1, (r.gate_v, r.up_v, r.down_v)):
        weight.arrived()
        loads.append(links.local(weight.whole, place))
    collect_a.finish()
    wait(loads)
    hidden_rows(r, r.rows_b, pl.ds(0, 8 * tok))
    spread_a.finish()
    outs[0].wait()
    del outs[0]
    collect_b = Collect(links, part, r.core_b, r.far_b, True, tok)
    collect_b.run(plain_rows(r.hidden, r.down_v, part))
    up_2.over_z(2, 1, 3)
    each(weights_q, Gather.over_y, 3)
    gate_2.over_y(2, 1, 3)
    landed(k_moves)
    landed(v_moves)
    keep(r.k_heads, r.k_heads_out)
    keep(r.v_heads, r.v_heads_out)
    keep(r.gate, r.gate_out)
    keep(r.up, r.up_out)
    keep(r.hidden, r.hidden_out)
    r.x_two[...] = r.x_one[...] + collect_b.result()
    keep(r.x_two, r.x_two_out)

    spread_c = Spread(links, r.rows_a, False, tok)
    r.rows_a[spread_c.own(), :] = normed_block(r.x_two[...], r.gain_c[...])
    spread_c.start()
    loads = []
    for weight, place in zip(weights_q, (r.in_v, r.out_v)):
        weight.arrived()
        loads.append(links.local(weight.whole, place))
    spread_c.forward()
    wait(loads)
    spread_c.wait()
    keep(r.rows_a, r.rows_c_out)

    def query_step(at):
        r.q_cols[:, at] = dot_plain(r.rows_a[...], r.in_v[:, at]).astype(BF)

    columns_loop(cols, 512, query_step)
    q_moves = to_heads(links, r.q_cols, r.q_heads, tok)
    up_2.own()
    up_2.over_y(2, 1)
    landed(q_moves)
    keep(r.q_heads, r.q_heads_out)
    attend(r.q_heads, r.k_heads, r.v_heads, r.docs_col, r.docs_row, r.out_heads)
    spread_b.finish()
    wait(outs)
    outs.clear()
    out_moves = from_heads(links, r.out_heads, r.attended, tok)
    down_2.over_z(2, 1, 3)
    up_2.over_y(3)
    down_2.own()
    landed(out_moves)
    keep(r.attended, r.attended_out)
    collect_b.finish()
    collect_c = Collect(links, part, r.core_c, r.far_c, False, tok)
    collect_c.run(plain_rows(r.attended, r.out_v, part))
    down_2.over_y(2, 1)
    r.x_three[...] = r.x_two[...] + collect_c.result()
    keep(r.x_three, r.x_three_out)
    spread_d = Spread(links, r.rows_b, True, tok)
    r.rows_b[spread_d.own(), :] = normed_block(r.x_three[...], r.gain_d[...])
    spread_d.start()
    spread_d.forward()
    down_2.over_y(3)
    spread_d.wait()
    keep(r.rows_b, r.rows_d_out)
    for weight in weights_2:
        weight.arrived()
    spread_y.wait()
    wait(outs)
    links.finish()


def forward_pass(large, small):
    tok, width = small["x"].shape
    cols = large["gmu_gate"].shape[1]
    half = large["f1_gate"].shape[1] // 2
    tokens = 4 * tok
    positions = small["docs_col"].shape[0]
    heads = (positions, cols * tokens // positions)
    inner, outer = (width, half), (half, width)
    outs = typed(
        BF,
        gmu_gate_w=(width, cols),
        gmu_out_w=(cols, width),
        f1_gate_w=inner,
        f1_up_w=inner,
        f1_down_w=outer,
        query_w=(width, cols),
        attn_out_w=(cols, width),
        f2_gate_w=inner,
        f2_up_w=inner,
        f2_down_w=outer,
        rows_a_out=(tokens, width),
        mem_out=(tokens, cols),
        pre_out=(tokens, cols),
        act_out=(tokens, cols),
        rows_b_out=(2 * tokens, width),
        gate_out=(2 * tokens, half),
        up_out=(2 * tokens, half),
        hidden_out=(2 * tokens, half),
        rows_c_out=(tokens, width),
        q_heads_out=heads,
        k_heads_out=heads,
        v_heads_out=heads,
        attended_out=(tokens, cols),
        rows_d_out=(2 * tokens, width),
        cot_rows=(2 * tokens, width),
    ) | typed(F32, x_one_out=(tok, width), x_two_out=(tok, width), x_three_out=(tok, width))
    scratch = typed(
        BF,
        rows_a=(tokens, width),
        mem=(tokens, cols),
        k_cols=(tokens, cols),
        v_cols=(tokens, cols),
        in_v=(width, cols),
        out_v=(cols, width),
        pre=(tokens, cols),
        act=(tokens, cols),
        part=(2 * tokens, width),
        core_a=(2 * tok, width),
        far_a=(tok, width),
        core_b=(4 * tok, width),
        far_b=(3 * tok, width),
        core_c=(2 * tok, width),
        far_c=(tok, width),
        rows_b=(2 * tokens, width),
        gate_v=inner,
        up_v=inner,
        down_v=outer,
        gate=(2 * tokens, half),
        up=(2 * tokens, half),
        hidden=(2 * tokens, half),
        q_cols=(tokens, cols),
        q_heads=heads,
        k_heads=heads,
        v_heads=heads,
        out_heads=heads,
        attended=(tokens, cols),
    ) | typed(F32, x_one=(tok, width), x_two=(tok, width), x_three=(tok, width))
    return run_kernel(forward_kernel, 0, 256, large, small, outs, scratch)


def weight_blocks(links, order, pairs, stages, blocks):
    size = stages[0].shape[0]
    depth = size // len(pairs)
    moves = [None, None]
    for count, block in enumerate(order):
        stage, kind = stages[count % 2], count % 2
        if moves[kind] is not None:
            moves[kind].wait()
        at = rows_at(block, depth)
        for k, (left, right) in enumerate(pairs):
            stage[part_of(k, depth), :] = dot_left_t(left[:, at], right[...]).astype(BF)
        moves[kind] = links.local(stage, blocks.at[rows_at(block, size), :])
    for move in moves:
        if move is not None:
            move.wait()


class Scatter:
    def __init__(self, links, blocks, land_y, land_z, here, there, total, turned, parts, *outs):
        self.links, self.blocks, self.land_y, self.land_z = links, blocks, land_y, land_z
        self.here, self.there, self.total, self.turned, self.parts, self.outs = here, there, total, turned, parts, outs
        self.size = blocks.shape[0] // 8
        self.y_moves, self.z_moves = {}, {}

    def slot(self, ref, k):
        return ref.at[part_of(k, self.size), :]

    def block(self, step, y):
        return self.blocks.at[rows_at(2 * flipped(self.links.z, step) + y, self.size), :]

    def over_y(self, *steps):
        for step in steps:
            self.y_moves[step] = self.links.copy(
                self.block(step, 1 - self.links.y), self.slot(self.land_y, step), 0, 1
            )

    def over_z(self, *steps):
        for step in steps:
            first = self.links.local(self.block(step, self.links.y), self.here)
            self.y_moves[step].wait_recv()
            mine = self.slot(self.land_y, step)
            second = self.links.local(mine, self.there)
            first.wait()
            second.wait()
            total = self.here[...].astype(F32) + self.there[...].astype(F32)
            mask = 2 * step
            if self.parts == 1 and step == 2:
                self.z_moves[3].wait_recv()
                self.links.local(self.slot(self.land_z, 2), self.there).wait()
                total = total + self.there[...].astype(F32)
            elif self.parts == 1 and step == 3:
                mask = 2
            self.here[...] = total.astype(BF)
            self.links.local(self.here, mine).wait()
            self.z_moves[step] = self.links.copy(mine, self.slot(self.land_z, step - 1), 0, mask)

    def store(self, k, half):
        rows, width = self.total.shape
        if k < len(self.outs) - 1:
            self.links.local(self.total, self.outs[k].at[:, rows_at(half, width)]).wait()
        else:
            self.turned[...] = self.total[...].T
            self.links.local(self.turned, self.outs[k].at[rows_at(half, width), :]).wait()

    def spots(self):
        rows = self.total.shape[0]
        return [ref.at[part_of(n, rows), :] for ref in (self.here, self.there) for n in range(2)]

    def add(self, sources, half):
        rows, spots = self.total.shape[0], self.spots()
        for k in range(len(self.outs)):
            wait([self.links.local(source.at[part_of(k, rows), :], spot) for source, spot in zip(sources, spots)])
            total = spots[0][...].astype(F32)
            for spot in spots[1 : len(sources)]:
                total = total + spot[...].astype(F32)
            self.total[...] = total
            self.store(k, half)

    def finish_other(self):
        for step in (1, 3):
            self.z_moves[step].wait_recv()
        self.add([self.slot(self.land_z, 0), self.slot(self.land_z, 2)], 1 - self.links.parity)

    def finish(self):
        self.y_moves[0].wait_recv()
        self.z_moves[2].wait_recv()
        sources = [self.block(0, self.links.y), self.slot(self.land_y, 0), self.slot(self.land_z, 1)]
        if self.parts == 1:
            self.z_moves[1].wait_recv()
            self.add([*sources, self.slot(self.land_z, 0)], 0)
        else:
            self.add(sources, self.links.parity)


def backward_kernel(links, r):
    links.greet(ALL_MASKS)
    row, seq, y = links.row, links.seq, links.y
    tok, width = r.grad.shape
    cols = r.left.shape[1]
    half = r.gate.shape[1]
    part, grad = r.part, r.grad
    everything = pl.ds(0, 8 * tok)
    outs = []
    stages = [r.stage_0, r.stage_1]
    depth = r.total.shape[0]
    small_stages = [ref.at[part_of(0, 2 * depth), part_of(0, cols)] for ref in stages]
    totals = [r.total, r.turned]
    small_totals = [r.total.at[:, part_of(0, cols)], r.turned.at[part_of(0, cols), :]]
    far_y = [2 * z + 1 - y for z in range(4)]
    own_y = [2 * z + y for z in range(4)]

    loads = [
        links.local(r.rows_d, r.rows),
        links.local(r.f2_gate_w, r.gate_v),
        links.local(r.f2_up_w, r.up_v),
        links.local(r.f2_down_w, r.down_v),
        links.local(r.cot_rows, r.cot),
        links.local(r.x_three, r.values),
    ]
    wait(loads[:3])
    hidden_rows(r, r.rows, everything)
    wait(loads[3:])
    for k in range(2):
        hidden_back(r, part_of(k, 4 * tok))
    pairs = [(r.rows, r.gate), (r.rows, r.up), (r.cot, r.hidden)]
    collect_d = Collect(links, part, r.core_b, r.far_b, True, tok)
    collect_d.run(turned_rows([(r.gate, r.gate_v), (r.up, r.up_v)], part))
    weight_blocks(links, far_y, pairs, stages, r.blocks_2)
    stream_2 = Scatter(links, r.blocks_2, r.land_y_2, r.land_z_2, *stages, *totals, 2, r.f2_gate_g, r.f2_up_g, r.f2_down_g)
    stream_2.over_y(2)
    dx, gain_grad = norm_back(r.values[...], r.gain_d[...], collect_d.result())
    r.gains[pl.ds(3, 1), :] = gain_grad
    grad[...] = r.cotangent[...].astype(F32) + dx

    spread_a = Spread(links, r.cot_a, False, tok)
    r.cot_a[spread_a.own(), :] = grad[...].astype(BF)
    spread_a.start()
    weight_blocks(links, own_y, pairs, stages, r.blocks_2)
    in_v = r.gate_v.at[:, pl.ds(0, cols)]
    heads = r.q_heads.shape[1]
    q_v, k_v, v_v = (r.gate.at[:, part_of(k, heads)] for k in range(3))
    dout_v = r.dout_v
    dq_v, dk_v, dv_v = (r.up.at[:, part_of(k, heads)] for k in range(3))
    loads = [
        links.local(r.attn_out_w, r.out_w),
        links.local(r.query_w, in_v),
        links.local(r.attended, r.left),
        links.local(r.q_heads, q_v),
        links.local(r.k_heads, k_v),
        links.local(r.v_heads, v_v),
    ]
    spread_a.forward()
    for k in range(4):
        plain_rows(r.hidden, r.down_v, r.rows)(part_of(k, 2 * tok))
    collect_d.finish()
    wait(loads)
    spread_a.wait()

    def back_step(at):
        r.dcols[:, at] = dot_right_t(r.cot_a[...], r.out_w[at, :]).astype(BF)

    columns_loop(cols, 512, back_step)
    dout_moves = to_heads(links, r.dcols, dout_v, tok)
    landed(dout_moves)
    attend_back(
        q_v, k_v, v_v, dout_v, r.docs_col, r.docs_row, dq_v, dk_v, dv_v, r.dk_acc, r.dv_acc
    )
    dq_moves = from_heads(links, dq_v, r.dq_cols, tok)
    dk_moves = from_heads(links, dk_v, r.k_cols, tok)
    dv_moves = from_heads(links, dv_v, r.v_cols, tok)
    stream_2.over_y(3, 1, 0)
    rows_c = part.at[pl.ds(4 * tok, 4 * tok), :]
    load = links.local(r.rows_c, rows_c)
    collect_m = Collect(links, r.rows, r.core_m, r.far_m, True, tok)
    collect_m.run(lambda rows: None)
    stream_2.over_z(2)
    load.wait()
    landed(dq_moves)
    collect_c = Collect(links, part, r.core_c, r.far_c, False, tok)
    collect_c.run(turned_rows([(r.dq_cols, in_v)], part))
    weight_blocks(links, range(8), [(rows_c, r.dq_cols), (r.cot_a, r.left)], small_stages, r.blocks_q)
    stream_q = Scatter(links, r.blocks_q, r.land_y_q, r.land_z_q, *small_stages, *small_totals, 1, r.query_g, r.attn_out_g)
    stream_q.over_y(3, 1, 2, 0)
    r.values[...] = r.values[...] + collect_m.result()
    links.local(r.values, r.mixed).wait()
    links.local(r.x_two, r.values).wait()
    dx, gain_grad = norm_back(r.values[...], r.gain_c[...], collect_c.result())
    r.gains[pl.ds(2, 1), :] = gain_grad
    grad[...] = grad[...] + dx

    spread_b = Spread(links, r.cot, True, tok)
    r.cot[spread_b.own(), :] = grad[...].astype(BF)
    spread_b.start()
    landed(dk_moves)
    landed(dv_moves)
    links.finish(dout_moves[0] + dq_moves[0] + dk_moves[0] + dv_moves[0])
    collect_m.finish()
    loads = [
        links.local(r.f1_down_w, r.down_v),
        links.local(r.gate_1, r.gate),
        links.local(r.up_1, r.up),
        links.local(r.f1_gate_w, r.gate_v),
        links.local(r.f1_up_w, r.up_v),
        links.local(r.hidden_1, r.hidden),
        links.local(r.rows_b, r.rows),
        links.local(r.x_one, r.values),
    ]
    home = [
        from_columns(links, r.k_cols, r.key_land, tok, cols),
        from_columns(links, r.v_cols, r.value_land, tok, cols),
    ]
    stream_2.over_z(3)
    wait(loads)
    spread_b.by_chip(lambda rows: hidden_back(r, rows))
    collect_c.finish()
    spread_a.finish()
    collect_b = Collect(links, part, r.core_b, r.far_b, True, tok)
    collect_b.run(turned_rows([(r.gate, r.gate_v), (r.up, r.up_v)], part))
    weight_blocks(links, far_y, pairs, stages, r.blocks_1)
    stream_1 = Scatter(links, r.blocks_1, r.land_y_1, r.land_z_1, *stages, *totals, 2, r.f1_gate_g, r.f1_up_g, r.f1_down_g)
    stream_1.over_y(2, 1, 3)
    weight_blocks(links, own_y, pairs, stages, r.blocks_1)
    stream_2.over_z(1)
    dx, gain_grad = norm_back(r.values[...], r.gain_b[...], collect_b.result())
    r.gains[pl.ds(1, 1), :] = gain_grad
    grad[...] = grad[...] + dx

    spread_g = Spread(links, r.cot_a, False, tok)
    r.cot_a[spread_g.own(), :] = grad[...].astype(BF)
    spread_g.start()
    spread_b.finish()
    collect_b.finish()
    rows_a = part.at[pl.ds(4 * tok, 4 * tok), :]
    loads = [
        links.local(r.gmu_out_w, r.out_w),
        links.local(r.gmu_gate_w, in_v),
        links.local(r.pre, r.dcols),
        links.local(r.mem, r.dq_cols),
        links.local(r.act, r.left),
        links.local(r.rows_a, rows_a),
    ]
    spread_g.forward()
    stream_q.over_z(3, 1)
    stream_1.over_z(2)
    wait(loads)
    spread_g.wait()

    def gmu_back(at):
        dact = dot_right_t(r.cot_a[...], r.out_w[at, :])
        pre, mem = r.dcols[:, at].astype(F32), r.dq_cols[:, at].astype(F32)
        sigmoid = jax.nn.sigmoid(pre)
        r.dcols[:, at] = (dact * (pre * sigmoid)).astype(BF)
        r.dq_cols[:, at] = (dact * mem * (sigmoid * (1.0 + pre * (1.0 - sigmoid)))).astype(BF)

    columns_loop(cols, 256, gmu_back)
    collect_g = Collect(links, part, r.core_c, r.far_c, False, tok)
    collect_g.run(turned_rows([(r.dq_cols, in_v)], part))
    home.append(from_columns(links, r.dcols, r.mem_land, tok, cols))
    weight_blocks(links, range(8), [(rows_a, r.dq_cols), (r.cot_a, r.left)], small_stages, r.blocks_g)
    stream_g = Scatter(links, r.blocks_g, r.land_y_g, r.land_z_g, *small_stages, *small_totals, 1, r.gmu_gate_g, r.gmu_out_g)
    stream_g.over_y(3, 1, 2, 0)
    stream_1.over_y(0)
    stream_q.over_z(2)
    stream_1.over_z(1)
    dx, gain_grad = norm_back(r.x[...].astype(F32), r.gain_a[...], collect_g.result())
    grad[...] = grad[...] + dx
    outs.append(links.local(grad, r.input_grad))

    r.gains[pl.ds(0, 1), :] = gain_grad
    r.row_sums[row] = r.gains[...]
    for move in [links.copy(r.gains, r.row_sums.at[row], mask, 0) for mask in (1, 2, 3)]:
        move.wait_recv()
    r.seq_sums[seq] = r.row_sums[0] + r.row_sums[1] + r.row_sums[2] + r.row_sums[3]
    gain_moves = [links.copy(r.seq_sums.at[seq], r.seq_sums.at[seq], 0, mask) for mask in range(1, 8)]
    wide_grads = ((r.key_land, r.key_grad), (r.value_land, r.value_grad), (r.mem_land, r.mem_grad))
    for moves, (land, out) in zip(home, wide_grads):
        landed(moves)
        links.local(land, r.rows.at[pl.ds(0, tok), :]).wait()
        r.values[...] = r.rows[pl.ds(0, tok), :].astype(F32)
        links.local(r.values, out).wait()

    stream_1.over_z(3)
    stream_2.finish()
    stream_2.finish_other()
    stream_g.over_z(3, 1)
    stream_q.finish()
    for move in gain_moves:
        move.wait_recv()
    total = r.seq_sums[0]
    for k in range(1, 8):
        total = total + r.seq_sums[k]
    r.gain_total[...] = total
    outs.append(links.local(r.gain_total, r.gain_grads))
    stream_g.over_z(2)
    stream_1.finish_other()
    stream_1.finish()
    stream_g.finish()
    wait(outs)
    links.finish()


def backward_pass(large, small):
    tok, width = small["x"].shape
    tokens, cols = large["mem"].shape
    wide, half = large["gate_1"].shape
    depth = width // 8
    ffn, unit = (3 * depth, half), (2 * depth, cols)

    def times(count, shape):
        return (count * shape[0], shape[1])

    outs = typed(
        F32,
        mixed=(tok, width),
        input_grad=(tok, width),
        key_grad=(tok, width),
        value_grad=(tok, width),
        mem_grad=(tok, width),
        gain_grads=(4, width),
        f2_gate_g=(depth, 2 * half),
        f2_up_g=(depth, 2 * half),
        f2_down_g=(2 * half, depth),
        f1_gate_g=(depth, 2 * half),
        f1_up_g=(depth, 2 * half),
        f1_down_g=(2 * half, depth),
        query_g=(depth, cols),
        attn_out_g=(cols, depth),
        gmu_gate_g=(depth, cols),
        gmu_out_g=(cols, depth),
    ) | typed(
        BF,
        key_land=(tok, width),
        value_land=(tok, width),
        mem_land=(tok, width),
        blocks_2=times(8, ffn),
        blocks_1=times(8, ffn),
        blocks_q=times(8, unit),
        blocks_g=times(8, unit),
        land_y_2=times(4, ffn),
        land_y_1=times(4, ffn),
        land_y_q=times(4, unit),
        land_y_g=times(4, unit),
        land_z_2=times(3, ffn),
        land_z_1=times(3, ffn),
        land_z_q=times(3, unit),
        land_z_g=times(3, unit),
    )
    scratch = typed(
        BF,
        rows=(wide, width),
        cot=(wide, width),
        cot_a=(tokens, width),
        gate_v=(width, half),
        up_v=(width, half),
        down_v=(half, width),
        out_w=(cols, width),
        gate=(wide, half),
        up=(wide, half),
        hidden=(wide, half),
        part=(wide, width),
        left=(tokens, cols),
        dcols=(tokens, cols),
        dq_cols=(tokens, cols),
        k_cols=(tokens, cols),
        v_cols=(tokens, cols),
        dout_v=(small["docs_col"].shape[0], cols // 2),
        core_b=(4 * tok, width),
        far_b=(3 * tok, width),
        core_m=(4 * tok, width),
        far_m=(3 * tok, width),
        core_c=(2 * tok, width),
        far_c=(tok, width),
        stage_0=ffn,
        stage_1=ffn,
    ) | typed(
        F32,
        values=(tok, width),
        grad=(tok, width),
        dk_acc=(small["docs_col"].shape[0], HEAD_DIM),
        dv_acc=(small["docs_col"].shape[0], HEAD_DIM),
        total=(depth, half),
        turned=(half, depth),
        gains=(4, width),
        gain_total=(4, width),
        row_sums=(4, 4, width),
        seq_sums=(8, 4, width),
    )
    return run_kernel(backward_kernel, 1, 384, large, small, outs, scratch)


def body_general(
    block_input,
    memory,
    key_cache,
    value_cache,
    doc_lengths,
    gmu_gate,
    gmu_out,
    ffn1_gate,
    ffn1_up,
    ffn1_down,
    query_weight,
    attn_out,
    ffn2_gate,
    ffn2_up,
    ffn2_down,
    gain_a,
    gain_b,
    gain_c,
    gain_d,
    cotangent,
):
    seq_count = lax.axis_size("seq")
    row_count = lax.axis_size("row")
    seq_index = lax.axis_index("seq")
    tok_len = block_input.shape[1]
    width = block_input.shape[2]
    head_count = query_weight.shape[1] // HEAD_DIM
    depth = ffn1_gate.shape[0]
    half = ffn1_gate.shape[1] // 2
    z_count = seq_count // 2
    z_index, y_index = seq_index // 2, seq_index % 2
    parity = z_index % 2

    def spread(normed):
        return lax.all_gather(normed[None], "row", axis=0, tiled=True).reshape(
            row_count * tok_len, width
        )

    def collect(partial_value):
        return lax.psum_scatter(
            partial_value.reshape(row_count, tok_len, width).astype(BF),
            "row",
            scatter_dimension=0,
            tiled=True,
        ).astype(F32)[0]

    def spread_wide(normed):
        both = jnp.stack([normed, swapped(normed, "seq", 2)])
        return lax.all_gather(both[None], "row", axis=0, tiled=True).reshape(
            2 * row_count * tok_len, width
        )

    def collect_wide(partial_value):
        parts = partial_value.reshape(row_count, 2, tok_len, width).astype(BF)
        summed = lax.psum_scatter(parts, "row", scatter_dimension=0, tiled=True)[0]
        other = swapped(summed[1], "seq", 2)
        return summed[0].astype(F32) + other.astype(F32)

    def gather_ffn(gate, up, down):
        shard = jnp.stack([gate, up, down.T])
        whole = jnp.zeros((z_count, 2, 3, depth, half), BF)
        for step in range(z_count):
            want = (parity + step) % 2
            piece = lax.dynamic_slice_in_dim(shard, want * half, half, axis=2)
            if step:
                piece = swapped(piece, "seq", 2 * step)
            over = swapped(piece, "seq", 1)
            source = z_index ^ step
            whole = lax.dynamic_update_slice(whole, piece[None, None], (source, y_index, 0, 0, 0))
            whole = lax.dynamic_update_slice(whole, over[None, None], (source, 1 - y_index, 0, 0, 0))
        whole = whole.transpose(2, 0, 1, 3, 4).reshape(3, seq_count * depth, half)
        return whole[0], whole[1], whole[2]

    def scatter_ffn(gate_grad, up_grad, down_grad_t):
        whole = jnp.stack([gate_grad.astype(BF), up_grad.astype(BF), down_grad_t.astype(BF)])
        whole = whole.reshape(3, z_count, 2, depth, half)
        sums = [None, None]
        for step in range(z_count):
            target = z_index ^ step
            there = lax.dynamic_slice(
                whole, (0, target, 1 - y_index, 0, 0), (3, 1, 1, depth, half)
            )[:, 0, 0]
            here = lax.dynamic_slice(whole, (0, target, y_index, 0, 0), (3, 1, 1, depth, half))[:, 0, 0]
            total = here.astype(F32) + swapped(there, "seq", 1).astype(F32)
            if step:
                total = swapped(total.astype(BF), "seq", 2 * step).astype(F32)
            kind = step % 2
            sums[kind] = total if sums[kind] is None else sums[kind] + total
        pair = jnp.stack(sums)
        lower = lax.dynamic_index_in_dim(pair, parity, 0, keepdims=False)
        upper = lax.dynamic_index_in_dim(pair, 1 - parity, 0, keepdims=False)
        full = jnp.concatenate([lower, upper], axis=2)
        return full[0], full[1], full[2].T

    gmu_gate_full = lax.all_gather(gmu_gate, "seq", axis=0, tiled=True)
    gmu_out_full = lax.all_gather(gmu_out, "seq", axis=1, tiled=True)
    gate_one_w, up_one_w, down_one_t = gather_ffn(ffn1_gate, ffn1_up, ffn1_down)
    query_full = lax.all_gather(query_weight, "seq", axis=0, tiled=True)
    aout_full = lax.all_gather(attn_out, "seq", axis=1, tiled=True)
    gate_two_w, up_two_w, down_two_t = gather_ffn(ffn2_gate, ffn2_up, ffn2_down)

    def ffn_forward(rows_in, gate_weight, up_weight, down_weight_t):
        gate_val = dot_plain(rows_in, gate_weight)
        up_val = dot_plain(rows_in, up_weight)
        hidden = (jax.nn.silu(gate_val) * up_val).astype(BF)
        return (dot_right_t(hidden, down_weight_t), gate_val, up_val, hidden)

    def ffn_backward(cot_rows, rows_in, gate_val, up_val, hidden, gate_weight, up_weight, down_weight_t):
        dhid = dot_plain(cot_rows, down_weight_t)
        dgate = (dhid * up_val * silu_slope(gate_val)).astype(BF)
        dup = (dhid * jax.nn.silu(gate_val)).astype(BF)
        drows = dot_right_t(dgate, gate_weight) + dot_right_t(dup, up_weight)
        down_grad_t = dot_left_t(cot_rows, hidden)
        gate_grad = dot_left_t(rows_in, dgate)
        up_grad = dot_left_t(rows_in, dup)
        return (drows, gate_grad, up_grad, down_grad_t)

    mem_cols = lax.all_to_all(memory, "row", split_axis=2, concat_axis=0, tiled=True)
    mem_cols = mem_cols.reshape(row_count * tok_len, -1).astype(F32)
    kv_here = lax.all_to_all(
        jnp.concatenate([key_cache, value_cache], axis=0)[:, None], "row", split_axis=3, concat_axis=1, tiled=True
    )

    x_zero = block_input[0].astype(F32)
    normed_a, inv_a = rms_forward(x_zero, gain_a)
    rows_a = spread(normed_a.astype(BF))
    gmu_pre = dot_plain(rows_a, gmu_gate_full)
    gmu_act = (mem_cols * jax.nn.silu(gmu_pre)).astype(BF)
    x_one = x_zero + collect(dot_plain(gmu_act, gmu_out_full))
    normed_b, inv_b = rms_forward(x_one, gain_b)
    rows_b = spread_wide(normed_b.astype(BF))
    part_one, gate_one, up_one, hidden_one = ffn_forward(rows_b, gate_one_w, up_one_w, down_one_t)
    x_two = x_one + collect_wide(part_one)
    normed_c, inv_c = rms_forward(x_two, gain_c)
    rows_c = spread(normed_c.astype(BF))
    queries = dot_plain(rows_c, query_full).astype(BF)
    head_shape = (row_count, tok_len, head_count, HEAD_DIM)
    attended, ring_grad = ring_attention(
        queries.reshape(head_shape), kv_here.reshape((2,) + head_shape), doc_lengths, tok_len, head_count
    )

    def attention_grad(dout):
        return ring_grad(dout.reshape(head_shape))

    attended = attended.reshape(row_count * tok_len, head_count * HEAD_DIM)
    x_three = x_two + collect(dot_plain(attended, aout_full))
    normed_d, inv_d = rms_forward(x_three, gain_d)
    rows_d = spread_wide(normed_d.astype(BF))
    part_two, gate_two, up_two, hidden_two = ffn_forward(rows_d, gate_two_w, up_two_w, down_two_t)
    mixed = x_three + collect_wide(part_two)

    grad_y = cotangent[0].astype(F32)
    drows_d, gate_two_grad, up_two_grad, down_two_grad = ffn_backward(
        spread_wide(cotangent[0]), rows_d, gate_two, up_two, hidden_two, gate_two_w, up_two_w, down_two_t
    )
    dx_d, gain_d_grad = rms_backward(x_three, inv_d, gain_d, collect_wide(drows_d))
    grad_three = grad_y + dx_d
    cot_three = spread(grad_three.astype(BF))
    dattended = dot_right_t(cot_three, aout_full)
    aout_grad = dot_left_t(attended, cot_three)
    dqueries, kv_grad = attention_grad(dattended.astype(BF))
    dqueries = dqueries.reshape(row_count * tok_len, head_count * HEAD_DIM)
    query_grad = dot_left_t(rows_c, dqueries)
    dx_c, gain_c_grad = rms_backward(x_two, inv_c, gain_c, collect(dot_right_t(dqueries, query_full)))
    grad_two = grad_three + dx_c
    drows_b, gate_one_grad, up_one_grad, down_one_grad = ffn_backward(
        spread_wide(grad_two.astype(BF)), rows_b, gate_one, up_one, hidden_one, gate_one_w, up_one_w, down_one_t
    )
    dx_b, gain_b_grad = rms_backward(x_one, inv_b, gain_b, collect_wide(drows_b))
    grad_one = grad_two + dx_b
    cot_one = spread(grad_one.astype(BF))
    dact = dot_right_t(cot_one, gmu_out_full)
    gout_grad = dot_left_t(gmu_act, cot_one)
    mem_grad_cols = dact * jax.nn.silu(gmu_pre)
    dpre = (dact * mem_cols * silu_slope(gmu_pre)).astype(BF)
    gate_a_grad = dot_left_t(rows_a, dpre)
    dx_a, gain_a_grad = rms_backward(x_zero, inv_a, gain_a, collect(dot_right_t(dpre, gmu_gate_full)))
    input_grad = grad_one + dx_a

    mem_grad = lax.all_to_all(
        mem_grad_cols.reshape(row_count, tok_len, -1).astype(BF), "row", split_axis=0, concat_axis=2, tiled=True
    ).astype(F32)
    kv_home = lax.all_to_all(
        kv_grad.reshape(2, row_count, tok_len, -1), "row", split_axis=1, concat_axis=3, tiled=True
    ).astype(F32)

    def scatter(grad, dim):
        return lax.psum_scatter(grad.astype(BF), "seq", scatter_dimension=dim, tiled=True).astype(F32)

    gate_two_out, up_two_out, down_two_out = scatter_ffn(gate_two_grad, up_two_grad, down_two_grad)
    aout_out = scatter(aout_grad, 1)
    query_out = scatter(query_grad, 0)
    gate_one_out, up_one_out, down_one_out = scatter_ffn(gate_one_grad, up_one_grad, down_one_grad)
    gout_out = scatter(gout_grad, 1)
    gate_a_out = scatter(gate_a_grad, 0)
    gain_grads = lax.psum((gain_a_grad, gain_b_grad, gain_c_grad, gain_d_grad), ("seq", "row"))
    return (
        mixed[None],
        input_grad[None],
        mem_grad,
        kv_home[0],
        kv_home[1],
        gate_a_out,
        gout_out,
        gate_one_out,
        up_one_out,
        down_one_out,
        query_out,
        aout_out,
        gate_two_out,
        up_two_out,
        down_two_out,
        gain_grads[0],
        gain_grads[1],
        gain_grads[2],
        gain_grads[3],
    )


def body_fast(
    block_input,
    memory,
    key_cache,
    value_cache,
    doc_lengths,
    gmu_gate,
    gmu_out,
    ffn1_gate,
    ffn1_up,
    ffn1_down,
    query_weight,
    attn_out,
    ffn2_gate,
    ffn2_up,
    ffn2_down,
    gain_a,
    gain_b,
    gain_c,
    gain_d,
    cotangent,
):
    seq_count = lax.axis_size("seq")
    row_count = lax.axis_size("row")
    seq_index = lax.axis_index("seq")
    positions = jnp.arange(seq_count * block_input.shape[1], dtype=jnp.int32)
    docs = lax.dynamic_index_in_dim(
        doc_numbers(doc_lengths, positions), seq_index // (seq_count // row_count), 0, keepdims=False
    )
    shared = dict(x=block_input[0], docs_col=docs[:, None], docs_row=docs[None, :])
    shared |= dict(gain_a=gain_a[None], gain_b=gain_b[None], gain_c=gain_c[None], gain_d=gain_d[None])
    kept = forward_pass(
        dict(
            cotangent=cotangent[0],
            memory=memory[0],
            keys=key_cache[0],
            values=value_cache[0],
            gmu_gate=gmu_gate,
            gmu_out=gmu_out,
            f1_gate=ffn1_gate,
            f1_up=ffn1_up,
            f1_down=ffn1_down,
            query=query_weight,
            attn_out=attn_out,
            f2_gate=ffn2_gate,
            f2_up=ffn2_up,
            f2_down=ffn2_down,
        ),
        shared,
    )
    back = backward_pass(
        dict(
            cot_rows=kept.cot_rows,
            rows_a=kept.rows_a_out,
            rows_b=kept.rows_b_out,
            rows_c=kept.rows_c_out,
            rows_d=kept.rows_d_out,
            q_heads=kept.q_heads_out,
            k_heads=kept.k_heads_out,
            v_heads=kept.v_heads_out,
            attended=kept.attended_out,
            mem=kept.mem_out,
            pre=kept.pre_out,
            act=kept.act_out,
            gate_1=kept.gate_out,
            up_1=kept.up_out,
            hidden_1=kept.hidden_out,
            x_one=kept.x_one_out,
            x_two=kept.x_two_out,
            x_three=kept.x_three_out,
            gmu_gate_w=kept.gmu_gate_w,
            gmu_out_w=kept.gmu_out_w,
            query_w=kept.query_w,
            attn_out_w=kept.attn_out_w,
            f1_gate_w=kept.f1_gate_w,
            f1_up_w=kept.f1_up_w,
            f1_down_w=kept.f1_down_w,
            f2_gate_w=kept.f2_gate_w,
            f2_up_w=kept.f2_up_w,
            f2_down_w=kept.f2_down_w,
        ),
        shared | dict(cotangent=cotangent[0]),
    )
    return (
        back.mixed[None],
        back.input_grad[None],
        back.mem_grad[None],
        back.key_grad[None],
        back.value_grad[None],
        back.gmu_gate_g,
        back.gmu_out_g,
        back.f1_gate_g,
        back.f1_up_g,
        back.f1_down_g,
        back.query_g,
        back.attn_out_g,
        back.f2_gate_g,
        back.f2_up_g,
        back.f2_down_g,
        *(back.gain_grads[k] for k in range(4)),
    )


def solution(mesh):
    tokens = P("row", "seq", None)
    inner, outer = P("seq", "row"), P("row", "seq")
    in_specs = (
        (tokens,) * 4
        + (P(), inner, outer, inner, inner, outer, inner, outer, inner, inner, outer)
        + (P(),) * 4
        + (tokens,)
    )
    out_specs = (
        (tokens,) * 5
        + (inner, outer, inner, inner, outer, inner, outer, inner, inner, outer)
        + (P(),) * 4
    )
    seq_count, row_count = mesh.shape["seq"], mesh.shape["row"]
    body = body_fast if seq_count == 8 and row_count == 4 else body_general
    return jax.shard_map(body, mesh=mesh, in_specs=in_specs, out_specs=out_specs, check_vma=False)
```
